128 devices in a mesh: row: 16 (over z, y), col: 8 (over x, core).
Axes of the slice: x: 4, y: 4, z: 4, core: 2. Of those that a mesh axis runs over, the one named last changes fastest.
Arguments:
- slc: float32 [2, 16, 1536, 6144], P(None, 'row', None, 'col'), may hold values from -6 to 6
- valid_rows: int32 [16, 2], replicated, may hold values from 0 to 1536, as said below
Outputs:
- linked: float32 [2, 16, 256, 2048], P(None, None, 'row', 'col')
The draws below stay inside these ranges and needn't reach their ends.
Inputs may be any that keep to these rules, and one draw needn't show every extreme that they name: valid_rows[t, 0] is below 192 and valid_rows[t, 1] is above 1344; some date starts at row 0 and some date ends at row 1536.
All inputs are finite; a program needn't handle non-finite values.
Results may differ from the reference program's by a relative error of at most 0.00029.
Values sent between devices are 32-bit elements; how exact they have to be, the bound alone decides.
No kernel may reach another device: no remote copies, remote signals or barrier semaphores. Data moves between devices by JAX's collectives and lax.ppermute only.
A program may use at most 128 MiB of HBM per device.

```python
import jax
import jax.numpy as jnp
from jax import lax

DATES = 16
ITERS = 10
HEIGHT = 1536
WIDTH = 6144


def draw_valid_rows(key, part):
    key = jax.random.fold_in(key, 7)
    first_key, second_key = jax.random.split(key)
    edge_rows = HEIGHT // 8
    start_rows = jax.random.randint(first_key, (DATES,), 0, edge_rows)
    cut_rows = jax.random.randint(second_key, (DATES,), 0, edge_rows)
    start_rows = start_rows - jnp.min(start_rows)
    end_rows = HEIGHT - (cut_rows - jnp.min(cut_rows))
    return jnp.stack([start_rows, end_rows], axis=1).astype(jnp.int32)


def steps_of(rng, dims, cuts, least, top_value):
    loudness = 1.0
    for axis_at, blocks in cuts:
        heights = jax.random.uniform(jax.random.fold_in(jax.random.fold_in(rng, 6), axis_at), (blocks,), jnp.float32, least / len(cuts), top_value / len(cuts))
        loudness = loudness * jnp.repeat(jnp.exp(heights), dims[axis_at] // blocks).reshape((-1,) + (1,) * (len(dims) - 1 - axis_at))
    return loudness


def bell_draw(key, shape, deviation, reach, pieces=(), kind=jnp.bfloat16):
    array = jax.random.normal(key, shape, jnp.float32) * deviation
    if len(pieces) > 0:
        array = steps_of(key, shape, pieces, -0.22, 0.18) * array
    return jnp.clip(array, min=-reach, max=reach).astype(kind)


def setup_inputs(seed: int = 0) -> dict:
    seeds = jax.random.split(jax.random.key(seed), 3)
    slc = bell_draw(seeds[0], (2, DATES, HEIGHT, WIDTH), 1.0, 6.0, ((1, 16), (3, 8)), jnp.float32)
    valid_rows = draw_valid_rows(jax.random.fold_in(seeds[2], 71), 0)
    return {"slc": slc, "valid_rows": valid_rows}


coherence_floor = 20.0

def pool_window(field):
    out_rows = (field.shape[-2] - 6) // 6
    out_cols = (field.shape[-1] - 2) // 3
    row_sum = field[..., 0:6 * out_rows:6, :]
    for offset in range(1, 11):
        row_sum = row_sum + field[..., offset:offset + 6 * out_rows:6, :]
    col_sum = row_sum[..., 0:3 * out_cols:3]
    for offset in range(1, 5):
        col_sum = col_sum + row_sum[..., offset:offset + 3 * out_cols:3]
    return col_sum

def covariance(padded):
    real_part = padded[0]
    imag_part = padded[1]

    def one_date(pair):
        date_real, date_imag = pair
        prod_real = date_real[None] * real_part + date_imag[None] * imag_part
        prod_imag = date_imag[None] * real_part - date_real[None] * imag_part
        return (pool_window(prod_real), pool_window(prod_imag))
    return lax.map(one_date, (real_part, imag_part))

def phase_link(cov_real, cov_imag):
    count = cov_real.shape[0]
    index_all = jnp.arange(count)
    power = jnp.maximum(cov_real[index_all, index_all], coherence_floor)
    inv_root = 1.0 / jnp.sqrt(power)
    factor = inv_root[:, None] * inv_root[None, :]
    coh_real = cov_real * factor
    coh_imag = cov_imag * factor
    vec_real = jnp.full(cov_real.shape[1:], 0.25, jnp.float32)
    vec_imag = jnp.zeros(cov_real.shape[1:], jnp.float32)
    for iteration in range(ITERS):
        new_real = lax.optimization_barrier(jnp.sum(coh_real * vec_real[None] - coh_imag * vec_imag[None], axis=1)) + vec_real
        new_imag = lax.optimization_barrier(jnp.sum(coh_real * vec_imag[None] + coh_imag * vec_real[None], axis=1)) + vec_imag
        length = jnp.sqrt(lax.optimization_barrier(jnp.sum(new_real * new_real + new_imag * new_imag, axis=0)))
        vec_real = new_real / length[None]
        vec_imag = new_imag / length[None]
    return jnp.stack([vec_real, vec_imag])

def reference(slc, valid_rows):
    row_index = jnp.arange(slc.shape[2], dtype=jnp.int32)[None, :]
    keep_mask = (row_index >= valid_rows[:, 0:1]) & (row_index < valid_rows[:, 1:2])
    masked = slc * keep_mask[None, :, :, None].astype(jnp.float32)
    padded = jnp.pad(masked, ((0, 0), (0, 0), (3, 3), (1, 1)))
    cov_real, cov_imag = covariance(padded)
    return phase_link(cov_real, cov_imag)
```

```python
import functools

import jax
import jax.numpy as jnp
import numpy as np
from jax import lax
from jax.experimental import pallas as pl
from jax.experimental.pallas import tpu as pltpu
from jax.sharding import PartitionSpec as P

ITERS = 10
FLOOR = 20.0
DATES = 16
TILES = 16
COLS = 768
OUT_COLS = 256
BLOCKS = 16
TILE_ROWS = 6 * BLOCKS
MSG_ROWS = 208
HALO_ROW = 192
EDGE_ROW = 202
GROUP = 4
PAIRS = [(t, u) for t in range(DATES) for u in range(t + 1, DATES)]
PAIR_AT = {pair: i for i, pair in enumerate(PAIRS)}
FIELDS = DATES + 2 * len(PAIRS)
CHUNK = 512
VMEM_LIMIT = 56 * 1024 * 1024


def column_tables():
    source = np.arange(COLS)[:, None]
    target = 3 * np.arange(OUT_COLS)[None, :]
    main = ((source >= target - 1) & (source <= target + 3)).astype(np.float32)
    row = np.arange(128)[:, None]
    lane = np.arange(128)[None, :]
    pool = np.zeros((2, 128, 128), np.float32)
    for side in range(2):
        block = lane - 16 * side
        inside = (block >= 0) & (block < 16) & (row >= 6 * block) & (row <= 6 * block + 10)
        pool[side] = inside
    edge = np.zeros((128, OUT_COLS), np.float32)
    edge[0:16, 0] = 1.0
    edge[16:32, OUT_COLS - 1] = 1.0
    return main, pool, edge


def edge_kernel(valid_ref, left_ref, right_ref, first_ref, last_ref):
    me = lax.axis_index("row")
    low, high = valid_ref[me, 0], valid_ref[me, 1]
    lane = lax.broadcasted_iota(jnp.int32, (8, 128), 1)
    row = lax.broadcasted_iota(jnp.int32, (1, 1536), 1)
    keep = (row >= low) & (row < high)
    for ref, pick, out in ((left_ref, 0, first_ref), (right_ref, 127, last_ref)):
        one = jnp.where(lane == pick, 1.0, 0.0)
        for part in range(2):
            column = lax.dot_general(
                one, ref[part, 0], (((1,), (1,)), ((), ())),
                precision=lax.Precision.HIGHEST, preferred_element_type=jnp.float32,
            )
            out[part : part + 1, :] = jnp.where(keep, column[0:1, :], 0.0)


def edge_columns(slc, valid_rows):
    shape = jax.ShapeDtypeStruct((2, 1536), jnp.float32)
    return pl.pallas_call(
        edge_kernel,
        grid=(1,),
        in_specs=[
            pl.BlockSpec(memory_space=pltpu.SMEM),
            pl.BlockSpec((2, 1, 1536, 128), lambda i: (0, 0, 0, 0)),
            pl.BlockSpec((2, 1, 1536, 128), lambda i: (0, 0, 0, COLS // 128 - 1)),
        ],
        out_specs=[pl.BlockSpec((2, 1536), lambda i: (0, 0))] * 2,
        out_shape=[shape, shape],
        compiler_params=pltpu.CompilerParams(vmem_limit_bytes=VMEM_LIMIT),
        name="edge_columns",
    )(valid_rows, slc, slc)


def pack_kernel(valid_ref, before_ref, tile_ref, after_ref, out_ref, rows_ref):
    me = lax.axis_index("row")
    step = pl.program_id(0)
    low, high = valid_ref[me, 0], valid_ref[me, 1]
    span = GROUP * TILE_ROWS

    def masked(ref, start, count):
        row = lax.broadcasted_iota(jnp.int32, (count, COLS), 0) + (step * span + start)
        keep = (row >= low) & (row < high)
        for part in range(2):
            value = jnp.where(keep, ref[part, 0], 0.0)
            for lt in range(COLS // 128):
                rows_ref[part, lt, pl.ds(start + 8, count), :] = value[:, lt * 128 : lt * 128 + 128]

    masked(before_ref, -8, 8)
    masked(tile_ref, 0, span)
    masked(after_ref, span, 8)
    for tile in range(GROUP):
        base = 5 + tile * TILE_ROWS
        for part in range(2):
            for phase in range(6):
                for half in range(2):
                    at = part * 96 + phase * 16 + half * 8
                    for lt in range(COLS // 128):
                        lanes = pl.ds(lt * 128, 128)
                        out_ref[tile, pl.ds(at, 8), lanes] = rows_ref[
                            part, lt, pl.ds(base + 6 * half + phase, 8, stride=12), :
                        ]
            for lt in range(COLS // 128):
                out_ref[tile, pl.ds(HALO_ROW + 5 * part, 5), pl.ds(lt * 128, 128)] = rows_ref[
                    part, lt, pl.ds(base + TILE_ROWS, 5), :
                ]
        out_ref[tile, pl.ds(EDGE_ROW, 6), :] = jnp.zeros((6, COLS), jnp.float32)


def pack(slc, valid_rows):
    span = GROUP * TILE_ROWS // 8
    return pl.pallas_call(
        pack_kernel,
        grid=(TILES // GROUP,),
        in_specs=[
            pl.BlockSpec(memory_space=pltpu.SMEM),
            pl.BlockSpec((2, 1, 8, COLS), lambda i: (0, 0, jnp.maximum(i * span - 1, 0), 0)),
            pl.BlockSpec((2, 1, GROUP * TILE_ROWS, COLS), lambda i: (0, 0, i, 0)),
            pl.BlockSpec((2, 1, 8, COLS), lambda i: (0, 0, jnp.minimum(i * span + span, 191), 0)),
        ],
        out_specs=pl.BlockSpec((GROUP, MSG_ROWS, COLS), lambda i: (i, 0, 0)),
        out_shape=jax.ShapeDtypeStruct((TILES, MSG_ROWS, COLS), jnp.float32),
        scratch_shapes=[pltpu.VMEM((2, COLS // 128, GROUP * TILE_ROWS + 16, 128), jnp.float32)],
        compiler_params=pltpu.CompilerParams(vmem_limit_bytes=VMEM_LIMIT),
        cost_estimate=pl.CostEstimate(flops=10**6, bytes_accessed=2 * 10**7, transcendentals=0),
        name="pack",
    )(valid_rows, slc, slc, slc)


def insert_kernel(left_ref, right_ref, in_ref, out_ref, wide_ref):
    out_ref[...] = in_ref[...]
    wide_ref[...] = jnp.zeros_like(wide_ref)
    for side, ref in enumerate((left_ref, right_ref)):
        wide_ref[2 * side : 2 * side + 2, 128 : 128 + 1536] = ref[...]
    for tile in range(TILES):
        start = 128 + tile * TILE_ROWS - 3
        for row in range(4):
            out_ref[tile, EDGE_ROW % 8 : EDGE_ROW % 8 + 1, row * 128 : row * 128 + 128] = wide_ref[
                row : row + 1, start : start + 128
            ]


def insert_edges(left, right, message):
    spec = pl.BlockSpec((TILES, 8, COLS), lambda i: (0, EDGE_ROW // 8, 0))
    column = pl.BlockSpec((2, 1536), lambda i: (0, 0))
    return pl.pallas_call(
        insert_kernel,
        grid=(1,),
        in_specs=[column, column, spec],
        out_specs=spec,
        out_shape=jax.ShapeDtypeStruct(message.shape, message.dtype),
        input_output_aliases={2: 0},
        scratch_shapes=[pltpu.VMEM((8, 1920), jnp.float32)],
        compiler_params=pltpu.CompilerParams(vmem_limit_bytes=VMEM_LIMIT),
        name="insert_edges",
    )(left, right, message)


def split(x):
    high = x.astype(jnp.bfloat16)
    return high, (x - high.astype(jnp.float32)).astype(jnp.bfloat16)


def field_of(t, u):
    return t if t == u else DATES + 2 * PAIR_AT[t, u]


def cross_products(data, t_part, u_tile, lanes, rows):
    real = imag = None
    for re_row, im_row in rows:
        a_t = data[re_row, pl.ds(t_part, 1), lanes]
        b_t = data[im_row, pl.ds(t_part, 1), lanes]
        a_u = data[re_row, pl.ds(u_tile * 8, 8), lanes]
        b_u = data[im_row, pl.ds(u_tile * 8, 8), lanes]
        re = a_t * a_u + b_t * b_u
        im = b_t * a_u - a_t * b_u
        real = re if real is None else real + re
        imag = im if imag is None else imag + im
    return real, imag


def main_products(msg, sums, lhs, lt):
    lanes = pl.ds(pl.multiple_of(lt * 128, 128), 128)
    last = lax.broadcasted_iota(jnp.int32, (8, 128), 0) == 7

    def rows_at(phase, half):
        return pl.ds(phase * 16 + half * 8, 8)

    def load(kind, date, phase, half):
        if kind == "a":
            return msg[date, pl.ds(phase * 16 + half * 8, 8), lanes]
        if kind == "b":
            return msg[date, pl.ds(96 + phase * 16 + half * 8, 8), lanes]
        base = 0 if kind == "s" else 96
        return sums[date, pl.ds(base + phase * 16 + half * 8, 8), lanes]

    def emit(field, first, whole):
        out0 = whole[0] + first[1]
        rolled = jnp.where(last, 0.0, pltpu.roll(first[0], 7, 0))
        out1 = whole[1] + rolled
        high, low = split(jnp.concatenate([out0, out1], axis=0))
        lhs[0, pl.ds(field * 16, 16), lanes] = high
        lhs[1, pl.ds(field * 16, 16), lanes] = low

    for t in range(DATES):
        first, whole = [], []
        for half in range(2):
            total = None
            for phase in range(6):
                a, b = load("a", t, phase, half), load("b", t, phase, half)
                term = a * a + b * b
                if phase == 5:
                    first.append(total)
                total = term if total is None else total + term
            whole.append(total)
        emit(t, first, whole)

    groups = []
    for i in range(0, DATES, 2):
        groups.append(([i], [i + 1]))
        rest = list(range(i + 2, DATES))
        for j in range(0, len(rest), 4):
            groups.append(([i, i + 1], rest[j : j + 4]))
    for ts, us in groups:
        pairs = [(t, u) for t in ts for u in us]
        first = {pair: ([], []) for pair in pairs}
        whole = {pair: ([], []) for pair in pairs}
        for half in range(2):
            acc = {}
            for phase in range(6):
                s_t = {t: load("s", t, phase, half) for t in ts}
                a_t = {t: load("a", t, phase, half) for t in ts}
                b_t = {t: load("b", t, phase, half) for t in ts}
                a_u = {u: load("a", u, phase, half) for u in us}
                s_u = {u: load("s", u, phase, half) for u in us}
                d_u = {u: load("d", u, phase, half) for u in us}
                for t, u in pairs:
                    p = a_u[u] * s_t[t]
                    q = d_u[u] * b_t[t]
                    r = s_u[u] * a_t[t]
                    if phase == 0:
                        acc[t, u] = (p, q, r)
                    elif phase < 5:
                        p0, q0, r0 = acc[t, u]
                        acc[t, u] = (p0 + p, q0 + q, r0 + r)
                    else:
                        p0, q0, r0 = acc[t, u]
                        re5, im5 = p0 - q0, p0 - r0
                        first[t, u][0].append(re5)
                        first[t, u][1].append(im5)
                        whole[t, u][0].append(re5 + (p - q))
                        whole[t, u][1].append(im5 + (p - r))
        for pair in pairs:
            for part in range(2):
                emit(field_of(*pair) + part, first[pair][part], whole[pair][part])


def dot(a, b):
    return jnp.dot(a, b, preferred_element_type=jnp.float32)


def link_kernel(
    msg, table, pool, edge_table, out, sums, lhs, acc, small, side_lhs, halo, edge, coh, vec, weight,
    rows,
):
    step = pl.program_id(0)
    steps = COLS // 256

    @pl.when(step == 0)
    def _():
        edge[...] = jnp.zeros_like(edge)
        halo[...] = jnp.zeros_like(halo)
        side_lhs[...] = jnp.zeros_like(side_lhs)

    def fill(date, carry):
        a = msg[date, pl.ds(0, 96), :]
        b = msg[date, pl.ds(96, 96), :]
        sums[date, pl.ds(0, 96), :] = a + b
        sums[date, pl.ds(96, 96), :] = a - b
        return carry

    lax.fori_loop(0, DATES, fill, 0)

    def products(lt, carry):
        main_products(msg, sums, lhs, lt)
        return carry

    lax.fori_loop(0, 2, products, 0)

    for date in range(DATES):
        for row in range(11):
            small[row, date : date + 1, :] = msg[date, HALO_ROW + row : HALO_ROW + row + 1, :]
    halo_rows = [(p, 5 + p) for p in range(5)]
    for t in range(DATES):
        for u_tile in range(t // 8, 2):
            for lt in range(2):
                lanes = pl.ds(lt * 128, 128)
                values = cross_products(small, t, u_tile, lanes, halo_rows)
                for part in range(2):
                    at = part * 256 + t * 16 + u_tile * 8
                    side_lhs[pl.ds(at, 8), lanes] = values[part]
    high, low = split(side_lhs[...])
    halo[...] += dot(high, table[...]) + dot(low, table[...])

    @pl.when(step < 2)
    def _():
        for t in range(DATES):
            for u_tile in range(t // 8, 2):
                a_t = small[10, t : t + 1, 0:128]
                b_t = small[10, t : t + 1, 128:256]
                a_u = small[10, u_tile * 8 : u_tile * 8 + 8, 0:128]
                b_u = small[10, u_tile * 8 : u_tile * 8 + 8, 128:256]
                at = t * 16 + u_tile * 8
                side_lhs[pl.ds(at, 8), 0:128] = a_t * a_u + b_t * b_u
                side_lhs[pl.ds(256 + at, 8), 0:128] = b_t * a_u - a_t * b_u
        high, low = split(side_lhs[:, 0:128])
        edge[...] += dot(high, pool[0]) + dot(low, pool[0])

    def pooled(chunk, carry):
        at = pl.ds(pl.multiple_of(chunk * CHUNK, CHUNK), CHUNK)
        value = dot(lhs[0, at, :], table[...]) + dot(lhs[1, at, :], table[...])

        @pl.when(step == 0)
        def _():
            acc[at, :] = value

        @pl.when(step > 0)
        def _():
            acc[at, :] += value

        return carry

    lax.fori_loop(0, FIELDS * 16 // CHUNK, pooled, 0)

    @pl.when(step == steps - 1)
    def _():
        finish(acc, edge_table, halo, edge, lhs, coh, vec, weight, rows, out)


def finish(acc, edge_table, halo, edge, lhs, coh, vec, weight, rows, out):
    row = lax.broadcasted_iota(jnp.int32, (16, 128), 0)
    lane = lax.broadcasted_iota(jnp.int32, (16, 128), 1)
    block = jnp.where(row < 8, 2 * row, 2 * (row - 8) + 1)
    mine = ((lane == block) | (lane == block + 16))
    for t in range(DATES):
        for u in range(t, DATES):
            for part in range(1 if t == u else 2):
                field = field_of(t, u) + part
                at = part * 256 + t * 16 + u
                value = jnp.where(mine, edge[at : at + 1, :], 0.0)
                high, low = split(value)
                lhs[0, pl.ds(field * 16, 16), 0:128] = high
                lhs[1, pl.ds(field * 16, 16), 0:128] = low

    def pooled(chunk, carry):
        at = pl.ds(pl.multiple_of(chunk * CHUNK, CHUNK), CHUNK)
        acc[at, :] += dot(lhs[0, at, 0:128], edge_table[...]) + dot(
            lhs[1, at, 0:128], edge_table[...]
        )
        return carry

    lax.fori_loop(0, FIELDS * 16 // CHUNK, pooled, 0)

    last = lax.broadcasted_iota(jnp.int32, (8, 128), 0) == 7
    for half in range(2):
        for mt in range(2):
            lanes = pl.ds(mt * 128, 128)

            def cov(t, u, part):
                field = field_of(t, u) + part
                value = acc[pl.ds(field * 16 + half * 8, 8), lanes]
                if half == 1:
                    at = part * 256 + t * 16 + u
                    value = value + jnp.where(last, halo[pl.ds(at, 1), lanes], 0.0)
                return value

            solve(cov, coh, vec, weight)
            for date in range(DATES):
                for part in range(2):
                    rows[part, date, mt, pl.ds(half, 8, stride=2), :] = vec[part, date]
    for mt in range(2):
        out[:, :, :, mt * 128 : mt * 128 + 128] = rows[:, :, mt]


def solve(cov, coh, vec, weight):
    inv = []
    for t in range(DATES):
        diag = cov(t, t, 0)
        root = lax.rsqrt(jnp.maximum(diag, FLOOR))
        inv.append(root)
        weight[t] = diag * (root * root) + 1.0
    for i, (t, u) in enumerate(PAIRS):
        factor = inv[t] * inv[u]
        real = cov(t, u, 0) * factor
        imag = cov(t, u, 1) * factor
        coh[i, 0] = real
        coh[i, 1] = real + imag
        coh[i, 2] = imag - real
    for t in range(DATES):
        vec[0, t] = jnp.full((8, 128), 0.25, jnp.float32)
        vec[1, t] = jnp.zeros((8, 128), jnp.float32)
        vec[2, t] = jnp.full((8, 128), 0.25, jnp.float32)

    def iterate(_, carry):
        new_real, new_imag = [None] * DATES, [None] * DATES
        sums = [[None, None, None] for _ in range(DATES)]

        def add(t, which, value, minus=False):
            if sums[t][which] is None:
                sums[t][which] = -value if minus else value
            elif minus:
                sums[t][which] = sums[t][which] - value
            else:
                sums[t][which] = sums[t][which] + value

        def pair(t, u, v):
            i = PAIR_AT[t, u]
            real, plus, minus = coh[i, 0], coh[i, 1], coh[i, 2]
            add(t, 0, real * v[u][2])
            add(t, 1, plus * v[u][1])
            add(t, 2, minus * v[u][0])
            add(u, 0, real * v[t][2])
            add(u, 1, minus * v[t][1], True)
            add(u, 2, plus * v[t][0], True)

        for first in range(0, DATES, 4):
            for second in range(first, DATES, 4):
                dates = sorted(set(range(first, first + 4)) | set(range(second, second + 4)))
                v = {t: (vec[0, t], vec[1, t], vec[2, t]) for t in dates}
                for t in range(first, first + 4):
                    for u in range(second, second + 4):
                        if t < u:
                            pair(t, u, v)
        norm = None
        for t in range(DATES):
            own = weight[t]
            new_real[t] = (sums[t][0] - sums[t][1]) + own * vec[0, t]
            new_imag[t] = (sums[t][0] + sums[t][2]) + own * vec[1, t]
            square = new_real[t] * new_real[t] + new_imag[t] * new_imag[t]
            norm = square if norm is None else norm + square
        scale = lax.rsqrt(norm)
        for t in range(DATES):
            real, imag = new_real[t] * scale, new_imag[t] * scale
            vec[0, t] = real
            vec[1, t] = imag
            vec[2, t] = real + imag
        return carry

    lax.fori_loop(0, ITERS, iterate, 0)


def link(message, table, pool, edge_table):
    whole = lambda *shape: pl.BlockSpec(shape, lambda i: (0,) * len(shape))
    return pl.pallas_call(
        link_kernel,
        grid=(COLS // 256,),
        in_specs=[
            pl.BlockSpec((DATES, MSG_ROWS, 256), lambda i: (0, 0, i)),
            pl.BlockSpec((256, OUT_COLS), lambda i: (i, 0)),
            pl.BlockSpec((1, 128, 128), lambda i: (jnp.minimum(i, 1), 0, 0)),
            whole(128, OUT_COLS),
        ],
        out_specs=whole(2, DATES, BLOCKS, OUT_COLS),
        out_shape=jax.ShapeDtypeStruct((2, DATES, BLOCKS, OUT_COLS), jnp.float32),
        scratch_shapes=[
            pltpu.VMEM((DATES, 192, 256), jnp.float32),
            pltpu.VMEM((2, FIELDS * 16, 256), jnp.bfloat16),
            pltpu.VMEM((FIELDS * 16, OUT_COLS), jnp.float32),
            pltpu.VMEM((11, DATES, 256), jnp.float32),
            pltpu.VMEM((512, 256), jnp.float32),
            pltpu.VMEM((512, 256), jnp.float32),
            pltpu.VMEM((512, 128), jnp.float32),
            pltpu.VMEM((len(PAIRS), 3, 8, 128), jnp.float32),
            pltpu.VMEM((3, DATES, 8, 128), jnp.float32),
            pltpu.VMEM((DATES, 8, 128), jnp.float32),
            pltpu.VMEM((2, DATES, 2, BLOCKS, 128), jnp.float32),
        ],
        compiler_params=pltpu.CompilerParams(vmem_limit_bytes=VMEM_LIMIT),
        cost_estimate=pl.CostEstimate(flops=10**9, bytes_accessed=10**7, transcendentals=0),
        name="link",
    )(message, table, pool, edge_table)


def local(slc, valid_rows):
    size = lax.axis_size("col")
    up = [(i, i + 1) for i in range(size - 1)]
    down = [(i + 1, i) for i in range(size - 1)]
    first, last = edge_columns(slc, valid_rows)
    left = lax.ppermute(last, "col", up)
    right = lax.ppermute(first, "col", down)
    message = pack(slc, valid_rows)
    message = insert_edges(left, right, message)
    received = lax.all_to_all(message, "row", 0, 0, tiled=True)
    main, pool, edge = (jnp.asarray(x, jnp.bfloat16) for x in column_tables())
    return link(received, main, pool, edge)


def solution(mesh):
    return jax.shard_map(
        local,
        mesh=mesh,
        in_specs=(P(None, "row", None, "col"), P()),
        out_specs=P(None, None, "row", "col"),
        check_vma=False,
    )
```

```python
import functools

import jax
import jax.numpy as jnp
import numpy as np
from jax import lax
from jax.experimental import pallas as pl
from jax.experimental.pallas import tpu as pltpu
from jax.sharding import PartitionSpec as P

ITERS = 10
FLOOR = 20.0
DATES = 16
TILES = 16
COLS = 768
LANE_TILES = 6
FIRST = 5
OUT_COLS = 256
BLOCKS = 16
TILE_ROWS = 6 * BLOCKS
MSG_ROWS = 208
HALO_ROW = 192
EDGE_ROW = 202
GROUP = 4
PAIRS = [(t, u) for t in range(DATES) for u in range(t + 1, DATES)]
PAIR_AT = {pair: i for i, pair in enumerate(PAIRS)}
FIELDS = DATES + 2 * len(PAIRS)
CHUNK = 512
SIDE = 512
VMEM_LIMIT = 56 * 1024 * 1024
FEEDS = ((0, 2), (0,), (0,), (0, 1), (1, 2), (2,))


def lane_columns():
    lane = np.arange(128)
    group_a = np.where(lane < 32, 128 + lane, lane)
    group_b = np.where((lane >= 32) & (lane < 96), 128 + lane, 128 + (lane + 64) % 128)
    own = np.where(lane < 32, lane, 128 + lane)
    other = (lane + 64) % 128
    far = np.where(other < 32, other, 128 + other)
    group_c = np.where((lane < 32) | (lane >= 96), own, far)
    return group_a, group_b, group_c


def column_tables():
    groups = lane_columns()
    tables = np.zeros((LANE_TILES, 256, 256), np.float32)
    for lt in range(LANE_TILES):
        column = (lt * 128 + np.arange(128) + 64) % COLS
        for place, group in enumerate(FEEDS[lt]):
            target = 3 * groups[group][None, :]
            inside = (column[:, None] >= target - 1) & (column[:, None] <= target + 3)
            for copy in range(2):
                tables[lt, copy * 128 : copy * 128 + 128, place * 128 : place * 128 + 128] = inside
    row = np.arange(128)
    pool = np.zeros((2, 8, 128), np.float32)
    for half in range(2):
        for s in range(8):
            block = 2 * s + half
            pool[half, s] = (row >= 6 * block) & (row <= 6 * block + 10)
    return tables, pool


def pack_kernel(
    valid_ref, before_ref, tile_ref, after_ref, out1_ref, out2_ref, first_ref, last_ref, rows_ref
):
    me = lax.axis_index("row")
    step = pl.program_id(0)
    low, high = valid_ref[0, me], valid_ref[1, me]
    span = GROUP * TILE_ROWS
    lane = lax.broadcasted_iota(jnp.int32, (8, 128), 1)

    def masked(ref, start, count):
        row = lax.broadcasted_iota(jnp.int32, (count, 128), 0) + (step * span + start)
        keep = (row >= low) & (row < high)
        left = lax.broadcasted_iota(jnp.int32, (count, 128), 1) < 64
        for part in range(2):
            value = [
                jnp.where(keep, ref[part, 0, :, lt * 128 : lt * 128 + 128], 0.0)
                for lt in range(LANE_TILES)
            ]
            if count == span:
                for at, pick, out in ((0, 0, first_ref), (LANE_TILES - 1, 127, last_ref)):
                    column = lax.dot_general(
                        jnp.where(lane == pick, 1.0, 0.0), value[at], (((1,), (1,)), ((), ())),
                        precision=lax.Precision.HIGHEST, preferred_element_type=jnp.float32,
                    )
                    out[part : part + 1, :] = column[0:1, :]
            turned = [pltpu.roll(v, 64, 1) for v in value]
            for lt in range(LANE_TILES):
                rows_ref[part, lt, pl.ds(start + 8, count), :] = jnp.where(
                    left, turned[lt], turned[(lt + 1) % LANE_TILES]
                )

    masked(before_ref, -8, 8)
    masked(tile_ref, 0, span)
    masked(after_ref, span, 8)
    for tile in range(GROUP):
        base = 5 + tile * TILE_ROWS
        for lt in range(LANE_TILES):
            out = out1_ref if lt < FIRST else out2_ref
            lanes = pl.ds((lt if lt < FIRST else 0) * 128, 128)
            for part in range(2):
                for phase in range(6):
                    for half in range(2):
                        out[tile, pl.ds(part * 96 + phase * 16 + half * 8, 8), lanes] = rows_ref[
                            part, lt, pl.ds(base + 6 * half + phase, 8, stride=12), :
                        ]
                out[tile, pl.ds(HALO_ROW + 5 * part, 5), lanes] = rows_ref[
                    part, lt, pl.ds(base + TILE_ROWS, 5), :
                ]
        out1_ref[tile, pl.ds(EDGE_ROW, 6), :] = jnp.zeros((6, FIRST * 128), jnp.float32)
        out2_ref[tile, pl.ds(EDGE_ROW, 6), :] = jnp.zeros((6, 128), jnp.float32)


def pack(slc, valid_rows):
    span = GROUP * TILE_ROWS
    eight = span // 8
    column = jax.ShapeDtypeStruct((2, 1536), jnp.float32)
    return pl.pallas_call(
        pack_kernel,
        grid=(TILES // GROUP,),
        in_specs=[
            pl.BlockSpec(memory_space=pltpu.SMEM),
            pl.BlockSpec((2, 1, 8, COLS), lambda i: (0, 0, jnp.maximum(i * eight - 1, 0), 0)),
            pl.BlockSpec((2, 1, span, COLS), lambda i: (0, 0, i, 0)),
            pl.BlockSpec((2, 1, 8, COLS), lambda i: (0, 0, jnp.minimum(i * eight + eight, 191), 0)),
        ],
        out_specs=[
            pl.BlockSpec((GROUP, MSG_ROWS, FIRST * 128), lambda i: (i, 0, 0)),
            pl.BlockSpec((GROUP, MSG_ROWS, 128), lambda i: (i, 0, 0)),
            pl.BlockSpec((2, span), lambda i: (0, i)),
            pl.BlockSpec((2, span), lambda i: (0, i)),
        ],
        out_shape=[
            jax.ShapeDtypeStruct((TILES, MSG_ROWS, FIRST * 128), jnp.float32),
            jax.ShapeDtypeStruct((TILES, MSG_ROWS, 128), jnp.float32),
            column,
            column,
        ],
        scratch_shapes=[pltpu.VMEM((2, LANE_TILES, span + 16, 128), jnp.float32)],
        compiler_params=pltpu.CompilerParams(vmem_limit_bytes=VMEM_LIMIT),
        cost_estimate=pl.CostEstimate(flops=10**6, bytes_accessed=2 * 10**7, transcendentals=0),
        name="pack",
    )(valid_rows.T, slc, slc, slc)


def insert_kernel(left_ref, right_ref, in_ref, out_ref, wide_ref):
    out_ref[...] = in_ref[...]
    wide_ref[...] = jnp.zeros_like(wide_ref)
    for side, ref in enumerate((left_ref, right_ref)):
        wide_ref[2 * side : 2 * side + 2, 128 : 128 + 1536] = ref[...]
    for tile in range(TILES):
        start = 128 + tile * TILE_ROWS - 3
        at = EDGE_ROW % 8
        out_ref[tile, at : at + 4, :] = wide_ref[0:4, start : start + 128]


def insert_edges(left, right, message):
    spec = pl.BlockSpec((TILES, 8, 128), lambda i: (0, EDGE_ROW // 8, 0))
    column = pl.BlockSpec((2, 1536), lambda i: (0, 0))
    return pl.pallas_call(
        insert_kernel,
        grid=(1,),
        in_specs=[column, column, spec],
        out_specs=spec,
        out_shape=jax.ShapeDtypeStruct(message.shape, message.dtype),
        input_output_aliases={2: 0},
        scratch_shapes=[pltpu.VMEM((8, 1920), jnp.float32)],
        name="insert_edges",
    )(left, right, message)


def split(x):
    high = x.astype(jnp.bfloat16)
    return high, (x - high.astype(jnp.float32)).astype(jnp.bfloat16)


def field_of(t, u):
    return t if t == u else DATES + 2 * PAIR_AT[t, u]


def cross_products(data, t_part, u_tile, lanes, rows):
    real = imag = None
    for re_row, im_row in rows:
        a_t = data[re_row, pl.ds(t_part, 1), lanes]
        b_t = data[im_row, pl.ds(t_part, 1), lanes]
        a_u = data[re_row, pl.ds(u_tile * 8, 8), lanes]
        b_u = data[im_row, pl.ds(u_tile * 8, 8), lanes]
        re = a_t * a_u + b_t * b_u
        im = b_t * a_u - a_t * b_u
        real = re if real is None else real + re
        imag = im if imag is None else imag + im
    return real, imag


def main_products(msg, sums, lhs):
    lanes = pl.ds(0, 128)
    last = lax.broadcasted_iota(jnp.int32, (8, 128), 0) == 7

    def rows_at(phase, half):
        return pl.ds(phase * 16 + half * 8, 8)

    def load(kind, date, phase, half):
        if kind == "a":
            return msg[date, pl.ds(phase * 16 + half * 8, 8), lanes]
        if kind == "b":
            return msg[date, pl.ds(96 + phase * 16 + half * 8, 8), lanes]
        base = 0 if kind == "s" else 96
        return sums[date, pl.ds(base + phase * 16 + half * 8, 8), lanes]

    def emit(field, first, whole):
        out0 = whole[0] + first[1]
        rolled = jnp.where(last, 0.0, pltpu.roll(first[0], 7, 0))
        out1 = whole[1] + rolled
        high, low = split(jnp.concatenate([out0, out1], axis=0))
        lhs[pl.ds(field * 16, 16), 0:128] = high
        lhs[pl.ds(field * 16, 16), 128:256] = low

    for t in range(DATES):
        first, whole = [], []
        for half in range(2):
            total = None
            for phase in range(6):
                a, b = load("a", t, phase, half), load("b", t, phase, half)
                term = a * a + b * b
                if phase == 5:
                    first.append(total)
                total = term if total is None else total + term
            whole.append(total)
        emit(t, first, whole)

    groups = []
    for i in range(0, DATES, 2):
        groups.append(([i], [i + 1]))
        rest = list(range(i + 2, DATES))
        for j in range(0, len(rest), 4):
            groups.append(([i, i + 1], rest[j : j + 4]))
    for ts, us in groups:
        pairs = [(t, u) for t in ts for u in us]
        first = {pair: ([], []) for pair in pairs}
        whole = {pair: ([], []) for pair in pairs}
        for half in range(2):
            acc = {}
            for phase in range(6):
                s_t = {t: load("s", t, phase, half) for t in ts}
                a_t = {t: load("a", t, phase, half) for t in ts}
                b_t = {t: load("b", t, phase, half) for t in ts}
                a_u = {u: load("a", u, phase, half) for u in us}
                s_u = {u: load("s", u, phase, half) for u in us}
                d_u = {u: load("d", u, phase, half) for u in us}
                for t, u in pairs:
                    p = a_u[u] * s_t[t]
                    q = d_u[u] * b_t[t]
                    r = s_u[u] * a_t[t]
                    if phase == 0:
                        acc[t, u] = (p, q, r)
                    elif phase < 5:
                        p0, q0, r0 = acc[t, u]
                        acc[t, u] = (p0 + p, q0 + q, r0 + r)
                    else:
                        p0, q0, r0 = acc[t, u]
                        re5, im5 = p0 - q0, p0 - r0
                        first[t, u][0].append(re5)
                        first[t, u][1].append(im5)
                        whole[t, u][0].append(re5 + (p - q))
                        whole[t, u][1].append(im5 + (p - r))
        for pair in pairs:
            for part in range(2):
                emit(field_of(*pair) + part, first[pair][part], whole[pair][part])


def dot(a, b):
    return jnp.dot(a, b, preferred_element_type=jnp.float32)


def lane_tile(msg, sums, lhs, small, side_lhs):
    def fill(date, carry):
        a = msg[date, pl.ds(0, 96), :]
        b = msg[date, pl.ds(96, 96), :]
        sums[date, pl.ds(0, 96), :] = a + b
        sums[date, pl.ds(96, 96), :] = a - b
        return carry

    lax.fori_loop(0, DATES, fill, 0)
    main_products(msg, sums, lhs)
    for date in range(DATES):
        for row in range(small.shape[0]):
            small[row, date : date + 1, :] = msg[date, HALO_ROW + row : HALO_ROW + row + 1, :]
    for t in range(DATES):
        for u_tile in range(2):
            if u_tile < t // 8:
                values = (jnp.zeros((8, 128), jnp.float32),) * 2
            else:
                rows = [(p, 5 + p) for p in range(5)]
                values = cross_products(small, t, u_tile, pl.ds(0, 128), rows)
            for part in range(2):
                at = pl.ds(part * 256 + t * 16 + u_tile * 8, 8)
                side_lhs[at, 0:128] = values[part]


def pool_columns(lhs, side_lhs, table, width, put, put_side):
    def pooled(chunk, carry):
        at = pl.ds(pl.multiple_of(chunk * CHUNK, CHUNK), CHUNK)
        put(at, dot(lhs[at, :], table[0, :, 0:width]))
        return carry

    lax.fori_loop(0, FIELDS * 16 // CHUNK, pooled, 0)
    high, low = split(side_lhs[...])
    put_side(dot(high, table[0, 0:128, 0:width]) + dot(low, table[0, 0:128, 0:width]))


def first_kernel(
    msg, table, part_out, out, sums, lhs, small, side_lhs, acc, halo, coh, vec, weight, rows
):
    step = pl.program_id(0)
    lane_tile(msg, sums, lhs, small, side_lhs)
    for lt in range(FIRST):

        @pl.when(step == lt)
        def _():
            def put(at, value):
                for place, group in enumerate(FEEDS[lt]):
                    own = value[:, place * 128 : place * 128 + 128]
                    if group == 2:
                        if lt == 0:
                            part_out[at, :] = own
                        else:
                            part_out[at, :] += own
                    elif lt == min(i for i in range(FIRST) if group in FEEDS[i]):
                        acc[group, at, :] = own
                    else:
                        acc[group, at, :] += own

            def put_side(value):
                for place, group in enumerate(FEEDS[lt]):
                    own = value[:, place * 128 : place * 128 + 128]
                    if group == 2:
                        at = pl.ds(FIELDS * 16, SIDE)
                        if lt == 0:
                            part_out[at, :] = own
                        else:
                            part_out[at, :] += own
                    elif lt == min(i for i in range(FIRST) if group in FEEDS[i]):
                        halo[group] = own
                    else:
                        halo[group] += own

            pool_columns(lhs, side_lhs, table, 128 * len(FEEDS[lt]), put, put_side)

    @pl.when(step == FIRST - 1)
    def _():
        lane = lax.broadcasted_iota(jnp.int32, (8, 128), 1)
        last = lax.broadcasted_iota(jnp.int32, (8, 128), 0) == 7

        def below(group, t, u, part):
            return halo[group, pl.ds(part * 256 + t * 16 + u, 1), :]

        for half in range(2):

            def cov(t, u, part):
                value = acc[0, pl.ds((field_of(t, u) + part) * 16 + half * 8, 8), :]
                if half == 1:
                    value = value + jnp.where(last, below(0, t, u, part), 0.0)
                return value

            solve(cov, coh, vec, weight)
            for date in range(DATES):
                for part in range(2):
                    rows[part, date, 0, pl.ds(half, 8, stride=2), :] = vec[part, date]

        even = (lane >= 32) & (lane < 96)

        def cov_b(t, u, part):
            at = (field_of(t, u) + part) * 16
            value = jnp.where(even, acc[1, pl.ds(at, 8), :], acc[1, pl.ds(at + 8, 8), :])
            return value + jnp.where(last & ~even, below(1, t, u, part), 0.0)

        solve(cov_b, coh, vec, weight)
        for date in range(DATES):
            for part in range(2):
                value = vec[part, date]
                rows[part, date, 1, pl.ds(0, 8, stride=2), :] = value
                rows[part, date, 1, pl.ds(1, 8, stride=2), :] = pltpu.roll(value, 64, 1)
        out[:, :, :, 0:128] = rows[:, :, 0]
        left = lax.broadcasted_iota(jnp.int32, (2, DATES, BLOCKS, 128), 3) < 32
        out[:, :, :, 128:256] = jnp.where(left, rows[:, :, 0], rows[:, :, 1])


def last_kernel(
    msg, table, pool, partial, done, out, sums, lhs, small, side_lhs, acc, halo, edge, coh, vec,
    weight, rows,
):
    lane_tile(msg, sums, lhs, small, side_lhs)

    def put(at, value):
        acc[at, :] = value + partial[at, :]

    def put_side(value):
        halo[...] = value + partial[pl.ds(FIELDS * 16, SIDE), :]

    pool_columns(lhs, side_lhs, table, 128, put, put_side)
    for side in range(2):
        for t in range(DATES):
            for u_tile in range(t // 8, 2):
                row = 10 + 2 * side
                value = cross_products(small, t, u_tile, pl.ds(0, 128), [(row, row + 1)])
                for part in range(2):
                    at = part * 256 + t * 16 + u_tile * 8
                    side_lhs[pl.ds(at, 8), :] = value[part]
        high, low = split(side_lhs[...])
        for half in range(2):
            dims = (((1,), (1,)), ((), ()))
            weights = pool[half].astype(jnp.bfloat16)
            edge[side, half] = lax.dot_general(
                weights, high, dims, preferred_element_type=jnp.float32
            ) + lax.dot_general(weights, low, dims, preferred_element_type=jnp.float32)

    lane = lax.broadcasted_iota(jnp.int32, (8, 128), 1)
    last = lax.broadcasted_iota(jnp.int32, (8, 128), 0) == 7
    even = (lane < 32) | (lane >= 96)
    places = ((0, 0, 0), (0, 1, 64), (1, 0, 127), (1, 1, 63))

    def cov(t, u, part):
        at = (field_of(t, u) + part) * 16
        value = jnp.where(even, acc[pl.ds(at, 8), :], acc[pl.ds(at + 8, 8), :])
        index = part * 256 + t * 16 + u
        beside = jnp.where(last & ~even, halo[pl.ds(index, 1), :], 0.0)
        for side, half, target in places:
            source = edge[side, half, :, pl.ds(index // 128 * 128, 128)]
            turned = pltpu.roll(source, (target - index) % 128, 1)
            beside = beside + jnp.where(lane == target, turned, 0.0)
        return value + beside

    solve(cov, coh, vec, weight)
    for date in range(DATES):
        for part in range(2):
            value = vec[part, date]
            rows[part, date, 0, pl.ds(0, 8, stride=2), :] = value
            rows[part, date, 0, pl.ds(1, 8, stride=2), :] = pltpu.roll(value, 64, 1)
    place = lax.broadcasted_iota(jnp.int32, (2, DATES, BLOCKS, 128), 3)
    out[:, :, :, 0:128] = jnp.where(place < 32, rows[:, :, 0], done[:, :, :, 0:128])
    out[:, :, :, 128:256] = jnp.where(place >= 96, rows[:, :, 0], done[:, :, :, 128:256])


def solve(cov, coh, vec, weight):
    inv = []
    for t in range(DATES):
        diag = cov(t, t, 0)
        root = lax.rsqrt(jnp.maximum(diag, FLOOR))
        inv.append(root)
        weight[t] = diag * (root * root) + 1.0
    for i, (t, u) in enumerate(PAIRS):
        factor = inv[t] * inv[u]
        real = cov(t, u, 0) * factor
        imag = cov(t, u, 1) * factor
        coh[i, 0] = real
        coh[i, 1] = real + imag
        coh[i, 2] = imag - real
    for t in range(DATES):
        vec[0, t] = jnp.full((8, 128), 0.25, jnp.float32)
        vec[1, t] = jnp.zeros((8, 128), jnp.float32)
        vec[2, t] = jnp.full((8, 128), 0.25, jnp.float32)

    def iterate(_, carry):
        new_real, new_imag = [None] * DATES, [None] * DATES
        sums = [[None, None, None] for _ in range(DATES)]

        def add(t, which, value, minus=False):
            if sums[t][which] is None:
                sums[t][which] = -value if minus else value
            elif minus:
                sums[t][which] = sums[t][which] - value
            else:
                sums[t][which] = sums[t][which] + value

        def pair(t, u, v):
            i = PAIR_AT[t, u]
            real, plus, minus = coh[i, 0], coh[i, 1], coh[i, 2]
            add(t, 0, real * v[u][2])
            add(t, 1, plus * v[u][1])
            add(t, 2, minus * v[u][0])
            add(u, 0, real * v[t][2])
            add(u, 1, minus * v[t][1], True)
            add(u, 2, plus * v[t][0], True)

        for first in range(0, DATES, 4):
            for second in range(first, DATES, 4):
                dates = sorted(set(range(first, first + 4)) | set(range(second, second + 4)))
                v = {t: (vec[0, t], vec[1, t], vec[2, t]) for t in dates}
                for t in range(first, first + 4):
                    for u in range(second, second + 4):
                        if t < u:
                            pair(t, u, v)
        norm = None
        for t in range(DATES):
            own = weight[t]
            new_real[t] = (sums[t][0] - sums[t][1]) + own * vec[0, t]
            new_imag[t] = (sums[t][0] + sums[t][2]) + own * vec[1, t]
            square = new_real[t] * new_real[t] + new_imag[t] * new_imag[t]
            norm = square if norm is None else norm + square
        scale = lax.rsqrt(norm)
        for t in range(DATES):
            real, imag = new_real[t] * scale, new_imag[t] * scale
            vec[0, t] = real
            vec[1, t] = imag
            vec[2, t] = real + imag
        return carry

    lax.fori_loop(0, ITERS, iterate, 0)


def whole(*shape):
    return pl.BlockSpec(shape, lambda i: (0,) * len(shape))


def common_scratch(small_rows):
    return [
        pltpu.VMEM((DATES, 192, 128), jnp.float32),
        pltpu.VMEM((FIELDS * 16, 256), jnp.bfloat16),
        pltpu.VMEM((small_rows, DATES, 128), jnp.float32),
        pltpu.VMEM((SIDE, 128), jnp.float32),
    ]


SOLVE_SCRATCH = [
    pltpu.VMEM((len(PAIRS), 3, 8, 128), jnp.float32),
    pltpu.VMEM((3, DATES, 8, 128), jnp.float32),
    pltpu.VMEM((DATES, 8, 128), jnp.float32),
]
LINKED = (2, DATES, BLOCKS, OUT_COLS)


def link_first(message, tables):
    rows = FIELDS * 16 + SIDE
    return pl.pallas_call(
        first_kernel,
        grid=(FIRST,),
        in_specs=[
            pl.BlockSpec((DATES, MSG_ROWS, 128), lambda i: (0, 0, i)),
            pl.BlockSpec((1, 256, 256), lambda i: (i, 0, 0)),
        ],
        out_specs=[whole(rows, 128), whole(*LINKED)],
        out_shape=[
            jax.ShapeDtypeStruct((rows, 128), jnp.float32),
            jax.ShapeDtypeStruct(LINKED, jnp.float32),
        ],
        scratch_shapes=common_scratch(10)
        + [
            pltpu.VMEM((2, FIELDS * 16, 128), jnp.float32),
            pltpu.VMEM((2, SIDE, 128), jnp.float32),
        ]
        + SOLVE_SCRATCH
        + [pltpu.VMEM((2, DATES, 2, BLOCKS, 128), jnp.float32)],
        compiler_params=pltpu.CompilerParams(vmem_limit_bytes=VMEM_LIMIT),
        cost_estimate=pl.CostEstimate(flops=10**9, bytes_accessed=10**7, transcendentals=0),
        name="link_first",
    )(message, tables)


def link_last(message, tables, pool, partial, done):
    rows = FIELDS * 16 + SIDE
    return pl.pallas_call(
        last_kernel,
        grid=(1,),
        in_specs=[
            whole(DATES, MSG_ROWS, 128),
            pl.BlockSpec((1, 256, 128), lambda i: (FIRST, 0, 0)),
            whole(2, 8, 128),
            whole(rows, 128),
            whole(*LINKED),
        ],
        out_specs=whole(*LINKED),
        out_shape=jax.ShapeDtypeStruct(LINKED, jnp.float32),
        scratch_shapes=common_scratch(14)
        + [
            pltpu.VMEM((FIELDS * 16, 128), jnp.float32),
            pltpu.VMEM((SIDE, 128), jnp.float32),
            pltpu.VMEM((2, 2, 8, SIDE), jnp.float32),
        ]
        + SOLVE_SCRATCH
        + [pltpu.VMEM((2, DATES, 1, BLOCKS, 128), jnp.float32)],
        compiler_params=pltpu.CompilerParams(vmem_limit_bytes=VMEM_LIMIT),
        cost_estimate=pl.CostEstimate(flops=10**8, bytes_accessed=10**7, transcendentals=0),
        name="link_last",
    )(message, tables, pool, partial, done)


def local(slc, valid_rows):
    size = lax.axis_size("col")
    up = [(i, i + 1) for i in range(size - 1)]
    down = [(i + 1, i) for i in range(size - 1)]
    message1, message2, first, last = pack(slc, valid_rows)
    left = lax.ppermute(last, "col", up)
    right = lax.ppermute(first, "col", down)
    received1 = lax.all_to_all(message1, "row", 0, 0, tiled=True)
    left, right, received1 = lax.optimization_barrier((left, right, received1))
    message2 = insert_edges(left, right, message2)
    received2 = lax.all_to_all(message2, "row", 0, 0, tiled=True)
    tables, pool = column_tables()
    tables = jnp.asarray(tables, jnp.bfloat16)
    partial, done = link_first(received1, tables)
    return link_last(received2, tables, jnp.asarray(pool), partial, done)


def solution(mesh):
    return jax.shard_map(
        local,
        mesh=mesh,
        in_specs=(P(None, "row", None, "col"), P()),
        out_specs=P(None, None, "row", "col"),
        check_vma=False,
    )
```

```python
import functools

import jax
import jax.numpy as jnp
import numpy as np
from jax import lax
from jax.experimental import pallas as pl
from jax.experimental.pallas import tpu as pltpu
from jax.sharding import PartitionSpec as P

ITERS = 10
FLOOR = 20.0
DATES = 16
TILES = 16
COLS = 768
LANE_TILES = 6
FIRST = 5
OUT_COLS = 256
BLOCKS = 16
TILE_ROWS = 6 * BLOCKS
TILE_LANES = 192
ROWS1 = 1024
HALO1 = FIRST * TILE_LANES
ROWS2 = 208
HALO2 = TILE_LANES
EDGE_ROW = 202
GROUP1 = 4
GROUP2 = 8


def pair_groups():
    groups = []
    for i in range(0, DATES, 2):
        groups.append(([i], [i + 1]))
        rest = list(range(i + 2, DATES))
        for j in range(0, len(rest), 4):
            groups.append(([i, i + 1], rest[j : j + 4]))
    return groups


GROUPS = pair_groups()
PAIRS = [(t, u) for ts, us in GROUPS for t in ts for u in us]
PAIR_AT = {pair: i for i, pair in enumerate(PAIRS)}
FIELDS = DATES + 2 * len(PAIRS)
CHUNK = 512
SIDE = 512
VMEM_LIMIT = 56 * 1024 * 1024
FEEDS = ((0, 2), (0,), (0,), (0, 1), (1, 2), (2,))


def lane_columns():
    lane = np.arange(128)
    group_a = np.where(lane < 32, 128 + lane, lane)
    group_b = np.where((lane >= 32) & (lane < 96), 128 + lane, 128 + (lane + 64) % 128)
    own = np.where(lane < 32, lane, 128 + lane)
    other = (lane + 64) % 128
    far = np.where(other < 32, other, 128 + other)
    group_c = np.where((lane < 32) | (lane >= 96), own, far)
    return group_a, group_b, group_c


def column_tables():
    groups = lane_columns()
    tables = np.zeros((LANE_TILES, 256, 256), np.float32)
    for lt in range(LANE_TILES):
        column = (lt * 128 + np.arange(128) + 64) % COLS
        for place, group in enumerate(FEEDS[lt]):
            target = 3 * groups[group][None, :]
            inside = (column[:, None] >= target - 1) & (column[:, None] <= target + 3)
            for copy in range(2):
                tables[lt, copy * 128 : copy * 128 + 128, place * 128 : place * 128 + 128] = inside
    row = np.arange(128)
    pool = np.zeros((2, 8, 128), np.float32)
    for half in range(2):
        for s in range(8):
            block = 2 * s + half
            pool[half, s] = (row >= 6 * block) & (row <= 6 * block + 10)
    return tables, pool.reshape(16, 128)


def masked_rows(valid_ref, parts, step, span, rows_ref):
    me = lax.axis_index("row")
    low, high = valid_ref[0, me], valid_ref[1, me]
    count_out = rows_ref.shape[1]
    kept = []
    for which, (start, count) in enumerate(((-8, 8), (0, span), (span, 8))):
        row = lax.broadcasted_iota(jnp.int32, (count, 128), 0) + (step * span + start)
        keep = (row >= low) & (row < high)
        left = lax.broadcasted_iota(jnp.int32, (count, 128), 1) < 64
        for part in range(2):
            value = [jnp.where(keep, v, 0.0) for v in parts(which, part)]
            if which == 1:
                kept.append(value)
            turned = [pltpu.roll(v, 64, 1) for v in value]
            for lt in range(count_out):
                rows_ref[part, lt, pl.ds(start + 8, count), :] = jnp.where(
                    left, turned[lt], turned[(lt + 1) % len(turned)]
                )
    return kept


def spread(out, tile, base, first_row, rows_ref, lt):
    for part in range(2):
        for phase in range(6):
            for half in range(2):
                at = first_row + part * 96 + phase * 16 + half * 8
                out[tile, pl.ds(at, 8), :] = rows_ref[
                    part, lt, pl.ds(base + 6 * half + phase, 8, stride=12), :
                ]


def pack_first_kernel(valid_ref, before_ref, tile_ref, after_ref, out_ref, rows_ref):
    refs = (before_ref, tile_ref, after_ref)

    def parts(which, part):
        return [refs[which][part, 0, :, lt * 128 : lt * 128 + 128] for lt in range(LANE_TILES)]

    masked_rows(valid_ref, parts, pl.program_id(0), GROUP1 * TILE_ROWS, rows_ref)
    for tile in range(GROUP1):
        base = 5 + tile * TILE_ROWS
        out_ref[tile, pl.ds(ROWS1 - 16, 16), :] = jnp.zeros((16, 128), jnp.float32)
        for lt in range(FIRST):
            spread(out_ref, tile, base, lt * TILE_LANES, rows_ref, lt)
            for part in range(2):
                out_ref[tile, pl.ds(HALO1 + lt * 10 + 5 * part, 5), :] = rows_ref[
                    part, lt, pl.ds(base + TILE_ROWS, 5), :
                ]


def pack_last_kernel(
    valid_ref, l_before, l_tile, l_after, r_before, r_tile, r_after, out_ref, first_ref, last_ref,
    rows_ref,
):
    refs = ((r_before, l_before), (r_tile, l_tile), (r_after, l_after))

    def parts(which, part):
        return [ref[part, 0] for ref in refs[which]]

    kept = masked_rows(valid_ref, parts, pl.program_id(0), GROUP2 * TILE_ROWS, rows_ref)
    lane = lax.broadcasted_iota(jnp.int32, (8, 128), 1)
    for at, pick, out in ((1, 0, first_ref), (0, 127, last_ref)):
        for part in range(2):
            column = lax.dot_general(
                jnp.where(lane == pick, 1.0, 0.0), kept[part][at], (((1,), (1,)), ((), ())),
                precision=lax.Precision.HIGHEST, preferred_element_type=jnp.float32,
            )
            out[part : part + 1, :] = column[0:1, :]
    for tile in range(GROUP2):
        base = 5 + tile * TILE_ROWS
        spread(out_ref, tile, base, 0, rows_ref, 0)
        for part in range(2):
            out_ref[tile, pl.ds(HALO2 + 5 * part, 5), :] = rows_ref[
                part, 0, pl.ds(base + TILE_ROWS, 5), :
            ]
        out_ref[tile, pl.ds(EDGE_ROW, 6), :] = jnp.zeros((6, 128), jnp.float32)


def row_specs(span, width, column):
    eight = span // 8
    return [
        pl.BlockSpec((2, 1, 8, width), lambda i: (0, 0, jnp.maximum(i * eight - 1, 0), column)),
        pl.BlockSpec((2, 1, span, width), lambda i: (0, 0, i, column)),
        pl.BlockSpec(
            (2, 1, 8, width), lambda i: (0, 0, jnp.minimum(i * eight + eight, 191), column)
        ),
    ]


def pack_first(slc, valid):
    span = GROUP1 * TILE_ROWS
    return pl.pallas_call(
        pack_first_kernel,
        grid=(TILES // GROUP1,),
        in_specs=[pl.BlockSpec(memory_space=pltpu.SMEM)] + row_specs(span, COLS, 0),
        out_specs=pl.BlockSpec((GROUP1, ROWS1, 128), lambda i: (i, 0, 0)),
        out_shape=jax.ShapeDtypeStruct((TILES, ROWS1, 128), jnp.float32),
        scratch_shapes=[pltpu.VMEM((2, LANE_TILES, span + 16, 128), jnp.float32)],
        compiler_params=pltpu.CompilerParams(vmem_limit_bytes=VMEM_LIMIT),
        cost_estimate=pl.CostEstimate(flops=10**6, bytes_accessed=2 * 10**7, transcendentals=0),
        name="pack_first",
    )(valid, slc, slc, slc)


def pack_last(slc, valid):
    span = GROUP2 * TILE_ROWS
    column = jax.ShapeDtypeStruct((2, 1536), jnp.float32)
    return pl.pallas_call(
        pack_last_kernel,
        grid=(TILES // GROUP2,),
        in_specs=[pl.BlockSpec(memory_space=pltpu.SMEM)]
        + row_specs(span, 128, 0)
        + row_specs(span, 128, LANE_TILES - 1),
        out_specs=[
            pl.BlockSpec((GROUP2, ROWS2, 128), lambda i: (i, 0, 0)),
            pl.BlockSpec((2, span), lambda i: (0, i)),
            pl.BlockSpec((2, span), lambda i: (0, i)),
        ],
        out_shape=[jax.ShapeDtypeStruct((TILES, ROWS2, 128), jnp.float32), column, column],
        scratch_shapes=[pltpu.VMEM((2, 1, span + 16, 128), jnp.float32)],
        compiler_params=pltpu.CompilerParams(vmem_limit_bytes=VMEM_LIMIT),
        cost_estimate=pl.CostEstimate(flops=10**6, bytes_accessed=5 * 10**6, transcendentals=0),
        name="pack_last",
    )(valid, *([slc] * 6))


def insert_kernel(left_ref, right_ref, in_ref, out_ref, wide_ref):
    out_ref[...] = in_ref[...]
    wide_ref[...] = jnp.zeros_like(wide_ref)
    for side, ref in enumerate((left_ref, right_ref)):
        wide_ref[2 * side : 2 * side + 2, 128 : 128 + 1536] = ref[...]
    for tile in range(TILES):
        start = 128 + tile * TILE_ROWS - 3
        at = EDGE_ROW % 8
        out_ref[tile, at : at + 4, :] = wide_ref[0:4, start : start + 128]


def insert_edges(left, right, message):
    spec = pl.BlockSpec((TILES, 8, 128), lambda i: (0, EDGE_ROW // 8, 0))
    column = pl.BlockSpec((2, 1536), lambda i: (0, 0))
    return pl.pallas_call(
        insert_kernel,
        grid=(1,),
        in_specs=[column, column, spec],
        out_specs=spec,
        out_shape=jax.ShapeDtypeStruct(message.shape, message.dtype),
        input_output_aliases={2: 0},
        scratch_shapes=[pltpu.VMEM((8, 1920), jnp.float32)],
        name="insert_edges",
    )(left, right, message)


def split(x):
    high = x.astype(jnp.bfloat16)
    return high, (x - high.astype(jnp.float32)).astype(jnp.bfloat16)


def field_of(t, u):
    return t if t == u else DATES + 2 * PAIR_AT[t, u]


def cross_products(data, t_part, u_tile, lanes, rows):
    real = imag = None
    for re_row, im_row in rows:
        a_t = data[re_row, pl.ds(t_part, 1), lanes]
        b_t = data[im_row, pl.ds(t_part, 1), lanes]
        a_u = data[re_row, pl.ds(u_tile * 8, 8), lanes]
        b_u = data[im_row, pl.ds(u_tile * 8, 8), lanes]
        re = a_t * a_u + b_t * b_u
        im = b_t * a_u - a_t * b_u
        real = re if real is None else real + re
        imag = im if imag is None else imag + im
    return real, imag


def dot(a, b):
    return jnp.dot(a, b, preferred_element_type=jnp.float32)


def main_products(msg, sums, lhs, pooled):
    last = lax.broadcasted_iota(jnp.int32, (8, 128), 0) == 7
    state = {"fields": 0, "chunks": 0}

    def load(kind, date, phase, half):
        source = msg if kind in "ab" else sums
        base = 0 if kind in "as" else 96
        return source[date, pl.ds(base + phase * 16 + half * 8, 8), :]

    def emit(field, first, whole):
        out0 = whole[0] + first[1]
        rolled = jnp.where(last, 0.0, pltpu.roll(first[0], 7, 0))
        out1 = whole[1] + rolled
        high, low = split(jnp.concatenate([out0, out1], axis=0))
        lhs[pl.ds(field * 16, 16), 0:128] = high
        lhs[pl.ds(field * 16, 16), 128:256] = low
        state["fields"] += 1

    def drain():
        while (state["chunks"] + 1) * CHUNK <= state["fields"] * 16:
            pooled(state["chunks"])
            state["chunks"] += 1

    for t in range(DATES):
        first, whole = [], []
        for half in range(2):
            total = None
            for phase in range(6):
                a, b = load("a", t, phase, half), load("b", t, phase, half)
                term = a * a + b * b
                if phase == 5:
                    first.append(total)
                total = term if total is None else total + term
            whole.append(total)
        emit(t, first, whole)

    for ts, us in GROUPS:
        pairs = [(t, u) for t in ts for u in us]
        first = {pair: ([], []) for pair in pairs}
        whole = {pair: ([], []) for pair in pairs}
        for half in range(2):
            acc = {}
            for phase in range(6):
                s_t = {t: load("s", t, phase, half) for t in ts}
                a_t = {t: load("a", t, phase, half) for t in ts}
                b_t = {t: load("b", t, phase, half) for t in ts}
                a_u = {u: load("a", u, phase, half) for u in us}
                s_u = {u: load("s", u, phase, half) for u in us}
                d_u = {u: load("d", u, phase, half) for u in us}
                for t, u in pairs:
                    p = a_u[u] * s_t[t]
                    q = d_u[u] * b_t[t]
                    r = s_u[u] * a_t[t]
                    if phase == 0:
                        acc[t, u] = (p, q, r)
                    elif phase < 5:
                        p0, q0, r0 = acc[t, u]
                        acc[t, u] = (p0 + p, q0 + q, r0 + r)
                    else:
                        p0, q0, r0 = acc[t, u]
                        re5, im5 = p0 - q0, p0 - r0
                        first[t, u][0].append(re5)
                        first[t, u][1].append(im5)
                        whole[t, u][0].append(re5 + (p - q))
                        whole[t, u][1].append(im5 + (p - r))
        for pair in pairs:
            for part in range(2):
                emit(field_of(*pair) + part, first[pair][part], whole[pair][part])
        drain()


def dot(a, b):
    return jnp.dot(a, b, preferred_element_type=jnp.float32)


def side_products(small, t, rows, put):
    for u_tile in range(2):
        if u_tile < t // 8:
            values = (jnp.zeros((8, 128), jnp.float32),) * 2
        else:
            values = cross_products(small, t, u_tile, pl.ds(0, 128), rows)
        for part in range(2):
            put(part * 256 + t * 16 + u_tile * 8, values[part])


def fill_sums(msg, sums):
    def fill(date, carry):
        a = msg[date, pl.ds(0, 96), :]
        b = msg[date, pl.ds(96, 96), :]
        sums[date, pl.ds(0, 96), :] = a + b
        sums[date, pl.ds(96, 96), :] = a - b
        return carry

    lax.fori_loop(0, DATES, fill, 0, unroll=2)


def halo_products(small, side_lhs):
    def put(at, value):
        side_lhs[pl.ds(at, 8), :] = value

    for t in range(DATES):
        side_products(small, t, [(p, 5 + p) for p in range(5)], put)


def pool_side(side_lhs, table):
    high, low = split(side_lhs[...])
    return dot(jnp.concatenate([high, low], axis=1), table[0])


def chunk_rows(chunk):
    return pl.ds(chunk * CHUNK, CHUNK)


def first_kernel(
    msg, below_msg, table, part_out, out, sums, lhs, small, side_lhs, res, halo, coh, vec, weight,
    rows,
):
    step = pl.program_id(0)
    fill_sums(msg, sums)
    for date in range(DATES):
        for row in range(10):
            small[row, date : date + 1, :] = below_msg[date, pl.ds(step * 10 + row, 1), :]
    halo_products(small, side_lhs)
    halo[step] = pool_side(side_lhs, table)

    def pooled(chunk):
        res[step, chunk_rows(chunk), :] = dot(lhs[chunk_rows(chunk), :], table[0])

    main_products(msg, sums, lhs, pooled)

    @pl.when(step == FIRST - 1)
    def _():
        lane = lax.broadcasted_iota(jnp.int32, (8, 128), 1)
        last = lax.broadcasted_iota(jnp.int32, (8, 128), 0) == 7

        def total(ref, group, at, count):
            value = None
            for lt in range(FIRST):
                if group in FEEDS[lt]:
                    place = FEEDS[lt].index(group) * 128
                    own = ref[lt, pl.ds(at, count), place : place + 128]
                    value = own if value is None else value + own
            return value

        def below(group, t, u, part):
            return total(halo, group, part * 256 + t * 16 + u, 1)

        def paired(group, even, t, u, part):
            at = (field_of(t, u) + part) * 16
            value = jnp.where(even, total(res, group, at, 8), total(res, group, at + 8, 8))
            return value + jnp.where(last & ~even, below(group, t, u, part), 0.0)

        even = (lane < 32) | (lane >= 96)
        for t in range(DATES):
            for u in range(t, DATES):
                for part in range(1 if t == u else 2):
                    at = (field_of(t, u) + part) * 8
                    part_out[pl.ds(at, 8), :] = paired(2, even, t, u, part)

        for half in range(2):

            def cov(t, u, part):
                value = total(res, 0, (field_of(t, u) + part) * 16 + half * 8, 8)
                if half == 1:
                    value = value + jnp.where(last, below(0, t, u, part), 0.0)
                return value

            solve(cov, coh, vec, weight)
            for date in range(DATES):
                for part in range(2):
                    rows[part, date, 0, pl.ds(half, 8, stride=2), :] = vec[part, date]

        even_b = (lane >= 32) & (lane < 96)
        solve(functools.partial(paired, 1, even_b), coh, vec, weight)
        for date in range(DATES):
            for part in range(2):
                value = vec[part, date]
                rows[part, date, 1, pl.ds(0, 8, stride=2), :] = value
                rows[part, date, 1, pl.ds(1, 8, stride=2), :] = pltpu.roll(value, 64, 1)
        out[:, :, :, 0:128] = rows[:, :, 0]
        left = lax.broadcasted_iota(jnp.int32, (2, DATES, BLOCKS, 128), 3) < 32
        out[:, :, :, 128:256] = jnp.where(left, rows[:, :, 0], rows[:, :, 1])


def last_kernel(
    msg, table, pool, partial_hbm, done_hbm, out, sums, lhs, small, side_lhs, res, halo,
    pairs, edge, coh, vec, weight, rows, partial, done, sems,
):
    copies = [
        pltpu.make_async_copy(partial_hbm, partial, sems.at[0]),
        pltpu.make_async_copy(done_hbm, done, sems.at[1]),
    ]
    for copy in copies:
        copy.start()
    fill_sums(msg, sums)
    for date in range(DATES):
        for row in range(14):
            small[row, date : date + 1, :] = msg[date, HALO2 + row : HALO2 + row + 1, :]
    halo_products(small, side_lhs)
    high, low = split(side_lhs[...])
    halo[...] = dot(jnp.concatenate([high, low], axis=1), table[0])
    for side in range(2):
        row = 10 + 2 * side

        def put(at, value):
            pairs[pl.ds(2 * at + 1 - side, 8, stride=2), :] = value

        for t in range(DATES):
            side_products(small, t, [(row, row + 1)], put)
    dims = (((1,), (1,)), ((), ()))
    high, low = split(pairs[...])
    pool2 = pool[...].astype(jnp.bfloat16)
    sides = lax.dot_general(
        pool2, high, dims, preferred_element_type=jnp.float32
    ) + lax.dot_general(pool2, low, dims, preferred_element_type=jnp.float32)
    lower = lax.broadcasted_iota(jnp.int32, (8, 128), 1) < 64
    for group in range(SIDE // 64):
        tile = slice(group * 128, group * 128 + 128)
        even_rows, odd_rows = sides[0:8, tile], sides[8:16, tile]
        edge[2 * group] = jnp.where(lower, even_rows, pltpu.roll(odd_rows, 64, 1))
        edge[2 * group + 1] = jnp.where(lower, pltpu.roll(even_rows, 64, 1), odd_rows)

    def pooled(chunk):
        res[chunk_rows(chunk), :] = dot(lhs[chunk_rows(chunk), :], table[0])

    main_products(msg, sums, lhs, pooled)

    lane = lax.broadcasted_iota(jnp.int32, (8, 128), 1)
    last = lax.broadcasted_iota(jnp.int32, (8, 128), 0) == 7
    even = (lane < 32) | (lane >= 96)
    beside = (lane == 0) | (lane == 127) | (lane == 63) | (lane == 64)
    for copy in copies:
        copy.wait()

    def cov(t, u, part):
        field = field_of(t, u) + part
        at = field * 16
        value = jnp.where(even, res[pl.ds(at, 8), :], res[pl.ds(at + 8, 8), :])
        index = part * 256 + t * 16 + u
        value = value + jnp.where(last & ~even, halo[pl.ds(index, 1), :], 0.0)
        turned = pltpu.roll(edge[index // 32], (127 - 2 * (index % 32)) % 128, 1)
        return value + partial[pl.ds(field * 8, 8), :] + jnp.where(beside, turned, 0.0)

    solve(cov, coh, vec, weight)
    for date in range(DATES):
        for part in range(2):
            value = vec[part, date]
            rows[part, date, 0, pl.ds(0, 8, stride=2), :] = value
            rows[part, date, 0, pl.ds(1, 8, stride=2), :] = pltpu.roll(value, 64, 1)
    place = lax.broadcasted_iota(jnp.int32, (2, DATES, BLOCKS, 128), 3)
    out[:, :, :, 0:128] = jnp.where(place < 32, rows[:, :, 0], done[:, :, :, 0:128])
    out[:, :, :, 128:256] = jnp.where(place >= 96, rows[:, :, 0], done[:, :, :, 128:256])


def inverse_norm(vec):
    terms = [vec[part, t] * vec[part, t] for t in range(DATES) for part in range(2)]
    while len(terms) > 1:
        terms = [terms[i] + terms[i + 1] for i in range(0, len(terms), 2)]
    return lax.rsqrt(terms[0])


def solve(cov, coh, vec, weight):
    inv = []
    for t in range(DATES):
        diag = cov(t, t, 0)
        root = lax.rsqrt(jnp.maximum(diag, FLOOR))
        inv.append(root)
        weight[t] = diag * (root * root) + 1.0
    for i, (t, u) in enumerate(PAIRS):
        factor = inv[t] * inv[u]
        real = cov(t, u, 0) * factor
        imag = cov(t, u, 1) * factor
        coh[i, 0] = real
        coh[i, 1] = real + imag
        coh[i, 2] = imag - real
    for t in range(DATES):
        vec[0, t] = jnp.full((8, 128), 0.25, jnp.float32)
        vec[1, t] = jnp.zeros((8, 128), jnp.float32)
        vec[2, t] = jnp.full((8, 128), 0.25, jnp.float32)

    def iterate(_, carry):
        scale = inverse_norm(vec)
        new_real, new_imag = [None] * DATES, [None] * DATES
        sums = [[None, None, None] for _ in range(DATES)]

        def add(t, which, value, minus=False):
            if sums[t][which] is None:
                sums[t][which] = -value if minus else value
            elif minus:
                sums[t][which] = sums[t][which] - value
            else:
                sums[t][which] = sums[t][which] + value

        def pair(t, u, v):
            i = PAIR_AT[t, u]
            real, plus, minus = coh[i, 0], coh[i, 1], coh[i, 2]
            add(t, 0, real * v[u][2])
            add(t, 1, plus * v[u][1])
            add(t, 2, minus * v[u][0])
            add(u, 0, real * v[t][2])
            add(u, 1, minus * v[t][1], True)
            add(u, 2, plus * v[t][0], True)

        for first in range(0, DATES, 4):
            for second in range(first, DATES, 4):
                dates = sorted(set(range(first, first + 4)) | set(range(second, second + 4)))
                v = {t: (vec[0, t], vec[1, t], vec[2, t]) for t in dates}
                for t in range(first, first + 4):
                    for u in range(second, second + 4):
                        if t < u:
                            pair(t, u, v)
        for t in range(DATES):
            own = weight[t]
            new_real[t] = (sums[t][0] - sums[t][1]) + own * vec[0, t]
            new_imag[t] = (sums[t][0] + sums[t][2]) + own * vec[1, t]
        for t in range(DATES):
            real, imag = new_real[t] * scale, new_imag[t] * scale
            vec[0, t] = real
            vec[1, t] = imag
            vec[2, t] = real + imag
        return carry

    lax.fori_loop(0, ITERS, iterate, 0)
    scale = inverse_norm(vec)
    for t in range(DATES):
        for part in range(2):
            vec[part, t] = vec[part, t] * scale


def whole(*shape):
    return pl.BlockSpec(shape, lambda i: (0,) * len(shape))


def common_scratch(small_rows):
    return [
        pltpu.VMEM((DATES, TILE_LANES, 128), jnp.float32),
        pltpu.VMEM((FIELDS * 16, 256), jnp.bfloat16),
        pltpu.VMEM((small_rows, DATES, 128), jnp.float32),
        pltpu.VMEM((SIDE, 128), jnp.float32),
    ]


SOLVE_SCRATCH = [
    pltpu.VMEM((len(PAIRS), 3, 8, 128), jnp.float32),
    pltpu.VMEM((3, DATES, 8, 128), jnp.float32),
    pltpu.VMEM((DATES, 8, 128), jnp.float32),
]
LINKED = (2, DATES, BLOCKS, OUT_COLS)
PARTIAL = (FIELDS * 8, 128)


def link_first(message, tables):
    return pl.pallas_call(
        first_kernel,
        grid=(FIRST,),
        in_specs=[
            pl.BlockSpec((DATES, TILE_LANES, 128), lambda i: (0, i, 0)),
            pl.BlockSpec((DATES, 64, 128), lambda i: (0, HALO1 // 64, 0)),
            pl.BlockSpec((1, 256, 256), lambda i: (i, 0, 0)),
        ],
        out_specs=[whole(*PARTIAL), whole(*LINKED)],
        out_shape=[
            jax.ShapeDtypeStruct(PARTIAL, jnp.float32),
            jax.ShapeDtypeStruct(LINKED, jnp.float32),
        ],
        scratch_shapes=common_scratch(10)
        + [
            pltpu.VMEM((FIRST, FIELDS * 16, 256), jnp.float32),
            pltpu.VMEM((FIRST, SIDE, 256), jnp.float32),
        ]
        + SOLVE_SCRATCH
        + [pltpu.VMEM((2, DATES, 2, BLOCKS, 128), jnp.float32)],
        compiler_params=pltpu.CompilerParams(vmem_limit_bytes=VMEM_LIMIT),
        cost_estimate=pl.CostEstimate(flops=10**9, bytes_accessed=10**7, transcendentals=0),
        name="link_first",
    )(message, message, tables)


def link_last(message, tables, pool, partial, done):
    return pl.pallas_call(
        last_kernel,
        grid=(1,),
        in_specs=[
            whole(DATES, ROWS2, 128),
            pl.BlockSpec((1, 256, 128), lambda i: (FIRST, 0, 0)),
            whole(16, 128),
            pl.BlockSpec(memory_space=pl.ANY),
            pl.BlockSpec(memory_space=pl.ANY),
        ],
        out_specs=whole(*LINKED),
        out_shape=jax.ShapeDtypeStruct(LINKED, jnp.float32),
        scratch_shapes=common_scratch(14)
        + [
            pltpu.VMEM((FIELDS * 16, 128), jnp.float32),
            pltpu.VMEM((SIDE, 128), jnp.float32),
            pltpu.VMEM((2 * SIDE, 128), jnp.float32),
            pltpu.VMEM((SIDE // 32, 8, 128), jnp.float32),
        ]
        + SOLVE_SCRATCH
        + [
            pltpu.VMEM((2, DATES, 1, BLOCKS, 128), jnp.float32),
            pltpu.VMEM(PARTIAL, jnp.float32),
            pltpu.VMEM(LINKED, jnp.float32),
            pltpu.SemaphoreType.DMA((2,)),
        ],
        compiler_params=pltpu.CompilerParams(vmem_limit_bytes=VMEM_LIMIT),
        cost_estimate=pl.CostEstimate(flops=10**8, bytes_accessed=10**7, transcendentals=0),
        name="link_last",
    )(message, tables, pool, partial, done)


def local(slc, valid_rows):
    size = lax.axis_size("col")
    up = [(i, i + 1) for i in range(size - 1)]
    down = [(i + 1, i) for i in range(size - 1)]
    valid = valid_rows.T
    message2, first, last = pack_last(slc, valid)
    left = lax.ppermute(last, "col", up)
    right = lax.ppermute(first, "col", down)
    slc, message2 = lax.optimization_barrier((slc, message2))
    message1 = pack_first(slc, valid)
    message2 = insert_edges(left, right, message2)
    message1, message2 = lax.optimization_barrier((message1, message2))
    received1 = lax.all_to_all(message1, "row", 0, 0, tiled=True)
    received1, message2 = lax.optimization_barrier((received1, message2))
    received2 = lax.all_to_all(message2, "row", 0, 0, tiled=True)
    tables, pool = column_tables()
    tables = jnp.asarray(tables, jnp.bfloat16)
    partial, done = link_first(received1, tables)
    return link_last(received2, tables, jnp.asarray(pool), partial, done)


def solution(mesh):
    return jax.shard_map(
        local,
        mesh=mesh,
        in_specs=(P(None, "row", None, "col"), P()),
        out_specs=P(None, None, "row", "col"),
        check_vma=False,
    )
```

```python
import functools

import jax
import jax.numpy as jnp
import numpy as np
from jax import lax
from jax.experimental import pallas as pl
from jax.experimental.pallas import tpu as pltpu
from jax.sharding import PartitionSpec as P

ITERS = 10
FLOOR = 20.0
DATES = 16
TILES = 16
COLS = 768
LANE_TILES = 6
FIRST = 5
OUT_COLS = 256
BLOCKS = 16
TILE_ROWS = 6 * BLOCKS
TILE_LANES = 192
ROWS1 = 1024
HALO1 = FIRST * TILE_LANES
OWN_TILE = 1008
OWN_ROW = 1010
ROWS2 = 208
HALO2 = TILE_LANES
WINDOW = TILE_ROWS + 5
GROUP = 4


def pair_groups():
    groups = []
    for i in range(0, DATES, 2):
        groups.append(([i], [i + 1]))
        rest = list(range(i + 2, DATES))
        for j in range(0, len(rest), 4):
            groups.append(([i, i + 1], rest[j : j + 4]))
    return groups


GROUPS = pair_groups()
PAIRS = [(t, u) for ts, us in GROUPS for t in ts for u in us]
PAIR_AT = {pair: i for i, pair in enumerate(PAIRS)}
FIELDS = DATES + 2 * len(PAIRS)
CHUNK = 512
SIDE = 512
FEEDS = ((0, 2), (0,), (0,), (0, 1), (1, 2), (2,))


def lane_columns():
    lane = np.arange(128)
    group_a = np.where(lane < 32, 128 + lane, lane)
    group_b = np.where((lane >= 32) & (lane < 96), 128 + lane, 128 + (lane + 64) % 128)
    own = np.where(lane < 32, lane, 128 + lane)
    other = (lane + 64) % 128
    far = np.where(other < 32, other, 128 + other)
    group_c = np.where((lane < 32) | (lane >= 96), own, far)
    return group_a, group_b, group_c


def column_tables():
    groups = lane_columns()
    tables = np.zeros((LANE_TILES, 256, 256), np.float32)
    for lt in range(LANE_TILES):
        column = (lt * 128 + np.arange(128) + 64) % COLS
        for place, group in enumerate(FEEDS[lt]):
            target = 3 * groups[group][None, :]
            inside = (column[:, None] >= target - 1) & (column[:, None] <= target + 3)
            for copy in range(2):
                tables[lt, copy * 128 : copy * 128 + 128, place * 128 : place * 128 + 128] = inside
    row = np.arange(128)
    pool = np.zeros((2, 8, 128), np.float32)
    for half in range(2):
        for s in range(8):
            block = 2 * s + half
            pool[half, s] = (row >= 6 * block) & (row <= 6 * block + 10)
    return tables, pool.reshape(16, 128)


def pack_kernel(valid_ref, before_ref, tile_ref, after_ref, out1_ref, out2_ref, rows_ref):
    me = lax.axis_index("row")
    step = pl.program_id(0)
    low, high = valid_ref[0, me], valid_ref[1, me]
    span = GROUP * TILE_ROWS
    for ref, start, count in ((before_ref, -8, 8), (tile_ref, 0, span), (after_ref, span, 8)):
        row = lax.broadcasted_iota(jnp.int32, (count, 128), 0) + (step * span + start)
        keep = (row >= low) & (row < high)
        left = lax.broadcasted_iota(jnp.int32, (count, 128), 1) < 64
        for part in range(2):
            turned = []
            for lt in range(LANE_TILES):
                value = ref[part, 0, :, lt * 128 : lt * 128 + 128]
                turned.append(pltpu.roll(jnp.where(keep, value, 0.0), 64, 1))
            for lt in range(LANE_TILES):
                rows_ref[part, lt, pl.ds(start + 8, count), :] = jnp.where(
                    left, turned[lt], turned[(lt + 1) % LANE_TILES]
                )
    lane = lax.broadcasted_iota(jnp.int32, (8, 128), 1)
    row = lax.broadcasted_iota(jnp.int32, (8, 128), 0)
    pick = jnp.where(((row == 0) & (lane == 64)) | ((row == 1) & (lane == 63)), 1.0, 0.0)
    for tile in range(GROUP):
        base = 5 + tile * TILE_ROWS
        out1_ref[tile, pl.ds(ROWS1 - 16, 16), :] = jnp.zeros((16, 128), jnp.float32)
        out2_ref[tile, pl.ds(ROWS2 - 16, 16), :] = jnp.zeros((16, 128), jnp.float32)
        for part in range(2):
            columns = lax.dot_general(
                pick, rows_ref[part, LANE_TILES - 1, pl.ds(base, 128), :],
                (((1,), (1,)), ((), ())),
                precision=lax.Precision.HIGHEST, preferred_element_type=jnp.float32,
            )
            columns = jnp.where(lane < WINDOW + 1, columns, 0.0)
            for side in range(2):
                out1_ref[tile, pl.ds(OWN_ROW + 2 * side + part, 1), :] = columns[side : side + 1]
        for lt in range(LANE_TILES):
            out = out1_ref if lt < FIRST else out2_ref
            top = lt * TILE_LANES if lt < FIRST else 0
            below = HALO1 + lt * 10 if lt < FIRST else HALO2
            for part in range(2):
                for phase in range(6):
                    for half in range(2):
                        at = top + part * 96 + phase * 16 + half * 8
                        out[tile, pl.ds(at, 8), :] = rows_ref[
                            part, lt, pl.ds(base + 6 * half + phase, 8, stride=12), :
                        ]
                out[tile, pl.ds(below + 5 * part, 5), :] = rows_ref[
                    part, lt, pl.ds(base + TILE_ROWS, 5), :
                ]


def pack(slc, valid):
    span = GROUP * TILE_ROWS
    eight = span // 8
    return pl.pallas_call(
        pack_kernel,
        grid=(TILES // GROUP,),
        in_specs=[
            pl.BlockSpec(memory_space=pltpu.SMEM),
            pl.BlockSpec((2, 1, 8, COLS), lambda i: (0, 0, jnp.maximum(i * eight - 1, 0), 0)),
            pl.BlockSpec((2, 1, span, COLS), lambda i: (0, 0, i, 0)),
            pl.BlockSpec((2, 1, 8, COLS), lambda i: (0, 0, jnp.minimum(i * eight + eight, 191), 0)),
        ],
        out_specs=[
            pl.BlockSpec((GROUP, ROWS1, 128), lambda i: (i, 0, 0)),
            pl.BlockSpec((GROUP, ROWS2, 128), lambda i: (i, 0, 0)),
        ],
        out_shape=[
            jax.ShapeDtypeStruct((TILES, ROWS1, 128), jnp.float32),
            jax.ShapeDtypeStruct((TILES, ROWS2, 128), jnp.float32),
        ],
        scratch_shapes=[pltpu.VMEM((2, LANE_TILES, span + 48, 128), jnp.float32)],
        compiler_params=pltpu.CompilerParams(vmem_limit_bytes=20 * 1024 * 1024),
        cost_estimate=pl.CostEstimate(flops=10**6, bytes_accessed=2 * 10**7, transcendentals=0),
        name="pack",
    )(valid, slc, slc, slc)


def split(x):
    high = x.astype(jnp.bfloat16)
    return high, (x - high.astype(jnp.float32)).astype(jnp.bfloat16)


def field_of(t, u):
    return t if t == u else DATES + 2 * PAIR_AT[t, u]


def cross_products(data, t_part, u_tile, lanes, rows):
    real = imag = None
    for re_row, im_row in rows:
        a_t = data[re_row, pl.ds(t_part, 1), lanes]
        b_t = data[im_row, pl.ds(t_part, 1), lanes]
        a_u = data[re_row, pl.ds(u_tile * 8, 8), lanes]
        b_u = data[im_row, pl.ds(u_tile * 8, 8), lanes]
        re = a_t * a_u + b_t * b_u
        im = b_t * a_u - a_t * b_u
        real = re if real is None else real + re
        imag = im if imag is None else imag + im
    return real, imag


def dot(a, b):
    return jnp.dot(a, b, preferred_element_type=jnp.float32)


def main_products(msg, sums, lhs, pooled):
    last = lax.broadcasted_iota(jnp.int32, (8, 128), 0) == 7
    state = {"fields": 0, "chunks": 0}

    def load(kind, date, phase, half):
        source = msg if kind in "ab" else sums
        base = 0 if kind in "as" else 96
        return source[date, pl.ds(base + phase * 16 + half * 8, 8), :]

    def emit(field, first, whole):
        out0 = whole[0] + first[1]
        rolled = jnp.where(last, 0.0, pltpu.roll(first[0], 7, 0))
        out1 = whole[1] + rolled
        high, low = split(jnp.concatenate([out0, out1], axis=0))
        lhs[pl.ds(field * 16, 16), 0:128] = high
        lhs[pl.ds(field * 16, 16), 128:256] = low
        state["fields"] += 1

    def drain():
        while (state["chunks"] + 1) * CHUNK <= state["fields"] * 16:
            pooled(state["chunks"])
            state["chunks"] += 1

    for t in range(DATES):
        first, whole = [], []
        for half in range(2):
            total = None
            for phase in range(6):
                a, b = load("a", t, phase, half), load("b", t, phase, half)
                term = a * a + b * b
                if phase == 5:
                    first.append(total)
                total = term if total is None else total + term
            whole.append(total)
        emit(t, first, whole)

    for ts, us in GROUPS:
        pairs = [(t, u) for t in ts for u in us]
        first = {pair: ([], []) for pair in pairs}
        whole = {pair: ([], []) for pair in pairs}
        for half in range(2):
            acc = {}
            for phase in range(6):
                s_t = {t: load("s", t, phase, half) for t in ts}
                a_t = {t: load("a", t, phase, half) for t in ts}
                b_t = {t: load("b", t, phase, half) for t in ts}
                a_u = {u: load("a", u, phase, half) for u in us}
                s_u = {u: load("s", u, phase, half) for u in us}
                d_u = {u: load("d", u, phase, half) for u in us}
                for t, u in pairs:
                    p = a_u[u] * s_t[t]
                    q = d_u[u] * b_t[t]
                    r = s_u[u] * a_t[t]
                    if phase == 0:
                        acc[t, u] = (p, q, r)
                    elif phase < 5:
                        p0, q0, r0 = acc[t, u]
                        acc[t, u] = (p0 + p, q0 + q, r0 + r)
                    else:
                        p0, q0, r0 = acc[t, u]
                        re5, im5 = p0 - q0, p0 - r0
                        first[t, u][0].append(re5)
                        first[t, u][1].append(im5)
                        whole[t, u][0].append(re5 + (p - q))
                        whole[t, u][1].append(im5 + (p - r))
        for pair in pairs:
            for part in range(2):
                emit(field_of(*pair) + part, first[pair][part], whole[pair][part])
        drain()


def dot(a, b):
    return jnp.dot(a, b, preferred_element_type=jnp.float32)


def side_products(small, t, rows, put):
    for u_tile in range(2):
        if u_tile < t // 8:
            values = (jnp.zeros((8, 128), jnp.float32),) * 2
        else:
            values = cross_products(small, t, u_tile, pl.ds(0, 128), rows)
        for part in range(2):
            put(part * 256 + t * 16 + u_tile * 8, values[part])


def fill_sums(msg, sums):
    def fill(date, carry):
        a = msg[date, pl.ds(0, 96), :]
        b = msg[date, pl.ds(96, 96), :]
        sums[date, pl.ds(0, 96), :] = a + b
        sums[date, pl.ds(96, 96), :] = a - b
        return carry

    lax.fori_loop(0, DATES, fill, 0, unroll=2)


def halo_products(small, side_lhs):
    def put(at, value):
        side_lhs[pl.ds(at, 8), :] = value

    for t in range(DATES):
        side_products(small, t, [(p, 5 + p) for p in range(5)], put)


def pool_side(side_lhs, table):
    high, low = split(side_lhs[...])
    return dot(jnp.concatenate([high, low], axis=1), table[0])


def chunk_rows(chunk):
    return pl.ds(chunk * CHUNK, CHUNK)


def first_kernel(
    msg, below_msg, table, part_out, out, sums, lhs, small, side_lhs, res, halo, coh, vec, weight,
    rows,
):
    step = pl.program_id(0)
    fill_sums(msg, sums)
    for date in range(DATES):
        for row in range(10):
            small[row, date : date + 1, :] = below_msg[date, pl.ds(step * 10 + row, 1), :]
    halo_products(small, side_lhs)
    halo[step] = pool_side(side_lhs, table)

    def pooled(chunk):
        res[step, chunk_rows(chunk), :] = dot(lhs[chunk_rows(chunk), :], table[0])

    main_products(msg, sums, lhs, pooled)

    @pl.when(step == FIRST - 1)
    def _():
        lane = lax.broadcasted_iota(jnp.int32, (8, 128), 1)
        last = lax.broadcasted_iota(jnp.int32, (8, 128), 0) == 7

        def total(ref, group, at, count):
            value = None
            for lt in range(FIRST):
                if group in FEEDS[lt]:
                    place = FEEDS[lt].index(group) * 128
                    own = ref[lt, pl.ds(at, count), place : place + 128]
                    value = own if value is None else value + own
            return value

        def below(group, t, u, part):
            return total(halo, group, part * 256 + t * 16 + u, 1)

        def paired(group, even, t, u, part):
            at = (field_of(t, u) + part) * 16
            value = jnp.where(even, total(res, group, at, 8), total(res, group, at + 8, 8))
            return value + jnp.where(last & ~even, below(group, t, u, part), 0.0)

        even = (lane < 32) | (lane >= 96)
        for t in range(DATES):
            for u in range(t, DATES):
                for part in range(1 if t == u else 2):
                    at = (field_of(t, u) + part) * 8
                    part_out[pl.ds(at, 8), :] = paired(2, even, t, u, part)

        for half in range(2):

            def cov(t, u, part):
                value = total(res, 0, (field_of(t, u) + part) * 16 + half * 8, 8)
                if half == 1:
                    value = value + jnp.where(last, below(0, t, u, part), 0.0)
                return value

            solve(cov, coh, vec, weight)
            for date in range(DATES):
                for part in range(2):
                    rows[part, date, 0, pl.ds(half, 8, stride=2), :] = vec[part, date]

        even_b = (lane >= 32) & (lane < 96)
        solve(functools.partial(paired, 1, even_b), coh, vec, weight)
        for date in range(DATES):
            for part in range(2):
                value = vec[part, date]
                rows[part, date, 1, pl.ds(0, 8, stride=2), :] = value
                rows[part, date, 1, pl.ds(1, 8, stride=2), :] = pltpu.roll(value, 64, 1)
        out[:, :, :, 0:128] = rows[:, :, 0]
        left = lax.broadcasted_iota(jnp.int32, (2, DATES, BLOCKS, 128), 3) < 32
        out[:, :, :, 128:256] = jnp.where(left, rows[:, :, 0], rows[:, :, 1])


def last_kernel(
    msg, left, right, table, pool, partial_hbm, done_hbm, out, sums, lhs, small, side_lhs, res, halo,
    pairs, edge, coh, vec, weight, rows, partial, done, sems,
):
    copies = [
        pltpu.make_async_copy(partial_hbm, partial, sems.at[0]),
        pltpu.make_async_copy(done_hbm, done, sems.at[1]),
    ]
    for copy in copies:
        copy.start()
    fill_sums(msg, sums)
    for date in range(DATES):
        for row in range(10):
            small[row, date : date + 1, :] = msg[date, HALO2 + row : HALO2 + row + 1, :]
        for part in range(2):
            own = OWN_ROW - OWN_TILE + part
            small[10 + part, date : date + 1, :] = left[date, own + 2 : own + 3, :]
            small[12 + part, date : date + 1, :] = right[date, own : own + 1, :]
    halo_products(small, side_lhs)
    high, low = split(side_lhs[...])
    halo[...] = dot(jnp.concatenate([high, low], axis=1), table[0])
    for side in range(2):
        row = 10 + 2 * side

        def put(at, value):
            pairs[pl.ds(2 * at + 1 - side, 8, stride=2), :] = value

        for t in range(DATES):
            side_products(small, t, [(row, row + 1)], put)
    dims = (((1,), (1,)), ((), ()))
    high, low = split(pairs[...])
    pool2 = pool[...].astype(jnp.bfloat16)
    sides = lax.dot_general(
        pool2, high, dims, preferred_element_type=jnp.float32
    ) + lax.dot_general(pool2, low, dims, preferred_element_type=jnp.float32)
    lower = lax.broadcasted_iota(jnp.int32, (8, 128), 1) < 64
    for group in range(SIDE // 64):
        tile = slice(group * 128, group * 128 + 128)
        even_rows, odd_rows = sides[0:8, tile], sides[8:16, tile]
        edge[2 * group] = jnp.where(lower, even_rows, pltpu.roll(odd_rows, 64, 1))
        edge[2 * group + 1] = jnp.where(lower, pltpu.roll(even_rows, 64, 1), odd_rows)

    def pooled(chunk):
        res[chunk_rows(chunk), :] = dot(lhs[chunk_rows(chunk), :], table[0])

    main_products(msg, sums, lhs, pooled)

    lane = lax.broadcasted_iota(jnp.int32, (8, 128), 1)
    last = lax.broadcasted_iota(jnp.int32, (8, 128), 0) == 7
    even = (lane < 32) | (lane >= 96)
    beside = (lane == 0) | (lane == 127) | (lane == 63) | (lane == 64)
    for copy in copies:
        copy.wait()

    def cov(t, u, part):
        field = field_of(t, u) + part
        at = field * 16
        value = jnp.where(even, res[pl.ds(at, 8), :], res[pl.ds(at + 8, 8), :])
        index = part * 256 + t * 16 + u
        value = value + jnp.where(last & ~even, halo[pl.ds(index, 1), :], 0.0)
        turned = pltpu.roll(edge[index // 32], (127 - 2 * (index % 32)) % 128, 1)
        return value + partial[pl.ds(field * 8, 8), :] + jnp.where(beside, turned, 0.0)

    solve(cov, coh, vec, weight)
    for date in range(DATES):
        for part in range(2):
            value = vec[part, date]
            rows[part, date, 0, pl.ds(0, 8, stride=2), :] = value
            rows[part, date, 0, pl.ds(1, 8, stride=2), :] = pltpu.roll(value, 64, 1)
    place = lax.broadcasted_iota(jnp.int32, (2, DATES, BLOCKS, 128), 3)
    out[:, :, :, 0:128] = jnp.where(place < 32, rows[:, :, 0], done[:, :, :, 0:128])
    out[:, :, :, 128:256] = jnp.where(place >= 96, rows[:, :, 0], done[:, :, :, 128:256])


def inverse_norm(vec):
    terms = [vec[part, t] * vec[part, t] for t in range(DATES) for part in range(2)]
    while len(terms) > 1:
        terms = [terms[i] + terms[i + 1] for i in range(0, len(terms), 2)]
    return lax.rsqrt(terms[0])


def solve(cov, coh, vec, weight):
    inv = []
    for t in range(DATES):
        diag = cov(t, t, 0)
        root = lax.rsqrt(jnp.maximum(diag, FLOOR))
        inv.append(root)
        weight[t] = diag * (root * root) + 1.0
    for i, (t, u) in enumerate(PAIRS):
        factor = inv[t] * inv[u]
        real = cov(t, u, 0) * factor
        imag = cov(t, u, 1) * factor
        coh[i, 0] = real
        coh[i, 1] = real + imag
        coh[i, 2] = imag - real
    for t in range(DATES):
        vec[0, t] = jnp.full((8, 128), 0.25, jnp.float32)
        vec[1, t] = jnp.zeros((8, 128), jnp.float32)
        vec[2, t] = jnp.full((8, 128), 0.25, jnp.float32)

    def iterate(_, carry):
        scale = inverse_norm(vec)
        new_real, new_imag = [None] * DATES, [None] * DATES
        sums = [[None, None, None] for _ in range(DATES)]

        def add(t, which, value, minus=False):
            if sums[t][which] is None:
                sums[t][which] = -value if minus else value
            elif minus:
                sums[t][which] = sums[t][which] - value
            else:
                sums[t][which] = sums[t][which] + value

        def pair(t, u, v):
            i = PAIR_AT[t, u]
            real, plus, minus = coh[i, 0], coh[i, 1], coh[i, 2]
            add(t, 0, real * v[u][2])
            add(t, 1, plus * v[u][1])
            add(t, 2, minus * v[u][0])
            add(u, 0, real * v[t][2])
            add(u, 1, minus * v[t][1], True)
            add(u, 2, plus * v[t][0], True)

        for first in range(0, DATES, 4):
            for second in range(first, DATES, 4):
                dates = sorted(set(range(first, first + 4)) | set(range(second, second + 4)))
                v = {t: (vec[0, t], vec[1, t], vec[2, t]) for t in dates}
                for t in range(first, first + 4):
                    for u in range(second, second + 4):
                        if t < u:
                            pair(t, u, v)
        for t in range(DATES):
            own = weight[t]
            new_real[t] = (sums[t][0] - sums[t][1]) + own * vec[0, t]
            new_imag[t] = (sums[t][0] + sums[t][2]) + own * vec[1, t]
        for t in range(DATES):
            real, imag = new_real[t] * scale, new_imag[t] * scale
            vec[0, t] = real
            vec[1, t] = imag
            vec[2, t] = real + imag
        return carry

    lax.fori_loop(0, ITERS, iterate, 0)
    scale = inverse_norm(vec)
    for t in range(DATES):
        for part in range(2):
            vec[part, t] = vec[part, t] * scale


def whole(*shape):
    return pl.BlockSpec(shape, lambda i: (0,) * len(shape))


def common_scratch(small_rows):
    return [
        pltpu.VMEM((DATES, TILE_LANES, 128), jnp.float32),
        pltpu.VMEM((FIELDS * 16, 256), jnp.bfloat16),
        pltpu.VMEM((small_rows, DATES, 128), jnp.float32),
        pltpu.VMEM((SIDE, 128), jnp.float32),
    ]


SOLVE_SCRATCH = [
    pltpu.VMEM((len(PAIRS), 3, 8, 128), jnp.float32),
    pltpu.VMEM((3, DATES, 8, 128), jnp.float32),
    pltpu.VMEM((DATES, 8, 128), jnp.float32),
]
LINKED = (2, DATES, BLOCKS, OUT_COLS)
PARTIAL = (FIELDS * 8, 128)


def link_first(message, tables):
    return pl.pallas_call(
        first_kernel,
        grid=(FIRST,),
        in_specs=[
            pl.BlockSpec((DATES, TILE_LANES, 128), lambda i: (0, i, 0)),
            pl.BlockSpec((DATES, 64, 128), lambda i: (0, HALO1 // 64, 0)),
            pl.BlockSpec((1, 256, 256), lambda i: (i, 0, 0)),
        ],
        out_specs=[whole(*PARTIAL), whole(*LINKED)],
        out_shape=[
            jax.ShapeDtypeStruct(PARTIAL, jnp.float32),
            jax.ShapeDtypeStruct(LINKED, jnp.float32),
        ],
        scratch_shapes=common_scratch(10)
        + [
            pltpu.VMEM((FIRST, FIELDS * 16, 256), jnp.float32),
            pltpu.VMEM((FIRST, SIDE, 256), jnp.float32),
        ]
        + SOLVE_SCRATCH
        + [pltpu.VMEM((2, DATES, 2, BLOCKS, 128), jnp.float32)],
        compiler_params=pltpu.CompilerParams(vmem_limit_bytes=40 * 1024 * 1024),
        cost_estimate=pl.CostEstimate(flops=10**9, bytes_accessed=10**7, transcendentals=0),
        name="link_first",
    )(message, message, tables)


def link_last(message, left, right, tables, pool, partial, done):
    return pl.pallas_call(
        last_kernel,
        grid=(1,),
        in_specs=[
            whole(DATES, ROWS2, 128),
            whole(DATES, 8, 128),
            whole(DATES, 8, 128),
            pl.BlockSpec((1, 256, 128), lambda i: (FIRST, 0, 0)),
            whole(16, 128),
            pl.BlockSpec(memory_space=pl.ANY),
            pl.BlockSpec(memory_space=pl.ANY),
        ],
        out_specs=whole(*LINKED),
        out_shape=jax.ShapeDtypeStruct(LINKED, jnp.float32),
        scratch_shapes=common_scratch(14)
        + [
            pltpu.VMEM((FIELDS * 16, 128), jnp.float32),
            pltpu.VMEM((SIDE, 128), jnp.float32),
            pltpu.VMEM((2 * SIDE, 128), jnp.float32),
            pltpu.VMEM((SIDE // 32, 8, 128), jnp.float32),
        ]
        + SOLVE_SCRATCH
        + [
            pltpu.VMEM((2, DATES, 1, BLOCKS, 128), jnp.float32),
            pltpu.VMEM(PARTIAL, jnp.float32),
            pltpu.VMEM(LINKED, jnp.float32),
            pltpu.SemaphoreType.DMA((2,)),
        ],
        compiler_params=pltpu.CompilerParams(vmem_limit_bytes=24 * 1024 * 1024),
        cost_estimate=pl.CostEstimate(flops=10**8, bytes_accessed=10**7, transcendentals=0),
        name="link_last",
    )(message, left, right, tables, pool, partial, done)


def local(slc, valid_rows):
    size = lax.axis_size("col")
    up = [(i, i + 1) for i in range(size - 1)]
    down = [(i + 1, i) for i in range(size - 1)]
    valid = valid_rows.T
    message1, message2 = pack(slc, valid)
    received1 = lax.all_to_all(message1, "row", 0, 0, tiled=True)
    received1, message2 = lax.optimization_barrier((received1, message2))
    received2 = lax.all_to_all(message2, "row", 0, 0, tiled=True)
    own = received1[:, OWN_TILE : OWN_TILE + 8]
    left = lax.ppermute(own, "col", up)
    right = lax.ppermute(own, "col", down)
    tables, pool = column_tables()
    tables = jnp.asarray(tables, jnp.bfloat16)
    partial, done = link_first(received1, tables)
    return link_last(received2, left, right, tables, jnp.asarray(pool), partial, done)


def solution(mesh):
    return jax.shard_map(
        local,
        mesh=mesh,
        in_specs=(P(None, "row", None, "col"), P()),
        out_specs=P(None, None, "row", "col"),
        check_vma=False,
    )
```

```python
import functools

import jax
import jax.numpy as jnp
import numpy as np
from jax import lax
from jax.experimental import pallas as pl
from jax.experimental.pallas import tpu as pltpu
from jax.sharding import PartitionSpec as P

ITERS = 10
FLOOR = 20.0
DATES = 16
TILES = 16
COLS = 768
LANE_TILES = 6
FIRST = 5
OUT_COLS = 256
BLOCKS = 16
TILE_ROWS = 6 * BLOCKS
TILE_LANES = 192
ROWS1 = 1024
HALO1 = FIRST * TILE_LANES
OWN_TILE = 1008
OWN_ROW = 1010
ROWS2 = 208
HALO2 = TILE_LANES
WINDOW = TILE_ROWS + 5
PIECES = 8
PIECE_ROWS = 192
GRANT = 60 * 1024 * 1024


def pair_groups():
    groups = []
    for i in range(0, DATES, 2):
        groups.append(([i], [i + 1]))
        rest = list(range(i + 2, DATES))
        for j in range(0, len(rest), 4):
            groups.append(([i, i + 1], rest[j : j + 4]))
    return groups


GROUPS = pair_groups()
PAIRS = [(t, u) for ts, us in GROUPS for t in ts for u in us]
PAIR_AT = {pair: i for i, pair in enumerate(PAIRS)}
FIELDS = DATES + 2 * len(PAIRS)
CHUNK = 512
SIDE = 512
FEEDS = ((0, 2), (0,), (0,), (0, 1), (1, 2), (2,))


def lane_columns():
    lane = np.arange(128)
    group_a = np.where(lane < 32, 128 + lane, lane)
    group_b = np.where((lane >= 32) & (lane < 96), 128 + lane, 128 + (lane + 64) % 128)
    own = np.where(lane < 32, lane, 128 + lane)
    other = (lane + 64) % 128
    far = np.where(other < 32, other, 128 + other)
    group_c = np.where((lane < 32) | (lane >= 96), own, far)
    return group_a, group_b, group_c


def column_tables():
    groups = lane_columns()
    tables = np.zeros((LANE_TILES, 256, 256), np.float32)
    for lt in range(LANE_TILES):
        column = (lt * 128 + np.arange(128) + 64) % COLS
        for place, group in enumerate(FEEDS[lt]):
            target = 3 * groups[group][None, :]
            inside = (column[:, None] >= target - 1) & (column[:, None] <= target + 3)
            for copy in range(2):
                tables[lt, copy * 128 : copy * 128 + 128, place * 128 : place * 128 + 128] = inside
    row = np.arange(128)
    pool = np.zeros((2, 8, 128), np.float32)
    for half in range(2):
        for s in range(8):
            block = 2 * s + half
            pool[half, s] = (row >= 6 * block) & (row <= 6 * block + 10)
    return tables, pool.reshape(16, 128)


def pack_kernel(valid_ref, slc, out1, out2, taken, rows_ref, stage1, stage2, in_sems, out_sems):
    me = lax.axis_index("row")
    low, high = valid_ref[0, me], valid_ref[1, me]
    lane = lax.broadcasted_iota(jnp.int32, (8, 128), 1)
    row = lax.broadcasted_iota(jnp.int32, (8, 128), 0)
    pick = jnp.where(((row == 0) & (lane == 64)) | ((row == 1) & (lane == 63)), 1.0, 0.0)
    count = TILE_ROWS + 16

    def piece(index):
        return pltpu.make_async_copy(
            slc.at[:, 0, pl.ds(index * PIECE_ROWS, PIECE_ROWS), :],
            taken.at[:, pl.ds(index * PIECE_ROWS + 8, PIECE_ROWS), :],
            in_sems.at[index],
        )

    def sends(tile):
        return (
            pltpu.make_async_copy(stage1.at[tile], out1.at[tile], out_sems.at[0, tile]),
            pltpu.make_async_copy(stage2.at[tile], out2.at[tile], out_sems.at[1, tile]),
        )

    def one_tile(tile):
        start = pl.multiple_of(tile * TILE_ROWS, 8)
        at_row = lax.broadcasted_iota(jnp.int32, (count, 128), 0) + (start - 8)
        keep = (at_row >= low) & (at_row < high)
        left = lax.broadcasted_iota(jnp.int32, (count, 128), 1) < 64
        for part in range(2):
            turned = []
            for lt in range(LANE_TILES):
                value = taken[part, pl.ds(start, count), lt * 128 : lt * 128 + 128]
                turned.append(pltpu.roll(jnp.where(keep, value, 0.0), 64, 1))
            for lt in range(LANE_TILES):
                rows_ref[part, lt, 0:count, :] = jnp.where(
                    left, turned[lt], turned[(lt + 1) % LANE_TILES]
                )
        base = 5
        stage1[tile, pl.ds(ROWS1 - 16, 16), :] = jnp.zeros((16, 128), jnp.float32)
        stage2[tile, pl.ds(ROWS2 - 16, 16), :] = jnp.zeros((16, 128), jnp.float32)
        for part in range(2):
            columns = lax.dot_general(
                pick, rows_ref[part, LANE_TILES - 1, pl.ds(base, 128), :],
                (((1,), (1,)), ((), ())),
                precision=lax.Precision.HIGHEST, preferred_element_type=jnp.float32,
            )
            columns = jnp.where(lane < WINDOW + 1, columns, 0.0)
            for side in range(2):
                stage1[tile, pl.ds(OWN_ROW + 2 * side + part, 1), :] = columns[side : side + 1]
        for lt in range(LANE_TILES):
            out = stage1 if lt < FIRST else stage2
            top = lt * TILE_LANES if lt < FIRST else 0
            below = HALO1 + lt * 10 if lt < FIRST else HALO2
            for part in range(2):
                for phase in range(6):
                    for half in range(2):
                        at = top + part * 96 + phase * 16 + half * 8
                        out[tile, pl.ds(at, 8), :] = rows_ref[
                            part, lt, pl.ds(base + 6 * half + phase, 8, stride=12), :
                        ]
                out[tile, pl.ds(below + 5 * part, 5), :] = rows_ref[
                    part, lt, pl.ds(base + TILE_ROWS, 5), :
                ]
        for send in sends(tile):
            send.start()

    for index in range(PIECES):
        piece(index).start()
    rows_ref[:, :, pl.ds(count, 24), :] = jnp.zeros((2, LANE_TILES, 24, 128), jnp.float32)
    piece(0).wait()

    def step(index, carry):
        one_tile(2 * index)

        @pl.when(index < PIECES - 1)
        def _():
            piece(index + 1).wait()

        one_tile(2 * index + 1)
        return carry

    lax.fori_loop(0, PIECES, step, 0)

    def finish(tile, carry):
        for send in sends(tile):
            send.wait()
        return carry

    lax.fori_loop(0, TILES, finish, 0)


def pack(slc, valid):
    return pl.pallas_call(
        pack_kernel,
        in_specs=[
            pl.BlockSpec(memory_space=pltpu.SMEM),
            pl.BlockSpec(memory_space=pl.ANY),
        ],
        out_specs=[pl.BlockSpec(memory_space=pl.ANY)] * 2,
        out_shape=[
            jax.ShapeDtypeStruct((TILES, ROWS1, 128), jnp.float32),
            jax.ShapeDtypeStruct((TILES, ROWS2, 128), jnp.float32),
        ],
        scratch_shapes=[
            pltpu.VMEM((2, 1536 + 16, COLS), jnp.float32),
            pltpu.VMEM((2, LANE_TILES, TILE_ROWS + 40, 128), jnp.float32),
            pltpu.VMEM((TILES, ROWS1, 128), jnp.float32),
            pltpu.VMEM((TILES, ROWS2, 128), jnp.float32),
            pltpu.SemaphoreType.DMA((PIECES,)),
            pltpu.SemaphoreType.DMA((2, TILES)),
        ],
        compiler_params=pltpu.CompilerParams(vmem_limit_bytes=GRANT),
        cost_estimate=pl.CostEstimate(flops=10**6, bytes_accessed=2 * 10**7, transcendentals=0),
        name="pack",
    )(valid, slc)


def split(x):
    high = x.astype(jnp.bfloat16)
    return high, (x - high.astype(jnp.float32)).astype(jnp.bfloat16)


def field_of(t, u):
    return t if t == u else DATES + 2 * PAIR_AT[t, u]


def cross_products(data, t_part, u_tile, lanes, rows):
    real = imag = None
    for re_row, im_row in rows:
        a_t = data[re_row, pl.ds(t_part, 1), lanes]
        b_t = data[im_row, pl.ds(t_part, 1), lanes]
        a_u = data[re_row, pl.ds(u_tile * 8, 8), lanes]
        b_u = data[im_row, pl.ds(u_tile * 8, 8), lanes]
        re = a_t * a_u + b_t * b_u
        im = b_t * a_u - a_t * b_u
        real = re if real is None else real + re
        imag = im if imag is None else imag + im
    return real, imag


def dot(a, b):
    return jnp.dot(a, b, preferred_element_type=jnp.float32)


def main_products(msg, sums, lhs, pooled):
    last = lax.broadcasted_iota(jnp.int32, (8, 128), 0) == 7
    state = {"fields": 0, "chunks": 0}

    def load(kind, date, phase, half):
        source = msg if kind in "ab" else sums
        base = 0 if kind in "as" else 96
        return source[date, pl.ds(base + phase * 16 + half * 8, 8), :]

    def emit(field, first, whole):
        out0 = whole[0] + first[1]
        rolled = jnp.where(last, 0.0, pltpu.roll(first[0], 7, 0))
        out1 = whole[1] + rolled
        high, low = split(jnp.concatenate([out0, out1], axis=0))
        lhs[pl.ds(field * 16, 16), 0:128] = high
        lhs[pl.ds(field * 16, 16), 128:256] = low
        state["fields"] += 1

    def drain():
        while (state["chunks"] + 1) * CHUNK <= state["fields"] * 16:
            pooled(state["chunks"])
            state["chunks"] += 1

    for t in range(DATES):
        first, whole = [], []
        for half in range(2):
            total = None
            for phase in range(6):
                a, b = load("a", t, phase, half), load("b", t, phase, half)
                term = a * a + b * b
                if phase == 5:
                    first.append(total)
                total = term if total is None else total + term
            whole.append(total)
        emit(t, first, whole)

    for ts, us in GROUPS:
        pairs = [(t, u) for t in ts for u in us]
        first = {pair: ([], []) for pair in pairs}
        whole = {pair: ([], []) for pair in pairs}
        for half in range(2):
            acc = {}
            for phase in range(6):
                s_t = {t: load("s", t, phase, half) for t in ts}
                a_t = {t: load("a", t, phase, half) for t in ts}
                b_t = {t: load("b", t, phase, half) for t in ts}
                a_u = {u: load("a", u, phase, half) for u in us}
                s_u = {u: load("s", u, phase, half) for u in us}
                d_u = {u: load("d", u, phase, half) for u in us}
                for t, u in pairs:
                    p = a_u[u] * s_t[t]
                    q = d_u[u] * b_t[t]
                    r = s_u[u] * a_t[t]
                    if phase == 0:
                        acc[t, u] = (p, q, r)
                    elif phase < 5:
                        p0, q0, r0 = acc[t, u]
                        acc[t, u] = (p0 + p, q0 + q, r0 + r)
                    else:
                        p0, q0, r0 = acc[t, u]
                        re5, im5 = p0 - q0, p0 - r0
                        first[t, u][0].append(re5)
                        first[t, u][1].append(im5)
                        whole[t, u][0].append(re5 + (p - q))
                        whole[t, u][1].append(im5 + (p - r))
        for pair in pairs:
            for part in range(2):
                emit(field_of(*pair) + part, first[pair][part], whole[pair][part])
        drain()


def dot(a, b):
    return jnp.dot(a, b, preferred_element_type=jnp.float32)


def side_products(small, t, rows, put):
    for u_tile in range(2):
        if u_tile < t // 8:
            values = (jnp.zeros((8, 128), jnp.float32),) * 2
        else:
            values = cross_products(small, t, u_tile, pl.ds(0, 128), rows)
        for part in range(2):
            put(part * 256 + t * 16 + u_tile * 8, values[part])


def fill_sums(msg, sums):
    def fill(date, carry):
        a = msg[date, pl.ds(0, 96), :]
        b = msg[date, pl.ds(96, 96), :]
        sums[date, pl.ds(0, 96), :] = a + b
        sums[date, pl.ds(96, 96), :] = a - b
        return carry

    lax.fori_loop(0, DATES, fill, 0, unroll=2)


def halo_products(small, side_lhs):
    def put(at, value):
        side_lhs[pl.ds(at, 8), :] = value

    for t in range(DATES):
        side_products(small, t, [(p, 5 + p) for p in range(5)], put)


def pool_side(side_lhs, table):
    high, low = split(side_lhs[...])
    return dot(jnp.concatenate([high, low], axis=1), table)


def chunk_rows(chunk):
    return pl.ds(chunk * CHUNK, CHUNK)


def first_kernel(
    msg, below_msg, table, part_out, out, sums, lhs, small, side_lhs, res, halo, coh, vec, weight,
    rows, weights,
):
    step = pl.program_id(0)
    weights[...] = table[0].astype(jnp.bfloat16)
    fill_sums(msg, sums)
    for date in range(DATES):
        for row in range(10):
            small[row, date : date + 1, :] = below_msg[date, pl.ds(step * 10 + row, 1), :]
    halo_products(small, side_lhs)
    halo[step] = pool_side(side_lhs, weights[...])

    def pooled(chunk):
        res[step, chunk_rows(chunk), :] = dot(lhs[chunk_rows(chunk), :], weights[...])

    main_products(msg, sums, lhs, pooled)

    @pl.when(step == FIRST - 1)
    def _():
        lane = lax.broadcasted_iota(jnp.int32, (8, 128), 1)
        last = lax.broadcasted_iota(jnp.int32, (8, 128), 0) == 7

        def total(ref, group, at, count):
            value = None
            for lt in range(FIRST):
                if group in FEEDS[lt]:
                    place = FEEDS[lt].index(group) * 128
                    own = ref[lt, pl.ds(at, count), place : place + 128]
                    value = own if value is None else value + own
            return value

        def below(group, t, u, part):
            return total(halo, group, part * 256 + t * 16 + u, 1)

        def paired(group, even, t, u, part):
            at = (field_of(t, u) + part) * 16
            value = jnp.where(even, total(res, group, at, 8), total(res, group, at + 8, 8))
            return value + jnp.where(last & ~even, below(group, t, u, part), 0.0)

        even = (lane < 32) | (lane >= 96)
        for t in range(DATES):
            for u in range(t, DATES):
                for part in range(1 if t == u else 2):
                    at = (field_of(t, u) + part) * 8
                    part_out[pl.ds(at, 8), :] = paired(2, even, t, u, part)

        for half in range(2):

            def cov(t, u, part):
                value = total(res, 0, (field_of(t, u) + part) * 16 + half * 8, 8)
                if half == 1:
                    value = value + jnp.where(last, below(0, t, u, part), 0.0)
                return value

            solve(cov, coh, vec, weight)
            for date in range(DATES):
                for part in range(2):
                    rows[part, date, 0, pl.ds(half, 8, stride=2), :] = vec[part, date]

        even_b = (lane >= 32) & (lane < 96)
        solve(functools.partial(paired, 1, even_b), coh, vec, weight)
        for date in range(DATES):
            for part in range(2):
                value = vec[part, date]
                rows[part, date, 1, pl.ds(0, 8, stride=2), :] = value
                rows[part, date, 1, pl.ds(1, 8, stride=2), :] = pltpu.roll(value, 64, 1)
        out[:, :, :, 0:128] = rows[:, :, 0]
        left = lax.broadcasted_iota(jnp.int32, (2, DATES, BLOCKS, 128), 3) < 32
        out[:, :, :, 128:256] = jnp.where(left, rows[:, :, 0], rows[:, :, 1])


def last_kernel(
    msg, left, right, table, pool, partial_hbm, done_hbm, out, sums, lhs, small, side_lhs, res, halo,
    pairs, edge, coh, vec, weight, rows, weights, partial, done, sems,
):
    copies = [
        pltpu.make_async_copy(partial_hbm, partial, sems.at[0]),
        pltpu.make_async_copy(done_hbm, done, sems.at[1]),
    ]
    for copy in copies:
        copy.start()
    fill_sums(msg, sums)
    for date in range(DATES):
        for row in range(10):
            small[row, date : date + 1, :] = msg[date, HALO2 + row : HALO2 + row + 1, :]
        for part in range(2):
            own = OWN_ROW - OWN_TILE + part
            small[10 + part, date : date + 1, :] = left[date, own + 2 : own + 3, :]
            small[12 + part, date : date + 1, :] = right[date, own : own + 1, :]
    halo_products(small, side_lhs)
    weights[...] = table[0].astype(jnp.bfloat16)
    halo[...] = pool_side(side_lhs, weights[...])
    for side in range(2):
        row = 10 + 2 * side

        def put(at, value):
            pairs[pl.ds(2 * at + 1 - side, 8, stride=2), :] = value

        for t in range(DATES):
            side_products(small, t, [(row, row + 1)], put)
    dims = (((1,), (1,)), ((), ()))
    high, low = split(pairs[...])
    pool2 = pool[...].astype(jnp.bfloat16)
    sides = lax.dot_general(
        pool2, high, dims, preferred_element_type=jnp.float32
    ) + lax.dot_general(pool2, low, dims, preferred_element_type=jnp.float32)
    lower = lax.broadcasted_iota(jnp.int32, (8, 128), 1) < 64
    for group in range(SIDE // 64):
        tile = slice(group * 128, group * 128 + 128)
        even_rows, odd_rows = sides[0:8, tile], sides[8:16, tile]
        edge[2 * group] = jnp.where(lower, even_rows, pltpu.roll(odd_rows, 64, 1))
        edge[2 * group + 1] = jnp.where(lower, pltpu.roll(even_rows, 64, 1), odd_rows)

    def pooled(chunk):
        res[chunk_rows(chunk), :] = dot(lhs[chunk_rows(chunk), :], weights[...])

    main_products(msg, sums, lhs, pooled)

    lane = lax.broadcasted_iota(jnp.int32, (8, 128), 1)
    last = lax.broadcasted_iota(jnp.int32, (8, 128), 0) == 7
    even = (lane < 32) | (lane >= 96)
    beside = (lane == 0) | (lane == 127) | (lane == 63) | (lane == 64)
    for copy in copies:
        copy.wait()

    def cov(t, u, part):
        field = field_of(t, u) + part
        at = field * 16
        value = jnp.where(even, res[pl.ds(at, 8), :], res[pl.ds(at + 8, 8), :])
        index = part * 256 + t * 16 + u
        value = value + jnp.where(last & ~even, halo[pl.ds(index, 1), :], 0.0)
        turned = pltpu.roll(edge[index // 32], (127 - 2 * (index % 32)) % 128, 1)
        return value + partial[pl.ds(field * 8, 8), :] + jnp.where(beside, turned, 0.0)

    solve(cov, coh, vec, weight)
    for date in range(DATES):
        for part in range(2):
            value = vec[part, date]
            rows[part, date, 0, pl.ds(0, 8, stride=2), :] = value
            rows[part, date, 0, pl.ds(1, 8, stride=2), :] = pltpu.roll(value, 64, 1)
    place = lax.broadcasted_iota(jnp.int32, (2, DATES, BLOCKS, 128), 3)
    out[:, :, :, 0:128] = jnp.where(place < 32, rows[:, :, 0], done[:, :, :, 0:128])
    out[:, :, :, 128:256] = jnp.where(place >= 96, rows[:, :, 0], done[:, :, :, 128:256])


def inverse_norm(vec):
    terms = [vec[part, t] * vec[part, t] for t in range(DATES) for part in range(2)]
    while len(terms) > 1:
        terms = [terms[i] + terms[i + 1] for i in range(0, len(terms), 2)]
    return lax.rsqrt(terms[0])


def solve(cov, coh, vec, weight):
    inv = []
    for t in range(DATES):
        diag = cov(t, t, 0)
        root = lax.rsqrt(jnp.maximum(diag, FLOOR))
        inv.append(root)
        weight[t] = diag * (root * root) + 1.0
    for i, (t, u) in enumerate(PAIRS):
        factor = inv[t] * inv[u]
        real = cov(t, u, 0) * factor
        imag = cov(t, u, 1) * factor
        coh[i, 0] = real
        coh[i, 1] = real + imag
        coh[i, 2] = imag - real
    for t in range(DATES):
        vec[0, t] = jnp.full((8, 128), 0.25, jnp.float32)
        vec[1, t] = jnp.zeros((8, 128), jnp.float32)
        vec[2, t] = jnp.full((8, 128), 0.25, jnp.float32)

    def iterate(_, carry):
        scale = inverse_norm(vec)
        new_real, new_imag = [None] * DATES, [None] * DATES
        sums = [[None, None, None] for _ in range(DATES)]

        def add(t, which, value, minus=False):
            if sums[t][which] is None:
                sums[t][which] = -value if minus else value
            elif minus:
                sums[t][which] = sums[t][which] - value
            else:
                sums[t][which] = sums[t][which] + value

        def pair(t, u, v):
            i = PAIR_AT[t, u]
            real, plus, minus = coh[i, 0], coh[i, 1], coh[i, 2]
            add(t, 0, real * v[u][2])
            add(t, 1, plus * v[u][1])
            add(t, 2, minus * v[u][0])
            add(u, 0, real * v[t][2])
            add(u, 1, minus * v[t][1], True)
            add(u, 2, plus * v[t][0], True)

        for first in range(0, DATES, 4):
            for second in range(first, DATES, 4):
                dates = sorted(set(range(first, first + 4)) | set(range(second, second + 4)))
                v = {t: (vec[0, t], vec[1, t], vec[2, t]) for t in dates}
                for t in range(first, first + 4):
                    for u in range(second, second + 4):
                        if t < u:
                            pair(t, u, v)
        for t in range(DATES):
            own = weight[t]
            new_real[t] = (sums[t][0] - sums[t][1]) + own * vec[0, t]
            new_imag[t] = (sums[t][0] + sums[t][2]) + own * vec[1, t]
        for t in range(DATES):
            real, imag = new_real[t] * scale, new_imag[t] * scale
            vec[0, t] = real
            vec[1, t] = imag
            vec[2, t] = real + imag
        return carry

    lax.fori_loop(0, ITERS, iterate, 0)
    scale = inverse_norm(vec)
    for t in range(DATES):
        for part in range(2):
            vec[part, t] = vec[part, t] * scale


def whole(*shape):
    return pl.BlockSpec(shape, lambda i: (0,) * len(shape))


def common_scratch(small_rows):
    return [
        pltpu.VMEM((DATES, TILE_LANES, 128), jnp.float32),
        pltpu.VMEM((FIELDS * 16, 256), jnp.bfloat16),
        pltpu.VMEM((small_rows, DATES, 128), jnp.float32),
        pltpu.VMEM((SIDE, 128), jnp.float32),
    ]


SOLVE_SCRATCH = [
    pltpu.VMEM((len(PAIRS), 3, 8, 128), jnp.float32),
    pltpu.VMEM((3, DATES, 8, 128), jnp.float32),
    pltpu.VMEM((DATES, 8, 128), jnp.float32),
]
LINKED = (2, DATES, BLOCKS, OUT_COLS)
PARTIAL = (FIELDS * 8, 128)


def cut_kernel(in_ref, out_ref):
    out_ref[...] = in_ref[...]


def cut_columns(message):
    return pl.pallas_call(
        cut_kernel,
        grid=(1,),
        in_specs=[pl.BlockSpec((DATES, 8, 128), lambda i: (0, OWN_TILE // 8, 0))],
        out_specs=whole(DATES, 8, 128),
        out_shape=jax.ShapeDtypeStruct((DATES, 8, 128), jnp.float32),
        compiler_params=pltpu.CompilerParams(vmem_limit_bytes=GRANT),
        name="cut_columns",
    )(message)


def link_first(message, tables):
    return pl.pallas_call(
        first_kernel,
        grid=(FIRST,),
        in_specs=[
            pl.BlockSpec((DATES, TILE_LANES, 128), lambda i: (0, i, 0)),
            pl.BlockSpec((DATES, 64, 128), lambda i: (0, HALO1 // 64, 0)),
            pl.BlockSpec((1, 256, 256), lambda i: (i, 0, 0)),
        ],
        out_specs=[whole(*PARTIAL), whole(*LINKED)],
        out_shape=[
            jax.ShapeDtypeStruct(PARTIAL, jnp.float32),
            jax.ShapeDtypeStruct(LINKED, jnp.float32),
        ],
        scratch_shapes=common_scratch(10)
        + [
            pltpu.VMEM((FIRST, FIELDS * 16, 256), jnp.float32),
            pltpu.VMEM((FIRST, SIDE, 256), jnp.float32),
        ]
        + SOLVE_SCRATCH
        + [pltpu.VMEM((2, DATES, 2, BLOCKS, 128), jnp.float32), pltpu.VMEM((256, 256), jnp.bfloat16)],
        compiler_params=pltpu.CompilerParams(vmem_limit_bytes=GRANT),
        cost_estimate=pl.CostEstimate(flops=10**9, bytes_accessed=10**7, transcendentals=0),
        name="link_first",
    )(message, message, tables)


def link_last(message, left, right, tables, pool, partial, done):
    return pl.pallas_call(
        last_kernel,
        grid=(1,),
        in_specs=[
            whole(DATES, ROWS2, 128),
            whole(DATES, 8, 128),
            whole(DATES, 8, 128),
            pl.BlockSpec((1, 256, 128), lambda i: (FIRST, 0, 0)),
            whole(16, 128),
            pl.BlockSpec(memory_space=pl.ANY),
            pl.BlockSpec(memory_space=pl.ANY),
        ],
        out_specs=whole(*LINKED),
        out_shape=jax.ShapeDtypeStruct(LINKED, jnp.float32),
        scratch_shapes=common_scratch(14)
        + [
            pltpu.VMEM((FIELDS * 16, 128), jnp.float32),
            pltpu.VMEM((SIDE, 128), jnp.float32),
            pltpu.VMEM((2 * SIDE, 128), jnp.float32),
            pltpu.VMEM((SIDE // 32, 8, 128), jnp.float32),
        ]
        + SOLVE_SCRATCH
        + [
            pltpu.VMEM((2, DATES, 1, BLOCKS, 128), jnp.float32),
            pltpu.VMEM((256, 128), jnp.bfloat16),
            pltpu.VMEM(PARTIAL, jnp.float32),
            pltpu.VMEM(LINKED, jnp.float32),
            pltpu.SemaphoreType.DMA((2,)),
        ],
        compiler_params=pltpu.CompilerParams(vmem_limit_bytes=GRANT),
        cost_estimate=pl.CostEstimate(flops=10**8, bytes_accessed=10**7, transcendentals=0),
        name="link_last",
    )(message, left, right, tables, pool, partial, done)


def local(slc, valid_rows):
    size = lax.axis_size("col")
    up = [(i, i + 1) for i in range(size - 1)]
    down = [(i + 1, i) for i in range(size - 1)]
    valid = valid_rows.T
    message1, message2 = pack(slc, valid)
    received1 = lax.all_to_all(message1, "row", 0, 0, tiled=True)
    received1, message2 = lax.optimization_barrier((received1, message2))
    received2 = lax.all_to_all(message2, "row", 0, 0, tiled=True)
    own = cut_columns(received1)
    left = lax.ppermute(own, "col", up)
    right = lax.ppermute(own, "col", down)
    tables, pool = column_tables()
    tables = jnp.asarray(tables)
    partial, done = link_first(received1, tables)
    return link_last(received2, left, right, tables, jnp.asarray(pool), partial, done)


def solution(mesh):
    return jax.shard_map(
        local,
        mesh=mesh,
        in_specs=(P(None, "row", None, "col"), P()),
        out_specs=P(None, None, "row", "col"),
        check_vma=False,
    )
```

```python
import functools

import jax
import jax.numpy as jnp
import numpy as np
from jax import lax
from jax.experimental import pallas as pl
from jax.experimental.pallas import tpu as pltpu
from jax.sharding import PartitionSpec as P

ITERS = 10
FLOOR = 20.0
DATES = 16
TILES = 16
COLS = 768
LANE_TILES = 6
FIRST = 5
OUT_COLS = 256
BLOCKS = 16
TILE_ROWS = 6 * BLOCKS
TILE_LANES = 192
ROWS1 = 1024
HALO1 = FIRST * TILE_LANES
OWN_TILE = 1008
OWN_ROW = 1010
ROWS2 = 208
HALO2 = TILE_LANES
WINDOW = TILE_ROWS + 5
PIECES = 8
PIECE_ROWS = 192
GRANT = 60 * 1024 * 1024


def pair_groups():
    groups = []
    for i in range(0, DATES, 2):
        groups.append(([i], [i + 1]))
        rest = list(range(i + 2, DATES))
        for j in range(0, len(rest), 4):
            groups.append(([i, i + 1], rest[j : j + 4]))
    return groups


GROUPS = pair_groups()
PAIRS = [(t, u) for ts, us in GROUPS for t in ts for u in us]
PAIR_AT = {pair: i for i, pair in enumerate(PAIRS)}
FIELDS = DATES + 2 * len(PAIRS)
CHUNK = 512
SIDE = 512
FEEDS = ((0, 2), (0,), (0,), (0, 1), (1, 2), (2,))


def lane_columns():
    lane = np.arange(128)
    group_a = np.where(lane < 32, 128 + lane, lane)
    group_b = np.where((lane >= 32) & (lane < 96), 128 + lane, 128 + (lane + 64) % 128)
    own = np.where(lane < 32, lane, 128 + lane)
    other = (lane + 64) % 128
    far = np.where(other < 32, other, 128 + other)
    group_c = np.where((lane < 32) | (lane >= 96), own, far)
    return group_a, group_b, group_c


def column_tables():
    groups = lane_columns()
    tables = np.zeros((LANE_TILES, 256, 256), np.float32)
    for lt in range(LANE_TILES):
        column = (lt * 128 + np.arange(128) + 64) % COLS
        for place, group in enumerate(FEEDS[lt]):
            target = 3 * groups[group][None, :]
            inside = (column[:, None] >= target - 1) & (column[:, None] <= target + 3)
            for copy in range(2):
                tables[lt, copy * 128 : copy * 128 + 128, place * 128 : place * 128 + 128] = inside
    row = np.arange(128)
    pool = np.zeros((2, 8, 128), np.float32)
    for half in range(2):
        for s in range(8):
            block = 2 * s + half
            pool[half, s] = (row >= 6 * block) & (row <= 6 * block + 10)
    return tables, pool.reshape(16, 128)


def pack_kernel(valid_ref, slc, out1, out2, taken, rows_ref, stage1, stage2, in_sems, out_sems):
    me = lax.axis_index("row")
    low, high = valid_ref[0, me], valid_ref[1, me]
    lane = lax.broadcasted_iota(jnp.int32, (8, 128), 1)
    row = lax.broadcasted_iota(jnp.int32, (8, 128), 0)
    pick = jnp.where(((row == 0) & (lane == 64)) | ((row == 1) & (lane == 63)), 1.0, 0.0)
    count = TILE_ROWS + 16

    def piece(index):
        return pltpu.make_async_copy(
            slc.at[:, 0, pl.ds(index * PIECE_ROWS, PIECE_ROWS), :],
            taken.at[:, pl.ds(index * PIECE_ROWS + 8, PIECE_ROWS), :],
            in_sems.at[index],
        )

    def sends(tile):
        return (
            pltpu.make_async_copy(stage1.at[tile], out1.at[tile], out_sems.at[0, tile]),
            pltpu.make_async_copy(stage2.at[tile], out2.at[tile], out_sems.at[1, tile]),
        )

    def mask_rows(tile, slot):
        start = pl.multiple_of(tile * TILE_ROWS, 8)
        at_row = lax.broadcasted_iota(jnp.int32, (count, 128), 0) + (start - 8)
        keep = (at_row >= low) & (at_row < high)
        left = lax.broadcasted_iota(jnp.int32, (count, 128), 1) < 64
        for part in range(2):
            turned = []
            for lt in range(LANE_TILES):
                value = taken[part, pl.ds(start, count), lt * 128 : lt * 128 + 128]
                turned.append(pltpu.roll(jnp.where(keep, value, 0.0), 64, 1))
            for lt in range(LANE_TILES):
                rows_ref[slot, part, lt, 0:count, :] = jnp.where(
                    left, turned[lt], turned[(lt + 1) % LANE_TILES]
                )

    def own_columns(tiles):
        blocks = [
            rows_ref[slot, part, LANE_TILES - 1, pl.ds(5, 128), :]
            for slot in range(2)
            for part in range(2)
        ]
        rest = jnp.concatenate(blocks, axis=0)
        columns = None
        for _ in range(3):
            piece_of = rest.astype(jnp.bfloat16)
            rest = rest - piece_of.astype(jnp.float32)
            term = lax.dot_general(
                pick.astype(jnp.bfloat16), piece_of, (((1,), (1,)), ((), ())),
                preferred_element_type=jnp.float32,
            )
            columns = term if columns is None else columns + term
        for slot, tile in enumerate(tiles):
            for part in range(2):
                at = (2 * slot + part) * 128
                value = jnp.where(lane < WINDOW + 1, columns[:, at : at + 128], 0.0)
                for side in range(2):
                    row_at = pl.ds(OWN_ROW + 2 * side + part, 1)
                    stage1[tile, row_at, :] = value[side : side + 1]

    def spread(tile, slot):
        base = 5
        for lt in range(LANE_TILES):
            out = stage1 if lt < FIRST else stage2
            top = lt * TILE_LANES if lt < FIRST else 0
            below = HALO1 + lt * 10 if lt < FIRST else HALO2
            for part in range(2):
                for phase in range(6):
                    for half in range(2):
                        at = top + part * 96 + phase * 16 + half * 8
                        out[tile, pl.ds(at, 8), :] = rows_ref[
                            slot, part, lt, pl.ds(base + 6 * half + phase, 8, stride=12), :
                        ]
                out[tile, pl.ds(below + 5 * part, 5), :] = rows_ref[
                    slot, part, lt, pl.ds(base + TILE_ROWS, 5), :
                ]

    def two_tiles(index):
        tiles = (2 * index, 2 * index + 1)
        for slot, tile in enumerate(tiles):
            mask_rows(tile, slot)
        for tile in tiles:
            stage1[tile, pl.ds(ROWS1 - 16, 16), :] = jnp.zeros((16, 128), jnp.float32)
            stage2[tile, pl.ds(ROWS2 - 16, 16), :] = jnp.zeros((16, 128), jnp.float32)
        own_columns(tiles)
        for slot, tile in enumerate(tiles):
            spread(tile, slot)
        for tile in tiles:
            for send in sends(tile):
                send.start()

    for index in range(PIECES):
        piece(index).start()
    rows_ref[:, :, :, pl.ds(count, 24), :] = jnp.zeros((2, 2, LANE_TILES, 24, 128), jnp.float32)
    piece(0).wait()

    def step(index, carry):
        piece(index + 1).wait()
        two_tiles(index)
        return carry

    lax.fori_loop(0, PIECES - 1, step, 0)
    two_tiles(PIECES - 1)

    def finish(tile, carry):
        for send in sends(tile):
            send.wait()
        return carry

    lax.fori_loop(0, TILES, finish, 0)


def pack(slc, valid):
    return pl.pallas_call(
        pack_kernel,
        in_specs=[
            pl.BlockSpec(memory_space=pltpu.SMEM),
            pl.BlockSpec(memory_space=pl.ANY),
        ],
        out_specs=[pl.BlockSpec(memory_space=pl.ANY)] * 2,
        out_shape=[
            jax.ShapeDtypeStruct((TILES, ROWS1, 128), jnp.float32),
            jax.ShapeDtypeStruct((TILES, ROWS2, 128), jnp.float32),
        ],
        scratch_shapes=[
            pltpu.VMEM((2, 1536 + 16, COLS), jnp.float32),
            pltpu.VMEM((2, 2, LANE_TILES, TILE_ROWS + 40, 128), jnp.float32),
            pltpu.VMEM((TILES, ROWS1, 128), jnp.float32),
            pltpu.VMEM((TILES, ROWS2, 128), jnp.float32),
            pltpu.SemaphoreType.DMA((PIECES,)),
            pltpu.SemaphoreType.DMA((2, TILES)),
        ],
        compiler_params=pltpu.CompilerParams(vmem_limit_bytes=GRANT),
        cost_estimate=pl.CostEstimate(flops=10**6, bytes_accessed=2 * 10**7, transcendentals=0),
        name="pack",
    )(valid, slc)


def split(x):
    high = x.astype(jnp.bfloat16)
    return high, (x - high.astype(jnp.float32)).astype(jnp.bfloat16)


def field_of(t, u):
    return t if t == u else DATES + 2 * PAIR_AT[t, u]


def cross_products(data, t_part, u_tile, lanes, rows):
    real = imag = None
    for re_row, im_row in rows:
        a_t = data[re_row, pl.ds(t_part, 1), lanes]
        b_t = data[im_row, pl.ds(t_part, 1), lanes]
        a_u = data[re_row, pl.ds(u_tile * 8, 8), lanes]
        b_u = data[im_row, pl.ds(u_tile * 8, 8), lanes]
        re = a_t * a_u + b_t * b_u
        im = b_t * a_u - a_t * b_u
        real = re if real is None else real + re
        imag = im if imag is None else imag + im
    return real, imag


def dot(a, b):
    return jnp.dot(a, b, preferred_element_type=jnp.float32)


def main_products(msg, sums, lhs, pooled):
    last = lax.broadcasted_iota(jnp.int32, (8, 128), 0) == 7
    state = {"fields": 0, "chunks": 0}

    def load(kind, date, phase, half):
        source = msg if kind in "ab" else sums
        base = 0 if kind in "as" else 96
        return source[date, pl.ds(base + phase * 16 + half * 8, 8), :]

    def emit(field, first, whole):
        out0 = whole[0] + first[1]
        rolled = jnp.where(last, 0.0, pltpu.roll(first[0], 7, 0))
        out1 = whole[1] + rolled
        high, low = split(jnp.concatenate([out0, out1], axis=0))
        lhs[pl.ds(field * 16, 16), 0:128] = high
        lhs[pl.ds(field * 16, 16), 128:256] = low
        state["fields"] += 1

    def drain():
        while (state["chunks"] + 1) * CHUNK <= state["fields"] * 16:
            pooled(state["chunks"])
            state["chunks"] += 1

    for t in range(DATES):
        first, whole = [], []
        for half in range(2):
            total = None
            for phase in range(6):
                a, b = load("a", t, phase, half), load("b", t, phase, half)
                term = a * a + b * b
                if phase == 5:
                    first.append(total)
                total = term if total is None else total + term
            whole.append(total)
        emit(t, first, whole)

    for ts, us in GROUPS:
        pairs = [(t, u) for t in ts for u in us]
        first = {pair: ([], []) for pair in pairs}
        whole = {pair: ([], []) for pair in pairs}
        for half in range(2):
            acc = {}
            for phase in range(6):
                s_t = {t: load("s", t, phase, half) for t in ts}
                a_t = {t: load("a", t, phase, half) for t in ts}
                b_t = {t: load("b", t, phase, half) for t in ts}
                a_u = {u: load("a", u, phase, half) for u in us}
                s_u = {u: load("s", u, phase, half) for u in us}
                d_u = {u: load("d", u, phase, half) for u in us}
                for t, u in pairs:
                    p = a_u[u] * s_t[t]
                    q = d_u[u] * b_t[t]
                    r = s_u[u] * a_t[t]
                    if phase == 0:
                        acc[t, u] = (p, q, r)
                    elif phase < 5:
                        p0, q0, r0 = acc[t, u]
                        acc[t, u] = (p0 + p, q0 + q, r0 + r)
                    else:
                        p0, q0, r0 = acc[t, u]
                        re5, im5 = p0 - q0, p0 - r0
                        first[t, u][0].append(re5)
                        first[t, u][1].append(im5)
                        whole[t, u][0].append(re5 + (p - q))
                        whole[t, u][1].append(im5 + (p - r))
        for pair in pairs:
            for part in range(2):
                emit(field_of(*pair) + part, first[pair][part], whole[pair][part])
        drain()


def dot(a, b):
    return jnp.dot(a, b, preferred_element_type=jnp.float32)


def side_products(small, t, rows, put):
    for u_tile in range(2):
        if u_tile < t // 8:
            values = (jnp.zeros((8, 128), jnp.float32),) * 2
        else:
            values = cross_products(small, t, u_tile, pl.ds(0, 128), rows)
        for part in range(2):
            put(part * 256 + t * 16 + u_tile * 8, values[part])


def fill_sums(msg, sums):
    def fill(date, carry):
        a = msg[date, pl.ds(0, 96), :]
        b = msg[date, pl.ds(96, 96), :]
        sums[date, pl.ds(0, 96), :] = a + b
        sums[date, pl.ds(96, 96), :] = a - b
        return carry

    lax.fori_loop(0, DATES, fill, 0, unroll=2)


def halo_products(small, side_lhs):
    def put(at, value):
        side_lhs[pl.ds(at, 8), :] = value

    for t in range(DATES):
        side_products(small, t, [(p, 5 + p) for p in range(5)], put)


def pool_side(side_lhs, table):
    high, low = split(side_lhs[...])
    return dot(jnp.concatenate([high, low], axis=1), table)


def chunk_rows(chunk):
    return pl.ds(chunk * CHUNK, CHUNK)


def first_kernel(
    msg, below_msg, table, part_out, out, sums, lhs, small, side_lhs, res, halo, coh, vec, weight,
    rows, weights,
):
    step = pl.program_id(0)
    weights[...] = table[0].astype(jnp.bfloat16)
    fill_sums(msg, sums)
    for date in range(DATES):
        for row in range(10):
            small[row, date : date + 1, :] = below_msg[date, pl.ds(step * 10 + row, 1), :]
    halo_products(small, side_lhs)
    halo[step] = pool_side(side_lhs, weights[...])

    def pooled(chunk):
        res[step, chunk_rows(chunk), :] = dot(lhs[chunk_rows(chunk), :], weights[...])

    main_products(msg, sums, lhs, pooled)

    @pl.when(step == FIRST - 1)
    def _():
        lane = lax.broadcasted_iota(jnp.int32, (8, 128), 1)
        last = lax.broadcasted_iota(jnp.int32, (8, 128), 0) == 7

        def total(ref, group, at, count):
            value = None
            for lt in range(FIRST):
                if group in FEEDS[lt]:
                    place = FEEDS[lt].index(group) * 128
                    own = ref[lt, pl.ds(at, count), place : place + 128]
                    value = own if value is None else value + own
            return value

        def below(group, t, u, part):
            return total(halo, group, part * 256 + t * 16 + u, 1)

        def paired(group, even, t, u, part):
            at = (field_of(t, u) + part) * 16
            value = jnp.where(even, total(res, group, at, 8), total(res, group, at + 8, 8))
            return value + jnp.where(last & ~even, below(group, t, u, part), 0.0)

        even = (lane < 32) | (lane >= 96)
        for t in range(DATES):
            for u in range(t, DATES):
                for part in range(1 if t == u else 2):
                    at = (field_of(t, u) + part) * 8
                    part_out[pl.ds(at, 8), :] = paired(2, even, t, u, part)

        for half in range(2):

            def cov(t, u, part):
                value = total(res, 0, (field_of(t, u) + part) * 16 + half * 8, 8)
                if half == 1:
                    value = value + jnp.where(last, below(0, t, u, part), 0.0)
                return value

            solve(cov, coh, vec, weight)
            for date in range(DATES):
                for part in range(2):
                    rows[part, date, 0, pl.ds(half, 8, stride=2), :] = vec[part, date]

        even_b = (lane >= 32) & (lane < 96)
        solve(functools.partial(paired, 1, even_b), coh, vec, weight)
        for date in range(DATES):
            for part in range(2):
                value = vec[part, date]
                rows[part, date, 1, pl.ds(0, 8, stride=2), :] = value
                rows[part, date, 1, pl.ds(1, 8, stride=2), :] = pltpu.roll(value, 64, 1)
        out[:, :, :, 0:128] = rows[:, :, 0]
        left = lax.broadcasted_iota(jnp.int32, (2, DATES, BLOCKS, 128), 3) < 32
        out[:, :, :, 128:256] = jnp.where(left, rows[:, :, 0], rows[:, :, 1])


def last_kernel(
    msg, beside_msg, table, pool, partial_hbm, done_hbm, out, sums, lhs, small, side_lhs, res, halo,
    pairs, edge, coh, vec, weight, rows, weights, partial, done, sems,
):
    copies = [
        pltpu.make_async_copy(partial_hbm, partial, sems.at[0]),
        pltpu.make_async_copy(done_hbm, done, sems.at[1]),
    ]
    for copy in copies:
        copy.start()
    col = lax.axis_index("col")
    cols = beside_msg.shape[0]
    fill_sums(msg, sums)
    for date in range(DATES):
        for row in range(10):
            small[row, date : date + 1, :] = msg[date, HALO2 + row : HALO2 + row + 1, :]
        for part in range(2):
            own = OWN_ROW - OWN_TILE + part
            before = beside_msg[jnp.maximum(col - 1, 0), date, own + 2 : own + 3, :]
            after = beside_msg[jnp.minimum(col + 1, cols - 1), date, own : own + 1, :]
            small[10 + part, date : date + 1, :] = jnp.where(col > 0, before, 0.0)
            small[12 + part, date : date + 1, :] = jnp.where(col < cols - 1, after, 0.0)
    halo_products(small, side_lhs)
    weights[...] = table[0].astype(jnp.bfloat16)
    halo[...] = pool_side(side_lhs, weights[...])
    for side in range(2):
        row = 10 + 2 * side

        def put(at, value):
            pairs[pl.ds(2 * at + 1 - side, 8, stride=2), :] = value

        for t in range(DATES):
            side_products(small, t, [(row, row + 1)], put)
    dims = (((1,), (1,)), ((), ()))
    high, low = split(pairs[...])
    pool2 = pool[...].astype(jnp.bfloat16)
    sides = lax.dot_general(
        pool2, high, dims, preferred_element_type=jnp.float32
    ) + lax.dot_general(pool2, low, dims, preferred_element_type=jnp.float32)
    lower = lax.broadcasted_iota(jnp.int32, (8, 128), 1) < 64
    for group in range(SIDE // 64):
        tile = slice(group * 128, group * 128 + 128)
        even_rows, odd_rows = sides[0:8, tile], sides[8:16, tile]
        edge[2 * group] = jnp.where(lower, even_rows, pltpu.roll(odd_rows, 64, 1))
        edge[2 * group + 1] = jnp.where(lower, pltpu.roll(even_rows, 64, 1), odd_rows)

    def pooled(chunk):
        res[chunk_rows(chunk), :] = dot(lhs[chunk_rows(chunk), :], weights[...])

    main_products(msg, sums, lhs, pooled)

    lane = lax.broadcasted_iota(jnp.int32, (8, 128), 1)
    last = lax.broadcasted_iota(jnp.int32, (8, 128), 0) == 7
    even = (lane < 32) | (lane >= 96)
    beside = (lane == 0) | (lane == 127) | (lane == 63) | (lane == 64)
    for copy in copies:
        copy.wait()

    def cov(t, u, part):
        field = field_of(t, u) + part
        at = field * 16
        value = jnp.where(even, res[pl.ds(at, 8), :], res[pl.ds(at + 8, 8), :])
        index = part * 256 + t * 16 + u
        value = value + jnp.where(last & ~even, halo[pl.ds(index, 1), :], 0.0)
        turned = pltpu.roll(edge[index // 32], (127 - 2 * (index % 32)) % 128, 1)
        return value + partial[pl.ds(field * 8, 8), :] + jnp.where(beside, turned, 0.0)

    solve(cov, coh, vec, weight)
    for date in range(DATES):
        for part in range(2):
            value = vec[part, date]
            rows[part, date, 0, pl.ds(0, 8, stride=2), :] = value
            rows[part, date, 0, pl.ds(1, 8, stride=2), :] = pltpu.roll(value, 64, 1)
    place = lax.broadcasted_iota(jnp.int32, (2, DATES, BLOCKS, 128), 3)
    out[:, :, :, 0:128] = jnp.where(place < 32, rows[:, :, 0], done[:, :, :, 0:128])
    out[:, :, :, 128:256] = jnp.where(place >= 96, rows[:, :, 0], done[:, :, :, 128:256])


def inverse_norm(vec):
    terms = [vec[part, t] * vec[part, t] for t in range(DATES) for part in range(2)]
    while len(terms) > 1:
        terms = [terms[i] + terms[i + 1] for i in range(0, len(terms), 2)]
    return lax.rsqrt(terms[0])


def solve(cov, coh, vec, weight):
    inv = []
    for t in range(DATES):
        diag = cov(t, t, 0)
        root = lax.rsqrt(jnp.maximum(diag, FLOOR))
        inv.append(root)
        weight[t] = diag * (root * root) + 1.0
    row_real = [weight[t] for t in range(DATES)]
    row_imag = [None] * DATES
    for i, (t, u) in enumerate(PAIRS):
        factor = inv[t] * inv[u]
        real = cov(t, u, 0) * factor
        imag = cov(t, u, 1) * factor
        coh[i, 0] = real
        coh[i, 1] = real + imag
        coh[i, 2] = imag - real
        row_real[t] = row_real[t] + real
        row_real[u] = row_real[u] + real
        row_imag[t] = imag if row_imag[t] is None else row_imag[t] + imag
        row_imag[u] = -imag if row_imag[u] is None else row_imag[u] - imag
    for t in range(DATES):
        real, imag = 0.25 * row_real[t], 0.25 * row_imag[t]
        vec[0, t] = real
        vec[1, t] = imag
        vec[2, t] = real + imag

    def iterate(_, carry):
        scale = inverse_norm(vec)
        new_real, new_imag = [None] * DATES, [None] * DATES
        sums = [[None, None, None] for _ in range(DATES)]

        def add(t, which, value, minus=False):
            if sums[t][which] is None:
                sums[t][which] = -value if minus else value
            elif minus:
                sums[t][which] = sums[t][which] - value
            else:
                sums[t][which] = sums[t][which] + value

        def pair(t, u, v):
            i = PAIR_AT[t, u]
            real, plus, minus = coh[i, 0], coh[i, 1], coh[i, 2]
            add(t, 0, real * v[u][2])
            add(t, 1, plus * v[u][1])
            add(t, 2, minus * v[u][0])
            add(u, 0, real * v[t][2])
            add(u, 1, minus * v[t][1], True)
            add(u, 2, plus * v[t][0], True)

        for first in range(0, DATES, 4):
            for second in range(first, DATES, 4):
                dates = sorted(set(range(first, first + 4)) | set(range(second, second + 4)))
                v = {t: (vec[0, t], vec[1, t], vec[2, t]) for t in dates}
                for t in range(first, first + 4):
                    for u in range(second, second + 4):
                        if t < u:
                            pair(t, u, v)
        for t in range(DATES):
            own = weight[t]
            new_real[t] = (sums[t][0] - sums[t][1]) + own * vec[0, t]
            new_imag[t] = (sums[t][0] + sums[t][2]) + own * vec[1, t]
        for t in range(DATES):
            real, imag = new_real[t] * scale, new_imag[t] * scale
            vec[0, t] = real
            vec[1, t] = imag
            vec[2, t] = real + imag
        return carry

    lax.fori_loop(0, ITERS - 1, iterate, 0)
    scale = inverse_norm(vec)
    for t in range(DATES):
        for part in range(2):
            vec[part, t] = vec[part, t] * scale


def whole(*shape):
    return pl.BlockSpec(shape, lambda i: (0,) * len(shape))


def common_scratch(small_rows):
    return [
        pltpu.VMEM((DATES, TILE_LANES, 128), jnp.float32),
        pltpu.VMEM((FIELDS * 16, 256), jnp.bfloat16),
        pltpu.VMEM((small_rows, DATES, 128), jnp.float32),
        pltpu.VMEM((SIDE, 128), jnp.float32),
    ]


SOLVE_SCRATCH = [
    pltpu.VMEM((len(PAIRS), 3, 8, 128), jnp.float32),
    pltpu.VMEM((3, DATES, 8, 128), jnp.float32),
    pltpu.VMEM((DATES, 8, 128), jnp.float32),
]
LINKED = (2, DATES, BLOCKS, OUT_COLS)
PARTIAL = (FIELDS * 8, 128)


def cut_kernel(in_ref, out_ref):
    out_ref[...] = in_ref[...]


def cut_columns(message):
    return pl.pallas_call(
        cut_kernel,
        grid=(1,),
        in_specs=[pl.BlockSpec((DATES, 8, 128), lambda i: (0, OWN_TILE // 8, 0))],
        out_specs=whole(DATES, 8, 128),
        out_shape=jax.ShapeDtypeStruct((DATES, 8, 128), jnp.float32),
        compiler_params=pltpu.CompilerParams(vmem_limit_bytes=GRANT),
        name="cut_columns",
    )(message)


def link_first(message, tables):
    return pl.pallas_call(
        first_kernel,
        grid=(FIRST,),
        in_specs=[
            pl.BlockSpec((DATES, TILE_LANES, 128), lambda i: (0, i, 0)),
            pl.BlockSpec((DATES, 64, 128), lambda i: (0, HALO1 // 64, 0)),
            pl.BlockSpec((1, 256, 256), lambda i: (i, 0, 0)),
        ],
        out_specs=[whole(*PARTIAL), whole(*LINKED)],
        out_shape=[
            jax.ShapeDtypeStruct(PARTIAL, jnp.float32),
            jax.ShapeDtypeStruct(LINKED, jnp.float32),
        ],
        scratch_shapes=common_scratch(10)
        + [
            pltpu.VMEM((FIRST, FIELDS * 16, 256), jnp.float32),
            pltpu.VMEM((FIRST, SIDE, 256), jnp.float32),
        ]
        + SOLVE_SCRATCH
        + [pltpu.VMEM((2, DATES, 2, BLOCKS, 128), jnp.float32), pltpu.VMEM((256, 256), jnp.bfloat16)],
        compiler_params=pltpu.CompilerParams(vmem_limit_bytes=GRANT),
        cost_estimate=pl.CostEstimate(flops=10**9, bytes_accessed=10**7, transcendentals=0),
        name="link_first",
    )(message, message, tables)


def link_last(message, beside, tables, pool, partial, done):
    return pl.pallas_call(
        last_kernel,
        grid=(1,),
        in_specs=[
            whole(DATES, ROWS2, 128),
            whole(*beside.shape),
            pl.BlockSpec((1, 256, 128), lambda i: (FIRST, 0, 0)),
            whole(16, 128),
            pl.BlockSpec(memory_space=pl.ANY),
            pl.BlockSpec(memory_space=pl.ANY),
        ],
        out_specs=whole(*LINKED),
        out_shape=jax.ShapeDtypeStruct(LINKED, jnp.float32),
        scratch_shapes=common_scratch(14)
        + [
            pltpu.VMEM((FIELDS * 16, 128), jnp.float32),
            pltpu.VMEM((SIDE, 128), jnp.float32),
            pltpu.VMEM((2 * SIDE, 128), jnp.float32),
            pltpu.VMEM((SIDE // 32, 8, 128), jnp.float32),
        ]
        + SOLVE_SCRATCH
        + [
            pltpu.VMEM((2, DATES, 1, BLOCKS, 128), jnp.float32),
            pltpu.VMEM((256, 128), jnp.bfloat16),
            pltpu.VMEM(PARTIAL, jnp.float32),
            pltpu.VMEM(LINKED, jnp.float32),
            pltpu.SemaphoreType.DMA((2,)),
        ],
        compiler_params=pltpu.CompilerParams(vmem_limit_bytes=GRANT),
        cost_estimate=pl.CostEstimate(flops=10**8, bytes_accessed=10**7, transcendentals=0),
        name="link_last",
    )(message, beside, tables, pool, partial, done)


def local(slc, valid_rows):
    valid = valid_rows.T
    message1, message2 = pack(slc, valid)
    received1 = lax.all_to_all(message1, "row", 0, 0, tiled=True)
    received1, message2 = lax.optimization_barrier((received1, message2))
    received2 = lax.all_to_all(message2, "row", 0, 0, tiled=True)
    own = cut_columns(received1)
    beside = lax.all_gather(own, "col")
    tables, pool = column_tables()
    tables = jnp.asarray(tables)
    partial, done = link_first(received1, tables)
    return link_last(received2, beside, tables, jnp.asarray(pool), partial, done)


def solution(mesh):
    return jax.shard_map(
        local,
        mesh=mesh,
        in_specs=(P(None, "row", None, "col"), P()),
        out_specs=P(None, None, "row", "col"),
        check_vma=False,
    )
```

```python
import functools

import jax
import jax.numpy as jnp
import numpy as np
from jax import lax
from jax.experimental import pallas as pl
from jax.experimental.pallas import tpu as pltpu
from jax.sharding import PartitionSpec as P

ITERS = 10
FLOOR = 20.0
DATES = 16
TILES = 16
COLS = 768
LANE_TILES = 6
FIRST = 5
OUT_COLS = 256
BLOCKS = 16
TILE_ROWS = 6 * BLOCKS
TILE_LANES = 192
ROWS1 = 1024
HALO1 = FIRST * TILE_LANES
OWN_TILE = 1008
OWN_ROW = 1010
ROWS2 = 208
HALO2 = TILE_LANES
WINDOW = TILE_ROWS + 5
PIECES = 8
PIECE_ROWS = 192
GRANT = 60 * 1024 * 1024


def pair_groups():
    groups = []
    for i in range(0, DATES, 2):
        groups.append(([i], [i + 1]))
        rest = list(range(i + 2, DATES))
        for j in range(0, len(rest), 4):
            groups.append(([i, i + 1], rest[j : j + 4]))
    return groups


GROUPS = pair_groups()
PAIRS = [(t, u) for ts, us in GROUPS for t in ts for u in us]
PAIR_AT = {pair: i for i, pair in enumerate(PAIRS)}
FIELDS = DATES + 2 * len(PAIRS)
CHUNK = 512
SIDE = 512
FEEDS = ((0, 2), (0,), (0,), (0, 1), (1, 2), (2,))


def lane_columns():
    lane = np.arange(128)
    group_a = np.where(lane < 32, 128 + lane, lane)
    group_b = np.where((lane >= 32) & (lane < 96), 128 + lane, 128 + (lane + 64) % 128)
    own = np.where(lane < 32, lane, 128 + lane)
    other = (lane + 64) % 128
    far = np.where(other < 32, other, 128 + other)
    group_c = np.where((lane < 32) | (lane >= 96), own, far)
    return group_a, group_b, group_c


def column_tables():
    groups = lane_columns()
    tables = np.zeros((LANE_TILES, 256, 256), np.float32)
    for lt in range(LANE_TILES):
        column = (lt * 128 + np.arange(128) + 64) % COLS
        for place, group in enumerate(FEEDS[lt]):
            target = 3 * groups[group][None, :]
            inside = (column[:, None] >= target - 1) & (column[:, None] <= target + 3)
            for copy in range(2):
                tables[lt, copy * 128 : copy * 128 + 128, place * 128 : place * 128 + 128] = inside
    row = np.arange(128)
    pool = np.zeros((2, 8, 128), np.float32)
    for half in range(2):
        for s in range(8):
            block = 2 * s + half
            pool[half, s] = (row >= 6 * block) & (row <= 6 * block + 10)
    return tables, pool.reshape(16, 128)


def pack_kernel(valid_ref, slc, out1, out2, taken, rows_ref, stage1, stage2, in_sems, out_sems):
    me = lax.axis_index("row")
    low, high = valid_ref[0, me], valid_ref[1, me]
    lane = lax.broadcasted_iota(jnp.int32, (8, 128), 1)
    row = lax.broadcasted_iota(jnp.int32, (8, 128), 0)
    pick = jnp.where(((row == 0) & (lane == 64)) | ((row == 1) & (lane == 63)), 1.0, 0.0)
    count = TILE_ROWS + 16

    def piece(index):
        return pltpu.make_async_copy(
            slc.at[:, 0, pl.ds(index * PIECE_ROWS, PIECE_ROWS), :],
            taken.at[:, pl.ds(index * PIECE_ROWS + 8, PIECE_ROWS), :],
            in_sems.at[index],
        )

    def sends(tile):
        return (
            pltpu.make_async_copy(stage1.at[tile], out1.at[tile], out_sems.at[0, tile]),
            pltpu.make_async_copy(stage2.at[tile], out2.at[tile], out_sems.at[1, tile]),
        )

    def mask_rows(tile, slot):
        start = pl.multiple_of(tile * TILE_ROWS, 8)
        at_row = lax.broadcasted_iota(jnp.int32, (count, 128), 0) + (start - 8)
        keep = (at_row >= low) & (at_row < high)
        left = lax.broadcasted_iota(jnp.int32, (count, 128), 1) < 64
        for part in range(2):
            turned = []
            for lt in range(LANE_TILES):
                value = taken[part, pl.ds(start, count), lt * 128 : lt * 128 + 128]
                turned.append(pltpu.roll(jnp.where(keep, value, 0.0), 64, 1))
            for lt in range(LANE_TILES):
                rows_ref[slot, part, lt, 0:count, :] = jnp.where(
                    left, turned[lt], turned[(lt + 1) % LANE_TILES]
                )

    def own_columns(tiles):
        blocks = [
            rows_ref[slot, part, LANE_TILES - 1, pl.ds(5, 128), :]
            for slot in range(2)
            for part in range(2)
        ]
        rest = jnp.concatenate(blocks, axis=0)
        columns = None
        for _ in range(3):
            piece_of = rest.astype(jnp.bfloat16)
            rest = rest - piece_of.astype(jnp.float32)
            term = lax.dot_general(
                pick.astype(jnp.bfloat16), piece_of, (((1,), (1,)), ((), ())),
                preferred_element_type=jnp.float32,
            )
            columns = term if columns is None else columns + term
        for slot, tile in enumerate(tiles):
            for part in range(2):
                at = (2 * slot + part) * 128
                value = jnp.where(lane < WINDOW + 1, columns[:, at : at + 128], 0.0)
                for side in range(2):
                    row_at = pl.ds(OWN_ROW + 2 * side + part, 1)
                    stage1[tile, row_at, :] = value[side : side + 1]

    def spread(tile, slot):
        base = 5
        for lt in range(LANE_TILES):
            out = stage1 if lt < FIRST else stage2
            top = lt * TILE_LANES if lt < FIRST else 0
            below = HALO1 + lt * 10 if lt < FIRST else HALO2
            for part in range(2):
                for phase in range(6):
                    for half in range(2):
                        at = top + part * 96 + phase * 16 + half * 8
                        out[tile, pl.ds(at, 8), :] = rows_ref[
                            slot, part, lt, pl.ds(base + 6 * half + phase, 8, stride=12), :
                        ]
                out[tile, pl.ds(below + 5 * part, 5), :] = rows_ref[
                    slot, part, lt, pl.ds(base + TILE_ROWS, 5), :
                ]

    def two_tiles(index):
        tiles = (2 * index, 2 * index + 1)
        for slot, tile in enumerate(tiles):
            mask_rows(tile, slot)
        for tile in tiles:
            stage1[tile, pl.ds(ROWS1 - 16, 16), :] = jnp.zeros((16, 128), jnp.float32)
            stage2[tile, pl.ds(ROWS2 - 16, 16), :] = jnp.zeros((16, 128), jnp.float32)
        own_columns(tiles)
        for slot, tile in enumerate(tiles):
            spread(tile, slot)
        for tile in tiles:
            for send in sends(tile):
                send.start()

    for index in range(PIECES):
        piece(index).start()
    rows_ref[:, :, :, pl.ds(count, 24), :] = jnp.zeros((2, 2, LANE_TILES, 24, 128), jnp.float32)
    piece(0).wait()

    def step(index, carry):
        piece(index + 1).wait()
        two_tiles(index)
        return carry

    lax.fori_loop(0, PIECES - 1, step, 0)
    two_tiles(PIECES - 1)

    def finish(tile, carry):
        for send in sends(tile):
            send.wait()
        return carry

    lax.fori_loop(0, TILES, finish, 0)


def pack(slc, valid):
    return pl.pallas_call(
        pack_kernel,
        in_specs=[
            pl.BlockSpec(memory_space=pltpu.SMEM),
            pl.BlockSpec(memory_space=pl.ANY),
        ],
        out_specs=[pl.BlockSpec(memory_space=pl.ANY)] * 2,
        out_shape=[
            jax.ShapeDtypeStruct((TILES, ROWS1, 128), jnp.float32),
            jax.ShapeDtypeStruct((TILES, ROWS2, 128), jnp.float32),
        ],
        scratch_shapes=[
            pltpu.VMEM((2, 1536 + 16, COLS), jnp.float32),
            pltpu.VMEM((2, 2, LANE_TILES, TILE_ROWS + 40, 128), jnp.float32),
            pltpu.VMEM((TILES, ROWS1, 128), jnp.float32),
            pltpu.VMEM((TILES, ROWS2, 128), jnp.float32),
            pltpu.SemaphoreType.DMA((PIECES,)),
            pltpu.SemaphoreType.DMA((2, TILES)),
        ],
        compiler_params=pltpu.CompilerParams(vmem_limit_bytes=GRANT),
        cost_estimate=pl.CostEstimate(flops=10**6, bytes_accessed=2 * 10**7, transcendentals=0),
        name="pack",
    )(valid, slc)


def split(x):
    high = x.astype(jnp.bfloat16)
    return high, (x - high.astype(jnp.float32)).astype(jnp.bfloat16)


def field_of(t, u):
    return t if t == u else DATES + 2 * PAIR_AT[t, u]


def cross_products(data, t_part, u_tile, lanes, rows):
    real = imag = None
    for re_row, im_row in rows:
        a_t = data[re_row, pl.ds(t_part, 1), lanes]
        b_t = data[im_row, pl.ds(t_part, 1), lanes]
        a_u = data[re_row, pl.ds(u_tile * 8, 8), lanes]
        b_u = data[im_row, pl.ds(u_tile * 8, 8), lanes]
        re = a_t * a_u + b_t * b_u
        im = b_t * a_u - a_t * b_u
        real = re if real is None else real + re
        imag = im if imag is None else imag + im
    return real, imag


def dot(a, b):
    return jnp.dot(a, b, preferred_element_type=jnp.float32)


def main_products(msg, sums, lhs, pooled):
    last = lax.broadcasted_iota(jnp.int32, (8, 128), 0) == 7
    state = {"fields": 0, "chunks": 0}

    def load(kind, date, phase, half):
        source = msg if kind in "ab" else sums
        base = 0 if kind in "as" else 96
        return source[date, pl.ds(base + phase * 16 + half * 8, 8), :]

    def emit(field, first, whole):
        out0 = whole[0] + first[1]
        rolled = jnp.where(last, 0.0, pltpu.roll(first[0], 7, 0))
        out1 = whole[1] + rolled
        high, low = split(jnp.concatenate([out0, out1], axis=0))
        lhs[pl.ds(field * 16, 16), 0:128] = high
        lhs[pl.ds(field * 16, 16), 128:256] = low
        state["fields"] += 1

    def drain():
        while (state["chunks"] + 1) * CHUNK <= state["fields"] * 16:
            pooled(state["chunks"])
            state["chunks"] += 1

    for t in range(DATES):
        first, whole = [], []
        for half in range(2):
            total = None
            for phase in range(6):
                a, b = load("a", t, phase, half), load("b", t, phase, half)
                term = a * a + b * b
                if phase == 5:
                    first.append(total)
                total = term if total is None else total + term
            whole.append(total)
        emit(t, first, whole)

    for ts, us in GROUPS:
        pairs = [(t, u) for t in ts for u in us]
        first = {pair: ([], []) for pair in pairs}
        whole = {pair: ([], []) for pair in pairs}
        for half in range(2):
            acc = {}
            for phase in range(6):
                s_t = {t: load("s", t, phase, half) for t in ts}
                a_t = {t: load("a", t, phase, half) for t in ts}
                b_t = {t: load("b", t, phase, half) for t in ts}
                a_u = {u: load("a", u, phase, half) for u in us}
                s_u = {u: load("s", u, phase, half) for u in us}
                d_u = {u: load("d", u, phase, half) for u in us}
                for t, u in pairs:
                    p = a_u[u] * s_t[t]
                    q = d_u[u] * b_t[t]
                    r = s_u[u] * a_t[t]
                    if phase == 0:
                        acc[t, u] = (p, q, r)
                    elif phase < 5:
                        p0, q0, r0 = acc[t, u]
                        acc[t, u] = (p0 + p, q0 + q, r0 + r)
                    else:
                        p0, q0, r0 = acc[t, u]
                        re5, im5 = p0 - q0, p0 - r0
                        first[t, u][0].append(re5)
                        first[t, u][1].append(im5)
                        whole[t, u][0].append(re5 + (p - q))
                        whole[t, u][1].append(im5 + (p - r))
        for pair in pairs:
            for part in range(2):
                emit(field_of(*pair) + part, first[pair][part], whole[pair][part])
        drain()


def dot(a, b):
    return jnp.dot(a, b, preferred_element_type=jnp.float32)


def side_products(small, t, rows, put):
    for u_tile in range(2):
        if u_tile < t // 8:
            values = (jnp.zeros((8, 128), jnp.float32),) * 2
        else:
            values = cross_products(small, t, u_tile, pl.ds(0, 128), rows)
        for part in range(2):
            put(part * 256 + t * 16 + u_tile * 8, values[part])


def fill_sums(msg, sums):
    def fill(date, carry):
        a = msg[date, pl.ds(0, 96), :]
        b = msg[date, pl.ds(96, 96), :]
        sums[date, pl.ds(0, 96), :] = a + b
        sums[date, pl.ds(96, 96), :] = a - b
        return carry

    for date in range(DATES):
        fill(date, 0)


def halo_products(small, side_lhs):
    def put(at, value):
        side_lhs[pl.ds(at, 8), :] = value

    for t in range(DATES):
        side_products(small, t, [(p, 5 + p) for p in range(5)], put)


def pool_side(side_lhs, table):
    high, low = split(side_lhs[...])
    return dot(jnp.concatenate([high, low], axis=1), table)


def chunk_rows(chunk):
    return pl.ds(chunk * CHUNK, CHUNK)


def done_rows(part, date, mt):
    return pl.ds(FIELDS * 8 + ((part * DATES + date) * 2 + mt) * BLOCKS, BLOCKS)


def first_kernel(
    msg, below_msg, table, part_out, sums, lhs, small, side_lhs, res, halo, coh, vec, weight,
    rows, weights,
):
    step = pl.program_id(0)
    weights[...] = table[0].astype(jnp.bfloat16)
    fill_sums(msg, sums)
    for date in range(DATES):
        for row in range(10):
            small[row, date : date + 1, :] = below_msg[date, pl.ds(step * 10 + row, 1), :]

    def pooled(chunk):
        res[step, chunk_rows(chunk), :] = dot(lhs[chunk_rows(chunk), :], weights[...])

    main_products(msg, sums, lhs, pooled)
    halo_products(small, side_lhs)
    halo[step] = pool_side(side_lhs, weights[...])

    @pl.when(step == FIRST - 1)
    def _():
        lane = lax.broadcasted_iota(jnp.int32, (8, 128), 1)
        last = lax.broadcasted_iota(jnp.int32, (8, 128), 0) == 7

        def total(ref, group, at, count):
            value = None
            for lt in range(FIRST):
                if group in FEEDS[lt]:
                    place = FEEDS[lt].index(group) * 128
                    own = ref[lt, pl.ds(at, count), place : place + 128]
                    value = own if value is None else value + own
            return value

        def below(group, t, u, part):
            return total(halo, group, part * 256 + t * 16 + u, 1)

        def paired(group, even, t, u, part):
            at = (field_of(t, u) + part) * 16
            value = jnp.where(even, total(res, group, at, 8), total(res, group, at + 8, 8))
            return value + jnp.where(last & ~even, below(group, t, u, part), 0.0)

        even = (lane < 32) | (lane >= 96)
        for t in range(DATES):
            for u in range(t, DATES):
                for part in range(1 if t == u else 2):
                    at = (field_of(t, u) + part) * 8
                    part_out[pl.ds(at, 8), :] = paired(2, even, t, u, part)

        for half in range(2):

            def cov(t, u, part):
                value = total(res, 0, (field_of(t, u) + part) * 16 + half * 8, 8)
                if half == 1:
                    value = value + jnp.where(last, below(0, t, u, part), 0.0)
                return value

            solve(cov, coh, vec, weight)
            for date in range(DATES):
                for part in range(2):
                    rows[part, date, 0, pl.ds(half, 8, stride=2), :] = vec[part, date]

        even_b = (lane >= 32) & (lane < 96)
        solve(functools.partial(paired, 1, even_b), coh, vec, weight)
        for date in range(DATES):
            for part in range(2):
                value = vec[part, date]
                rows[part, date, 1, pl.ds(0, 8, stride=2), :] = value
                rows[part, date, 1, pl.ds(1, 8, stride=2), :] = pltpu.roll(value, 64, 1)
        left = lax.broadcasted_iota(jnp.int32, (BLOCKS, 128), 1) < 32
        for part in range(2):
            for date in range(DATES):
                one, two = rows[part, date, 0], rows[part, date, 1]
                part_out[done_rows(part, date, 0), :] = one
                part_out[done_rows(part, date, 1), :] = jnp.where(left, one, two)


def last_kernel(
    msg, left, right, table, pool, partial_hbm, out, sums, lhs, small, side_lhs, res, halo,
    pairs, edge, coh, vec, weight, rows, weights, partial, sem,
):
    copy = pltpu.make_async_copy(partial_hbm, partial, sem)
    copy.start()
    fill_sums(msg, sums)
    for date in range(DATES):
        for row in range(10):
            small[row, date : date + 1, :] = msg[date, HALO2 + row : HALO2 + row + 1, :]
        for part in range(2):
            own = OWN_ROW - OWN_TILE + part
            small[10 + part, date : date + 1, :] = left[date, own + 2 : own + 3, :]
            small[12 + part, date : date + 1, :] = right[date, own : own + 1, :]
    halo_products(small, side_lhs)
    weights[...] = table[0].astype(jnp.bfloat16)
    halo[...] = pool_side(side_lhs, weights[...])
    for side in range(2):
        row = 10 + 2 * side

        def put(at, value):
            pairs[pl.ds(2 * at + 1 - side, 8, stride=2), :] = value

        for t in range(DATES):
            side_products(small, t, [(row, row + 1)], put)
    dims = (((1,), (1,)), ((), ()))
    high, low = split(pairs[...])
    pool2 = pool[...].astype(jnp.bfloat16)
    sides = lax.dot_general(
        pool2, high, dims, preferred_element_type=jnp.float32
    ) + lax.dot_general(pool2, low, dims, preferred_element_type=jnp.float32)
    lower = lax.broadcasted_iota(jnp.int32, (8, 128), 1) < 64
    for group in range(SIDE // 64):
        tile = slice(group * 128, group * 128 + 128)
        even_rows, odd_rows = sides[0:8, tile], sides[8:16, tile]
        edge[2 * group] = jnp.where(lower, even_rows, pltpu.roll(odd_rows, 64, 1))
        edge[2 * group + 1] = jnp.where(lower, pltpu.roll(even_rows, 64, 1), odd_rows)

    def pooled(chunk):
        res[chunk_rows(chunk), :] = dot(lhs[chunk_rows(chunk), :], weights[...])

    main_products(msg, sums, lhs, pooled)

    lane = lax.broadcasted_iota(jnp.int32, (8, 128), 1)
    last = lax.broadcasted_iota(jnp.int32, (8, 128), 0) == 7
    even = (lane < 32) | (lane >= 96)
    beside = (lane == 0) | (lane == 127) | (lane == 63) | (lane == 64)
    copy.wait()

    def cov(t, u, part):
        field = field_of(t, u) + part
        at = field * 16
        value = jnp.where(even, res[pl.ds(at, 8), :], res[pl.ds(at + 8, 8), :])
        index = part * 256 + t * 16 + u
        value = value + jnp.where(last & ~even, halo[pl.ds(index, 1), :], 0.0)
        turned = pltpu.roll(edge[index // 32], (127 - 2 * (index % 32)) % 128, 1)
        return value + partial[pl.ds(field * 8, 8), :] + jnp.where(beside, turned, 0.0)

    solve(cov, coh, vec, weight)
    for date in range(DATES):
        for part in range(2):
            value = vec[part, date]
            rows[part, date, 0, pl.ds(0, 8, stride=2), :] = value
            rows[part, date, 0, pl.ds(1, 8, stride=2), :] = pltpu.roll(value, 64, 1)
    place = lax.broadcasted_iota(jnp.int32, (BLOCKS, 128), 1)
    for part in range(2):
        for date in range(DATES):
            own = rows[part, date, 0]
            for mt, mine in ((0, place < 32), (1, place >= 96)):
                out[part, date, :, mt * 128 : mt * 128 + 128] = jnp.where(
                    mine, own, partial[done_rows(part, date, mt), :]
                )


def inverse_norm(vec):
    terms = [vec[part, t] * vec[part, t] for t in range(DATES) for part in range(2)]
    while len(terms) > 1:
        terms = [terms[i] + terms[i + 1] for i in range(0, len(terms), 2)]
    return lax.rsqrt(terms[0])


def solve(cov, coh, vec, weight):
    inv = []
    for t in range(DATES):
        diag = cov(t, t, 0)
        root = lax.rsqrt(jnp.maximum(diag, FLOOR))
        inv.append(root)
        weight[t] = diag * (root * root) + 1.0
    row_real = [weight[t] for t in range(DATES)]
    row_imag = [None] * DATES
    for i, (t, u) in enumerate(PAIRS):
        factor = inv[t] * inv[u]
        real = cov(t, u, 0) * factor
        imag = cov(t, u, 1) * factor
        coh[i, 0] = real
        coh[i, 1] = real + imag
        coh[i, 2] = imag - real
        row_real[t] = row_real[t] + real
        row_real[u] = row_real[u] + real
        row_imag[t] = imag if row_imag[t] is None else row_imag[t] + imag
        row_imag[u] = -imag if row_imag[u] is None else row_imag[u] - imag
    for t in range(DATES):
        real, imag = 0.25 * row_real[t], 0.25 * row_imag[t]
        vec[0, t] = real
        vec[1, t] = imag
        vec[2, t] = real + imag

    def iterate(_, carry):
        scale = inverse_norm(vec)
        new_real, new_imag = [None] * DATES, [None] * DATES
        sums = [[None, None, None] for _ in range(DATES)]

        def add(t, which, value, minus=False):
            if sums[t][which] is None:
                sums[t][which] = -value if minus else value
            elif minus:
                sums[t][which] = sums[t][which] - value
            else:
                sums[t][which] = sums[t][which] + value

        def pair(t, u, v):
            i = PAIR_AT[t, u]
            real, plus, minus = coh[i, 0], coh[i, 1], coh[i, 2]
            add(t, 0, real * v[u][2])
            add(t, 1, plus * v[u][1])
            add(t, 2, minus * v[u][0])
            add(u, 0, real * v[t][2])
            add(u, 1, minus * v[t][1], True)
            add(u, 2, plus * v[t][0], True)

        for first in range(0, DATES, 4):
            for second in range(first, DATES, 4):
                dates = sorted(set(range(first, first + 4)) | set(range(second, second + 4)))
                v = {t: (vec[0, t], vec[1, t], vec[2, t]) for t in dates}
                for t in range(first, first + 4):
                    for u in range(second, second + 4):
                        if t < u:
                            pair(t, u, v)
        for t in range(DATES):
            own = weight[t]
            new_real[t] = (sums[t][0] - sums[t][1]) + own * vec[0, t]
            new_imag[t] = (sums[t][0] + sums[t][2]) + own * vec[1, t]
        for t in range(DATES):
            real, imag = new_real[t] * scale, new_imag[t] * scale
            vec[0, t] = real
            vec[1, t] = imag
            vec[2, t] = real + imag
        return carry

    lax.fori_loop(0, ITERS - 1, iterate, 0, unroll=3)
    scale = inverse_norm(vec)
    for t in range(DATES):
        for part in range(2):
            vec[part, t] = vec[part, t] * scale


def whole(*shape):
    return pl.BlockSpec(shape, lambda i: (0,) * len(shape))


def common_scratch(small_rows):
    return [
        pltpu.VMEM((DATES, TILE_LANES, 128), jnp.float32),
        pltpu.VMEM((FIELDS * 16, 256), jnp.bfloat16),
        pltpu.VMEM((small_rows, DATES, 128), jnp.float32),
        pltpu.VMEM((SIDE, 128), jnp.float32),
    ]


SOLVE_SCRATCH = [
    pltpu.VMEM((len(PAIRS), 3, 8, 128), jnp.float32),
    pltpu.VMEM((3, DATES, 8, 128), jnp.float32),
    pltpu.VMEM((DATES, 8, 128), jnp.float32),
]
LINKED = (2, DATES, BLOCKS, OUT_COLS)
PARTIAL = (FIELDS * 8 + 2 * DATES * 2 * BLOCKS, 128)


def cut_kernel(in_ref, out_ref):
    out_ref[...] = in_ref[...]


def cut_columns(message):
    return pl.pallas_call(
        cut_kernel,
        grid=(1,),
        in_specs=[pl.BlockSpec((DATES, 8, 128), lambda i: (0, OWN_TILE // 8, 0))],
        out_specs=whole(DATES, 8, 128),
        out_shape=jax.ShapeDtypeStruct((DATES, 8, 128), jnp.float32),
        compiler_params=pltpu.CompilerParams(vmem_limit_bytes=GRANT),
        name="cut_columns",
    )(message)


def link_first(message, tables):
    return pl.pallas_call(
        first_kernel,
        grid=(FIRST,),
        in_specs=[
            pl.BlockSpec((DATES, TILE_LANES, 128), lambda i: (0, i, 0)),
            pl.BlockSpec((DATES, 64, 128), lambda i: (0, HALO1 // 64, 0)),
            pl.BlockSpec((1, 256, 256), lambda i: (i, 0, 0)),
        ],
        out_specs=whole(*PARTIAL),
        out_shape=jax.ShapeDtypeStruct(PARTIAL, jnp.float32),
        scratch_shapes=common_scratch(10)
        + [
            pltpu.VMEM((FIRST, FIELDS * 16, 256), jnp.float32),
            pltpu.VMEM((FIRST, SIDE, 256), jnp.float32),
        ]
        + SOLVE_SCRATCH
        + [pltpu.VMEM((2, DATES, 2, BLOCKS, 128), jnp.float32), pltpu.VMEM((256, 256), jnp.bfloat16)],
        compiler_params=pltpu.CompilerParams(vmem_limit_bytes=GRANT),
        cost_estimate=pl.CostEstimate(flops=10**9, bytes_accessed=10**7, transcendentals=0),
        name="link_first",
    )(message, message, tables)


def link_last(message, left, right, tables, pool, partial):
    return pl.pallas_call(
        last_kernel,
        grid=(1,),
        in_specs=[
            whole(DATES, ROWS2, 128),
            whole(DATES, 8, 128),
            whole(DATES, 8, 128),
            whole(1, 256, 128),
            whole(16, 128),
            pl.BlockSpec(memory_space=pl.ANY),
        ],
        out_specs=whole(*LINKED),
        out_shape=jax.ShapeDtypeStruct(LINKED, jnp.float32),
        scratch_shapes=common_scratch(14)
        + [
            pltpu.VMEM((FIELDS * 16, 128), jnp.float32),
            pltpu.VMEM((SIDE, 128), jnp.float32),
            pltpu.VMEM((2 * SIDE, 128), jnp.float32),
            pltpu.VMEM((SIDE // 32, 8, 128), jnp.float32),
        ]
        + SOLVE_SCRATCH
        + [
            pltpu.VMEM((2, DATES, 1, BLOCKS, 128), jnp.float32),
            pltpu.VMEM((256, 128), jnp.bfloat16),
            pltpu.VMEM(PARTIAL, jnp.float32),
            pltpu.SemaphoreType.DMA,
        ],
        compiler_params=pltpu.CompilerParams(vmem_limit_bytes=24 * 1024 * 1024),
        cost_estimate=pl.CostEstimate(flops=10**8, bytes_accessed=10**7, transcendentals=0),
        name="link_last",
    )(message, left, right, tables, pool, partial)


def local(slc, valid_rows):
    valid = valid_rows.T
    size = lax.axis_size("col")
    up = [(i, i + 1) for i in range(size - 1)]
    down = [(i + 1, i) for i in range(size - 1)]
    message1, message2 = pack(slc, valid)
    received1 = lax.all_to_all(message1, "row", 0, 0, tiled=True)
    received1, message2 = lax.optimization_barrier((received1, message2))
    received2 = lax.all_to_all(message2, "row", 0, 0, tiled=True)
    own = cut_columns(received1)
    left = lax.ppermute(own, "col", up)
    right = lax.ppermute(own, "col", down)
    tables, pool = column_tables()
    last_table = jnp.asarray(tables[FIRST:, :, 0:128])
    partial = link_first(received1, jnp.asarray(tables))
    return link_last(received2, left, right, last_table, jnp.asarray(pool), partial)


def solution(mesh):
    return jax.shard_map(
        local,
        mesh=mesh,
        in_specs=(P(None, "row", None, "col"), P()),
        out_specs=P(None, None, "row", "col"),
        check_vma=False,
    )
```

```python
import functools

import jax
import jax.numpy as jnp
import numpy as np
from jax import lax
from jax.experimental import pallas as pl
from jax.experimental.pallas import tpu as pltpu
from jax.sharding import PartitionSpec as P

ITERS = 10
FLOOR = 20.0
DATES = 16
TILES = 16
COLS = 768
LANE_TILES = 6
FIRST = 5
OUT_COLS = 256
BLOCKS = 16
TILE_ROWS = 6 * BLOCKS
TILE_LANES = 192
ROWS1 = 1024
HALO1 = FIRST * TILE_LANES
OWN_TILE = 1008
OWN_ROW = 1010
ROWS2 = 208
HALO2 = TILE_LANES
WINDOW = TILE_ROWS + 5
PIECES = 8
PIECE_ROWS = 192
GRANT = 60 * 1024 * 1024


def pair_groups():
    groups = []
    for i in range(0, DATES, 2):
        groups.append(([i], [i + 1]))
        rest = list(range(i + 2, DATES))
        for j in range(0, len(rest), 4):
            groups.append(([i, i + 1], rest[j : j + 4]))
    return groups


GROUPS = pair_groups()
PAIRS = [(t, u) for ts, us in GROUPS for t in ts for u in us]
PAIR_AT = {pair: i for i, pair in enumerate(PAIRS)}
FIELDS = DATES + 2 * len(PAIRS)
CHUNK = 512
SIDE = 512
FEEDS = ((0, 2), (0,), (0,), (0, 1), (1, 2), (2,))


def lane_columns():
    lane = np.arange(128)
    group_a = np.where(lane < 32, 128 + lane, lane)
    group_b = np.where((lane >= 32) & (lane < 96), 128 + lane, 128 + (lane + 64) % 128)
    own = np.where(lane < 32, lane, 128 + lane)
    other = (lane + 64) % 128
    far = np.where(other < 32, other, 128 + other)
    group_c = np.where((lane < 32) | (lane >= 96), own, far)
    return group_a, group_b, group_c


def column_tables():
    groups = lane_columns()
    tables = np.zeros((LANE_TILES, 256, 256), np.float32)
    for lt in range(LANE_TILES):
        column = (lt * 128 + np.arange(128) + 64) % COLS
        for place, group in enumerate(FEEDS[lt]):
            target = 3 * groups[group][None, :]
            inside = (column[:, None] >= target - 1) & (column[:, None] <= target + 3)
            for copy in range(2):
                tables[lt, copy * 128 : copy * 128 + 128, place * 128 : place * 128 + 128] = inside
    row = np.arange(128)
    pool = np.zeros((2, 8, 128), np.float32)
    for half in range(2):
        for s in range(8):
            block = 2 * s + half
            pool[half, s] = (row >= 6 * block) & (row <= 6 * block + 10)
    return tables, pool.reshape(16, 128)


def pack_kernel(valid_ref, slc, out1, out2, taken, rows_ref, stage1, stage2, in_sems, out_sems):
    me = lax.axis_index("row")
    low, high = valid_ref[0, me], valid_ref[1, me]
    lane = lax.broadcasted_iota(jnp.int32, (8, 128), 1)
    row = lax.broadcasted_iota(jnp.int32, (8, 128), 0)
    pick = jnp.where(((row == 0) & (lane == 64)) | ((row == 1) & (lane == 63)), 1.0, 0.0)
    count = TILE_ROWS + 16

    def piece(index):
        return pltpu.make_async_copy(
            slc.at[:, 0, pl.ds(index * PIECE_ROWS, PIECE_ROWS), :],
            taken.at[:, pl.ds(index * PIECE_ROWS + 8, PIECE_ROWS), :],
            in_sems.at[index],
        )

    def sends(tile):
        return (
            pltpu.make_async_copy(stage1.at[tile], out1.at[tile], out_sems.at[0, tile]),
            pltpu.make_async_copy(stage2.at[tile], out2.at[tile], out_sems.at[1, tile]),
        )

    def mask_rows(tile, slot):
        start = pl.multiple_of(tile * TILE_ROWS, 8)
        at_row = lax.broadcasted_iota(jnp.int32, (count, 128), 0) + (start - 8)
        keep = (at_row >= low) & (at_row < high)
        left = lax.broadcasted_iota(jnp.int32, (count, 128), 1) < 64
        for part in range(2):
            turned = []
            for lt in range(LANE_TILES):
                value = taken[part, pl.ds(start, count), lt * 128 : lt * 128 + 128]
                turned.append(pltpu.roll(jnp.where(keep, value, 0.0), 64, 1))
            for lt in range(LANE_TILES):
                rows_ref[slot, part, lt, 0:count, :] = jnp.where(
                    left, turned[lt], turned[(lt + 1) % LANE_TILES]
                )

    def own_columns(tiles):
        blocks = [
            rows_ref[slot, part, LANE_TILES - 1, pl.ds(5, 128), :]
            for slot in range(2)
            for part in range(2)
        ]
        rest = jnp.concatenate(blocks, axis=0)
        columns = None
        for _ in range(3):
            piece_of = rest.astype(jnp.bfloat16)
            rest = rest - piece_of.astype(jnp.float32)
            term = lax.dot_general(
                pick.astype(jnp.bfloat16), piece_of, (((1,), (1,)), ((), ())),
                preferred_element_type=jnp.float32,
            )
            columns = term if columns is None else columns + term
        for slot, tile in enumerate(tiles):
            for part in range(2):
                at = (2 * slot + part) * 128
                value = jnp.where(lane < WINDOW + 1, columns[:, at : at + 128], 0.0)
                for side in range(2):
                    row_at = pl.ds(OWN_ROW + 2 * side + part, 1)
                    stage1[tile, row_at, :] = value[side : side + 1]

    def spread(tile, slot):
        base = 5
        for lt in range(LANE_TILES):
            out = stage1 if lt < FIRST else stage2
            top = lt * TILE_LANES if lt < FIRST else 0
            below = HALO1 + lt * 10 if lt < FIRST else HALO2
            for part in range(2):
                for phase in range(6):
                    for half in range(2):
                        at = top + part * 96 + phase * 16 + half * 8
                        out[tile, pl.ds(at, 8), :] = rows_ref[
                            slot, part, lt, pl.ds(base + 6 * half + phase, 8, stride=12), :
                        ]
                out[tile, pl.ds(below + 5 * part, 5), :] = rows_ref[
                    slot, part, lt, pl.ds(base + TILE_ROWS, 5), :
                ]

    def two_tiles(index):
        tiles = (2 * index, 2 * index + 1)
        for slot, tile in enumerate(tiles):
            mask_rows(tile, slot)
        for tile in tiles:
            stage1[tile, pl.ds(ROWS1 - 16, 16), :] = jnp.zeros((16, 128), jnp.float32)
            stage2[tile, pl.ds(ROWS2 - 16, 16), :] = jnp.zeros((16, 128), jnp.float32)
        own_columns(tiles)
        for slot, tile in enumerate(tiles):
            spread(tile, slot)
        for tile in tiles:
            for send in sends(tile):
                send.start()

    for index in range(PIECES):
        piece(index).start()
    rows_ref[:, :, :, pl.ds(count, 24), :] = jnp.zeros((2, 2, LANE_TILES, 24, 128), jnp.float32)
    piece(0).wait()

    def step(index, carry):
        piece(index + 1).wait()
        two_tiles(index)
        return carry

    lax.fori_loop(0, PIECES - 1, step, 0)
    two_tiles(PIECES - 1)

    def finish(tile, carry):
        for send in sends(tile):
            send.wait()
        return carry

    lax.fori_loop(0, TILES, finish, 0)


def pack(slc, valid):
    return pl.pallas_call(
        pack_kernel,
        in_specs=[
            pl.BlockSpec(memory_space=pltpu.SMEM),
            pl.BlockSpec(memory_space=pl.ANY),
        ],
        out_specs=[pl.BlockSpec(memory_space=pl.ANY)] * 2,
        out_shape=[
            jax.ShapeDtypeStruct((TILES, ROWS1, 128), jnp.float32),
            jax.ShapeDtypeStruct((TILES, ROWS2, 128), jnp.float32),
        ],
        scratch_shapes=[
            pltpu.VMEM((2, 1536 + 16, COLS), jnp.float32),
            pltpu.VMEM((2, 2, LANE_TILES, TILE_ROWS + 40, 128), jnp.float32),
            pltpu.VMEM((TILES, ROWS1, 128), jnp.float32),
            pltpu.VMEM((TILES, ROWS2, 128), jnp.float32),
            pltpu.SemaphoreType.DMA((PIECES,)),
            pltpu.SemaphoreType.DMA((2, TILES)),
        ],
        compiler_params=pltpu.CompilerParams(vmem_limit_bytes=42 * 1024 * 1024),
        cost_estimate=pl.CostEstimate(flops=10**6, bytes_accessed=2 * 10**7, transcendentals=0),
        name="pack",
    )(valid, slc)


def split(x):
    high = x.astype(jnp.bfloat16)
    return high, (x - high.astype(jnp.float32)).astype(jnp.bfloat16)


def field_of(t, u):
    return t if t == u else DATES + 2 * PAIR_AT[t, u]


def cross_products(data, t_part, u_tile, lanes, rows):
    real = imag = None
    for re_row, im_row in rows:
        a_t = data[re_row, pl.ds(t_part, 1), lanes]
        b_t = data[im_row, pl.ds(t_part, 1), lanes]
        a_u = data[re_row, pl.ds(u_tile * 8, 8), lanes]
        b_u = data[im_row, pl.ds(u_tile * 8, 8), lanes]
        re = a_t * a_u + b_t * b_u
        im = b_t * a_u - a_t * b_u
        real = re if real is None else real + re
        imag = im if imag is None else imag + im
    return real, imag


def dot(a, b):
    return jnp.dot(a, b, preferred_element_type=jnp.float32)


def main_products(msg, sums, lhs, pooled):
    last = lax.broadcasted_iota(jnp.int32, (8, 128), 0) == 7
    state = {"fields": 0, "chunks": 0}

    def load(kind, date, phase, half):
        source = msg if kind in "ab" else sums
        base = 0 if kind in "as" else 96
        return source[date, pl.ds(base + phase * 16 + half * 8, 8), :]

    def emit(field, first, whole):
        out0 = whole[0] + first[1]
        rolled = jnp.where(last, 0.0, pltpu.roll(first[0], 7, 0))
        out1 = whole[1] + rolled
        high, low = split(jnp.concatenate([out0, out1], axis=0))
        lhs[pl.ds(field * 16, 16), 0:128] = high
        lhs[pl.ds(field * 16, 16), 128:256] = low
        state["fields"] += 1

    def drain():
        while (state["chunks"] + 1) * CHUNK <= state["fields"] * 16:
            pooled(state["chunks"])
            state["chunks"] += 1

    for t in range(DATES):
        first, whole = [], []
        for half in range(2):
            total = None
            for phase in range(6):
                a, b = load("a", t, phase, half), load("b", t, phase, half)
                term = a * a + b * b
                if phase == 5:
                    first.append(total)
                total = term if total is None else total + term
            whole.append(total)
        emit(t, first, whole)

    for ts, us in GROUPS:
        pairs = [(t, u) for t in ts for u in us]
        first = {pair: ([], []) for pair in pairs}
        whole = {pair: ([], []) for pair in pairs}
        for half in range(2):
            acc = {}
            for phase in range(6):
                s_t = {t: load("s", t, phase, half) for t in ts}
                a_t = {t: load("a", t, phase, half) for t in ts}
                b_t = {t: load("b", t, phase, half) for t in ts}
                a_u = {u: load("a", u, phase, half) for u in us}
                s_u = {u: load("s", u, phase, half) for u in us}
                d_u = {u: load("d", u, phase, half) for u in us}
                for t, u in pairs:
                    p = a_u[u] * s_t[t]
                    q = d_u[u] * b_t[t]
                    r = s_u[u] * a_t[t]
                    if phase == 0:
                        acc[t, u] = (p, q, r)
                    elif phase < 5:
                        p0, q0, r0 = acc[t, u]
                        acc[t, u] = (p0 + p, q0 + q, r0 + r)
                    else:
                        p0, q0, r0 = acc[t, u]
                        re5, im5 = p0 - q0, p0 - r0
                        first[t, u][0].append(re5)
                        first[t, u][1].append(im5)
                        whole[t, u][0].append(re5 + (p - q))
                        whole[t, u][1].append(im5 + (p - r))
        for pair in pairs:
            for part in range(2):
                emit(field_of(*pair) + part, first[pair][part], whole[pair][part])
        drain()


def dot(a, b):
    return jnp.dot(a, b, preferred_element_type=jnp.float32)


def side_products(small, t, rows, put):
    for u_tile in range(2):
        if u_tile < t // 8:
            values = (jnp.zeros((8, 128), jnp.float32),) * 2
        else:
            values = cross_products(small, t, u_tile, pl.ds(0, 128), rows)
        for part in range(2):
            put(part * 256 + t * 16 + u_tile * 8, values[part])


def fill_sums(msg, sums):
    def fill(date, carry):
        a = msg[date, pl.ds(0, 96), :]
        b = msg[date, pl.ds(96, 96), :]
        sums[date, pl.ds(0, 96), :] = a + b
        sums[date, pl.ds(96, 96), :] = a - b
        return carry

    for date in range(DATES):
        fill(date, 0)


def halo_products(small, side_lhs):
    def put(at, value):
        side_lhs[pl.ds(at, 8), :] = value

    for t in range(DATES):
        side_products(small, t, [(p, 5 + p) for p in range(5)], put)


def pool_side(side_lhs, table):
    high, low = split(side_lhs[...])
    return dot(jnp.concatenate([high, low], axis=1), table)


def chunk_rows(chunk):
    return pl.ds(chunk * CHUNK, CHUNK)


def done_rows(part, date, mt):
    return pl.ds(FIELDS * 8 + ((part * DATES + date) * 2 + mt) * BLOCKS, BLOCKS)


def first_kernel(
    msg, below_msg, table, part_out, sums, lhs, small, side_lhs, res, halo, coh, vec, weight,
    rows, weights,
):
    step = pl.program_id(0)
    weights[...] = table[0].astype(jnp.bfloat16)
    fill_sums(msg, sums)
    for date in range(DATES):
        for row in range(10):
            small[row, date : date + 1, :] = below_msg[date, pl.ds(step * 10 + row, 1), :]

    def pooled(chunk):
        res[step, chunk_rows(chunk), :] = dot(lhs[chunk_rows(chunk), :], weights[...])

    main_products(msg, sums, lhs, pooled)
    halo_products(small, side_lhs)
    halo[step] = pool_side(side_lhs, weights[...])

    @pl.when(step == FIRST - 1)
    def _():
        lane = lax.broadcasted_iota(jnp.int32, (8, 128), 1)
        last = lax.broadcasted_iota(jnp.int32, (8, 128), 0) == 7

        def total(ref, group, at, count):
            value = None
            for lt in range(FIRST):
                if group in FEEDS[lt]:
                    place = FEEDS[lt].index(group) * 128
                    own = ref[lt, pl.ds(at, count), place : place + 128]
                    value = own if value is None else value + own
            return value

        def below(group, t, u, part):
            return total(halo, group, part * 256 + t * 16 + u, 1)

        def paired(group, even, t, u, part):
            at = (field_of(t, u) + part) * 16
            value = jnp.where(even, total(res, group, at, 8), total(res, group, at + 8, 8))
            return value + jnp.where(last & ~even, below(group, t, u, part), 0.0)

        even = (lane < 32) | (lane >= 96)
        for t in range(DATES):
            for u in range(t, DATES):
                for part in range(1 if t == u else 2):
                    at = (field_of(t, u) + part) * 8
                    part_out[pl.ds(at, 8), :] = paired(2, even, t, u, part)

        for half in range(2):

            def cov(t, u, part):
                value = total(res, 0, (field_of(t, u) + part) * 16 + half * 8, 8)
                if half == 1:
                    value = value + jnp.where(last, below(0, t, u, part), 0.0)
                return value

            solve(cov, coh, vec, weight)
            for date in range(DATES):
                for part in range(2):
                    rows[part, date, 0, pl.ds(half, 8, stride=2), :] = vec[part, date]

        even_b = (lane >= 32) & (lane < 96)
        solve(functools.partial(paired, 1, even_b), coh, vec, weight)
        for date in range(DATES):
            for part in range(2):
                value = vec[part, date]
                rows[part, date, 1, pl.ds(0, 8, stride=2), :] = value
                rows[part, date, 1, pl.ds(1, 8, stride=2), :] = pltpu.roll(value, 64, 1)
        left = lax.broadcasted_iota(jnp.int32, (BLOCKS, 128), 1) < 32
        for part in range(2):
            for date in range(DATES):
                one, two = rows[part, date, 0], rows[part, date, 1]
                part_out[done_rows(part, date, 0), :] = one
                part_out[done_rows(part, date, 1), :] = jnp.where(left, one, two)


def last_kernel(
    msg, left, right, table, pool, partial_hbm, out, sums, lhs, small, side_lhs, res, halo,
    pairs, edge, coh, vec, weight, rows, weights, partial, sem,
):
    copy = pltpu.make_async_copy(partial_hbm, partial, sem)
    copy.start()
    fill_sums(msg, sums)
    for date in range(DATES):
        for row in range(10):
            small[row, date : date + 1, :] = msg[date, HALO2 + row : HALO2 + row + 1, :]
        for part in range(2):
            own = OWN_ROW - OWN_TILE + part
            small[10 + part, date : date + 1, :] = left[date, own + 2 : own + 3, :]
            small[12 + part, date : date + 1, :] = right[date, own : own + 1, :]
    halo_products(small, side_lhs)
    weights[...] = table[0].astype(jnp.bfloat16)
    halo[...] = pool_side(side_lhs, weights[...])
    for side in range(2):
        row = 10 + 2 * side

        def put(at, value):
            pairs[pl.ds(2 * at + 1 - side, 8, stride=2), :] = value

        for t in range(DATES):
            side_products(small, t, [(row, row + 1)], put)
    dims = (((1,), (1,)), ((), ()))
    high, low = split(pairs[...])
    pool2 = pool[...].astype(jnp.bfloat16)
    sides = lax.dot_general(
        pool2, high, dims, preferred_element_type=jnp.float32
    ) + lax.dot_general(pool2, low, dims, preferred_element_type=jnp.float32)
    lower = lax.broadcasted_iota(jnp.int32, (8, 128), 1) < 64
    for group in range(SIDE // 64):
        tile = slice(group * 128, group * 128 + 128)
        even_rows, odd_rows = sides[0:8, tile], sides[8:16, tile]
        edge[2 * group] = jnp.where(lower, even_rows, pltpu.roll(odd_rows, 64, 1))
        edge[2 * group + 1] = jnp.where(lower, pltpu.roll(even_rows, 64, 1), odd_rows)

    def pooled(chunk):
        res[chunk_rows(chunk), :] = dot(lhs[chunk_rows(chunk), :], weights[...])

    main_products(msg, sums, lhs, pooled)

    lane = lax.broadcasted_iota(jnp.int32, (8, 128), 1)
    last = lax.broadcasted_iota(jnp.int32, (8, 128), 0) == 7
    even = (lane < 32) | (lane >= 96)
    beside = (lane == 0) | (lane == 127) | (lane == 63) | (lane == 64)
    copy.wait()

    def cov(t, u, part):
        field = field_of(t, u) + part
        at = field * 16
        value = jnp.where(even, res[pl.ds(at, 8), :], res[pl.ds(at + 8, 8), :])
        index = part * 256 + t * 16 + u
        value = value + jnp.where(last & ~even, halo[pl.ds(index, 1), :], 0.0)
        turned = pltpu.roll(edge[index // 32], (127 - 2 * (index % 32)) % 128, 1)
        return value + partial[pl.ds(field * 8, 8), :] + jnp.where(beside, turned, 0.0)

    solve(cov, coh, vec, weight)
    for date in range(DATES):
        for part in range(2):
            value = vec[part, date]
            rows[part, date, 0, pl.ds(0, 8, stride=2), :] = value
            rows[part, date, 0, pl.ds(1, 8, stride=2), :] = pltpu.roll(value, 64, 1)
    place = lax.broadcasted_iota(jnp.int32, (BLOCKS, 128), 1)
    for part in range(2):
        for date in range(DATES):
            own = rows[part, date, 0]
            for mt, mine in ((0, place < 32), (1, place >= 96)):
                out[part, date, :, mt * 128 : mt * 128 + 128] = jnp.where(
                    mine, own, partial[done_rows(part, date, mt), :]
                )


def inverse_norm(vec):
    terms = [vec[part, t] * vec[part, t] for t in range(DATES) for part in range(2)]
    while len(terms) > 1:
        terms = [terms[i] + terms[i + 1] for i in range(0, len(terms), 2)]
    return lax.rsqrt(terms[0])


def solve(cov, coh, vec, weight):
    inv = []
    for t in range(DATES):
        diag = cov(t, t, 0)
        root = lax.rsqrt(jnp.maximum(diag, FLOOR))
        inv.append(root)
        weight[t] = diag * (root * root) + 1.0
    row_real = [weight[t] for t in range(DATES)]
    row_imag = [None] * DATES
    for i, (t, u) in enumerate(PAIRS):
        factor = inv[t] * inv[u]
        real = cov(t, u, 0) * factor
        imag = cov(t, u, 1) * factor
        coh[i, 0] = real
        coh[i, 1] = real + imag
        coh[i, 2] = imag - real
        row_real[t] = row_real[t] + real
        row_real[u] = row_real[u] + real
        row_imag[t] = imag if row_imag[t] is None else row_imag[t] + imag
        row_imag[u] = -imag if row_imag[u] is None else row_imag[u] - imag
    for t in range(DATES):
        real, imag = 0.25 * row_real[t], 0.25 * row_imag[t]
        vec[0, t] = real
        vec[1, t] = imag
        vec[2, t] = real + imag

    def iterate(_, carry):
        scale = inverse_norm(vec)
        new_real, new_imag = [None] * DATES, [None] * DATES
        sums = [[None, None, None] for _ in range(DATES)]

        def add(t, which, value, minus=False):
            if sums[t][which] is None:
                sums[t][which] = -value if minus else value
            elif minus:
                sums[t][which] = sums[t][which] - value
            else:
                sums[t][which] = sums[t][which] + value

        def pair(t, u, v):
            i = PAIR_AT[t, u]
            real, plus, minus = coh[i, 0], coh[i, 1], coh[i, 2]
            add(t, 0, real * v[u][2])
            add(t, 1, plus * v[u][1])
            add(t, 2, minus * v[u][0])
            add(u, 0, real * v[t][2])
            add(u, 1, minus * v[t][1], True)
            add(u, 2, plus * v[t][0], True)

        for first in range(0, DATES, 4):
            for second in range(first, DATES, 4):
                dates = sorted(set(range(first, first + 4)) | set(range(second, second + 4)))
                v = {t: (vec[0, t], vec[1, t], vec[2, t]) for t in dates}
                for t in range(first, first + 4):
                    for u in range(second, second + 4):
                        if t < u:
                            pair(t, u, v)
        for t in range(DATES):
            own = weight[t]
            new_real[t] = (sums[t][0] - sums[t][1]) + own * vec[0, t]
            new_imag[t] = (sums[t][0] + sums[t][2]) + own * vec[1, t]
        for t in range(DATES):
            real, imag = new_real[t] * scale, new_imag[t] * scale
            vec[0, t] = real
            vec[1, t] = imag
            vec[2, t] = real + imag
        return carry

    lax.fori_loop(0, ITERS - 1, iterate, 0, unroll=3)
    scale = inverse_norm(vec)
    for t in range(DATES):
        for part in range(2):
            vec[part, t] = vec[part, t] * scale


def whole(*shape):
    return pl.BlockSpec(shape, lambda i: (0,) * len(shape))


def common_scratch(small_rows):
    return [
        pltpu.VMEM((DATES, TILE_LANES, 128), jnp.float32),
        pltpu.VMEM((FIELDS * 16, 256), jnp.bfloat16),
        pltpu.VMEM((small_rows, DATES, 128), jnp.float32),
        pltpu.VMEM((SIDE, 128), jnp.float32),
    ]


SOLVE_SCRATCH = [
    pltpu.VMEM((len(PAIRS), 3, 8, 128), jnp.float32),
    pltpu.VMEM((3, DATES, 8, 128), jnp.float32),
    pltpu.VMEM((DATES, 8, 128), jnp.float32),
]
LINKED = (2, DATES, BLOCKS, OUT_COLS)
PARTIAL = (FIELDS * 8 + 2 * DATES * 2 * BLOCKS, 128)


def cut_kernel(in_ref, out_ref, sem):
    copy = pltpu.make_async_copy(in_ref.at[:, pl.ds(OWN_TILE, 8), :], out_ref, sem)
    copy.start()
    copy.wait()


def cut_columns(message):
    return pl.pallas_call(
        cut_kernel,
        in_specs=[pl.BlockSpec(memory_space=pl.ANY)],
        out_specs=pl.BlockSpec(memory_space=pl.ANY),
        out_shape=jax.ShapeDtypeStruct((DATES, 8, 128), jnp.float32),
        scratch_shapes=[pltpu.SemaphoreType.DMA],
        compiler_params=pltpu.CompilerParams(vmem_limit_bytes=GRANT),
        name="cut_columns",
    )(message)


def link_first(message, tables):
    return pl.pallas_call(
        first_kernel,
        grid=(FIRST,),
        in_specs=[
            pl.BlockSpec((DATES, TILE_LANES, 128), lambda i: (0, i, 0)),
            pl.BlockSpec((DATES, 64, 128), lambda i: (0, HALO1 // 64, 0)),
            pl.BlockSpec((1, 256, 256), lambda i: (i, 0, 0)),
        ],
        out_specs=whole(*PARTIAL),
        out_shape=jax.ShapeDtypeStruct(PARTIAL, jnp.float32),
        scratch_shapes=common_scratch(10)
        + [
            pltpu.VMEM((FIRST, FIELDS * 16, 256), jnp.float32),
            pltpu.VMEM((FIRST, SIDE, 256), jnp.float32),
        ]
        + SOLVE_SCRATCH
        + [pltpu.VMEM((2, DATES, 2, BLOCKS, 128), jnp.float32), pltpu.VMEM((256, 256), jnp.bfloat16)],
        compiler_params=pltpu.CompilerParams(vmem_limit_bytes=GRANT),
        cost_estimate=pl.CostEstimate(flops=10**9, bytes_accessed=10**7, transcendentals=0),
        name="link_first",
    )(message, message, tables)


def link_last(message, left, right, tables, pool, partial):
    return pl.pallas_call(
        last_kernel,
        grid=(1,),
        in_specs=[
            whole(DATES, ROWS2, 128),
            whole(DATES, 8, 128),
            whole(DATES, 8, 128),
            whole(1, 256, 128),
            whole(16, 128),
            pl.BlockSpec(memory_space=pl.ANY),
        ],
        out_specs=whole(*LINKED),
        out_shape=jax.ShapeDtypeStruct(LINKED, jnp.float32),
        scratch_shapes=common_scratch(14)
        + [
            pltpu.VMEM((FIELDS * 16, 128), jnp.float32),
            pltpu.VMEM((SIDE, 128), jnp.float32),
            pltpu.VMEM((2 * SIDE, 128), jnp.float32),
            pltpu.VMEM((SIDE // 32, 8, 128), jnp.float32),
        ]
        + SOLVE_SCRATCH
        + [
            pltpu.VMEM((2, DATES, 1, BLOCKS, 128), jnp.float32),
            pltpu.VMEM((256, 128), jnp.bfloat16),
            pltpu.VMEM(PARTIAL, jnp.float32),
            pltpu.SemaphoreType.DMA,
        ],
        compiler_params=pltpu.CompilerParams(vmem_limit_bytes=24 * 1024 * 1024),
        cost_estimate=pl.CostEstimate(flops=10**8, bytes_accessed=10**7, transcendentals=0),
        name="link_last",
    )(message, left, right, tables, pool, partial)


def local(slc, valid_rows):
    valid = valid_rows.T
    size = lax.axis_size("col")
    up = [(i, i + 1) for i in range(size - 1)]
    down = [(i + 1, i) for i in range(size - 1)]
    message1, message2 = pack(slc, valid)
    received1 = lax.all_to_all(message1, "row", 0, 0, tiled=True)
    received1, message2 = lax.optimization_barrier((received1, message2))
    received2 = lax.all_to_all(message2, "row", 0, 0, tiled=True)
    own = cut_columns(received1)
    left = lax.ppermute(own, "col", up)
    right = lax.ppermute(own, "col", down)
    tables, pool = column_tables()
    last_table = jnp.asarray(tables[FIRST:, :, 0:128])
    partial = link_first(received1, jnp.asarray(tables))
    return link_last(received2, left, right, last_table, jnp.asarray(pool), partial)


def solution(mesh):
    return jax.shard_map(
        local,
        mesh=mesh,
        in_specs=(P(None, "row", None, "col"), P()),
        out_specs=P(None, None, "row", "col"),
        check_vma=False,
    )
```

```python
import functools

import jax
import jax.numpy as jnp
import numpy as np
from jax import lax
from jax.experimental import pallas as pl
from jax.experimental.pallas import tpu as pltpu
from jax.sharding import PartitionSpec as P

ITERS = 10
FLOOR = 20.0
DATES = 16
TILES = 16
COLS = 768
LANE_TILES = 6
FIRST = 5
OUT_COLS = 256
BLOCKS = 16
TILE_ROWS = 6 * BLOCKS
TILE_LANES = 192
ROWS1 = 1024
HALO1 = FIRST * TILE_LANES
OWN_TILE = 1008
OWN_ROW = 1010
ROWS2 = 208
HALO2 = TILE_LANES
WINDOW = TILE_ROWS + 5
PIECES = 8
PIECE_ROWS = 192
GRANT = 60 * 1024 * 1024


def pair_groups():
    groups = []
    for i in range(0, DATES, 2):
        groups.append(([i], [i + 1]))
        rest = list(range(i + 2, DATES))
        for j in range(0, len(rest), 4):
            groups.append(([i, i + 1], rest[j : j + 4]))
    return groups


GROUPS = pair_groups()
PAIRS = [(t, u) for ts, us in GROUPS for t in ts for u in us]
PAIR_AT = {pair: i for i, pair in enumerate(PAIRS)}
FIELDS = DATES + 2 * len(PAIRS)
CHUNK = 512
SIDE = 512
FEEDS = ((0, 2), (0,), (0,), (0, 1), (1, 2), (2,))


def lane_columns():
    lane = np.arange(128)
    group_a = np.where(lane < 32, 128 + lane, lane)
    group_b = np.where((lane >= 32) & (lane < 96), 128 + lane, 128 + (lane + 64) % 128)
    own = np.where(lane < 32, lane, 128 + lane)
    other = (lane + 64) % 128
    far = np.where(other < 32, other, 128 + other)
    group_c = np.where((lane < 32) | (lane >= 96), own, far)
    return group_a, group_b, group_c


def column_tables():
    groups = lane_columns()
    tables = np.zeros((LANE_TILES, 256, 256), np.float32)
    for lt in range(LANE_TILES):
        column = (lt * 128 + np.arange(128) + 64) % COLS
        for place, group in enumerate(FEEDS[lt]):
            target = 3 * groups[group][None, :]
            inside = (column[:, None] >= target - 1) & (column[:, None] <= target + 3)
            for copy in range(2):
                tables[lt, copy * 128 : copy * 128 + 128, place * 128 : place * 128 + 128] = inside
    row = np.arange(128)
    pool = np.zeros((2, 8, 128), np.float32)
    for half in range(2):
        for s in range(8):
            block = 2 * s + half
            pool[half, s] = (row >= 6 * block) & (row <= 6 * block + 10)
    return tables, pool.reshape(16, 128)


def pack_kernel(valid_ref, slc, out1, out2, taken, rows_ref, stage1, stage2, in_sems, out_sems):
    me = lax.axis_index("row")
    low, high = valid_ref[0, me], valid_ref[1, me]
    lane = lax.broadcasted_iota(jnp.int32, (8, 128), 1)
    row = lax.broadcasted_iota(jnp.int32, (8, 128), 0)
    pick = jnp.where(((row == 0) & (lane == 64)) | ((row == 1) & (lane == 63)), 1.0, 0.0)
    count = TILE_ROWS + 16

    def piece(index):
        return pltpu.make_async_copy(
            slc.at[:, 0, pl.ds(index * PIECE_ROWS, PIECE_ROWS), :],
            taken.at[:, pl.ds(index * PIECE_ROWS + 8, PIECE_ROWS), :],
            in_sems.at[index],
        )

    def sends(tile):
        return (
            pltpu.make_async_copy(stage1.at[tile], out1.at[tile], out_sems.at[0, tile]),
            pltpu.make_async_copy(stage2.at[tile], out2.at[tile], out_sems.at[1, tile]),
        )

    def mask_rows(tile, slot):
        start = pl.multiple_of(tile * TILE_ROWS, 8)
        at_row = lax.broadcasted_iota(jnp.int32, (count, 128), 0) + (start - 8)
        keep = (at_row >= low) & (at_row < high)
        left = lax.broadcasted_iota(jnp.int32, (count, 128), 1) < 64
        for part in range(2):
            turned = []
            for lt in range(LANE_TILES):
                value = taken[part, pl.ds(start, count), lt * 128 : lt * 128 + 128]
                turned.append(pltpu.roll(jnp.where(keep, value, 0.0), 64, 1))
            for lt in range(LANE_TILES):
                rows_ref[slot, part, lt, 0:count, :] = jnp.where(
                    left, turned[lt], turned[(lt + 1) % LANE_TILES]
                )

    def own_columns(tiles):
        blocks = [
            rows_ref[slot, part, LANE_TILES - 1, pl.ds(5, 128), :]
            for slot in range(2)
            for part in range(2)
        ]
        rest = jnp.concatenate(blocks, axis=0)
        columns = None
        for _ in range(3):
            piece_of = rest.astype(jnp.bfloat16)
            rest = rest - piece_of.astype(jnp.float32)
            term = lax.dot_general(
                pick.astype(jnp.bfloat16), piece_of, (((1,), (1,)), ((), ())),
                preferred_element_type=jnp.float32,
            )
            columns = term if columns is None else columns + term
        for slot, tile in enumerate(tiles):
            for part in range(2):
                at = (2 * slot + part) * 128
                value = jnp.where(lane < WINDOW + 1, columns[:, at : at + 128], 0.0)
                for side in range(2):
                    row_at = pl.ds(OWN_ROW + 2 * side + part, 1)
                    stage1[tile, row_at, :] = value[side : side + 1]

    def spread(tile, slot):
        base = 5
        for lt in range(LANE_TILES):
            out = stage1 if lt < FIRST else stage2
            top = lt * TILE_LANES if lt < FIRST else 0
            below = HALO1 + lt * 10 if lt < FIRST else HALO2
            for part in range(2):
                for phase in range(6):
                    for half in range(2):
                        at = top + part * 96 + phase * 16 + half * 8
                        out[tile, pl.ds(at, 8), :] = rows_ref[
                            slot, part, lt, pl.ds(base + 6 * half + phase, 8, stride=12), :
                        ]
                out[tile, pl.ds(below + 5 * part, 5), :] = rows_ref[
                    slot, part, lt, pl.ds(base + TILE_ROWS, 5), :
                ]

    def two_tiles(index):
        tiles = (2 * index, 2 * index + 1)
        for slot, tile in enumerate(tiles):
            mask_rows(tile, slot)
        for tile in tiles:
            stage1[tile, pl.ds(ROWS1 - 16, 16), :] = jnp.zeros((16, 128), jnp.float32)
            stage2[tile, pl.ds(ROWS2 - 16, 16), :] = jnp.zeros((16, 128), jnp.float32)
        own_columns(tiles)
        for slot, tile in enumerate(tiles):
            spread(tile, slot)
        for tile in tiles:
            for send in sends(tile):
                send.start()

    for index in range(PIECES):
        piece(index).start()
    rows_ref[:, :, :, pl.ds(count, 24), :] = jnp.zeros((2, 2, LANE_TILES, 24, 128), jnp.float32)
    piece(0).wait()

    def step(index, carry):
        piece(index + 1).wait()
        two_tiles(index)
        return carry

    lax.fori_loop(0, PIECES - 1, step, 0)
    two_tiles(PIECES - 1)

    def finish(tile, carry):
        for send in sends(tile):
            send.wait()
        return carry

    lax.fori_loop(0, TILES, finish, 0)


def pack(slc, valid):
    return pl.pallas_call(
        pack_kernel,
        in_specs=[
            pl.BlockSpec(memory_space=pltpu.SMEM),
            pl.BlockSpec(memory_space=pl.ANY),
        ],
        out_specs=[pl.BlockSpec(memory_space=pl.ANY)] * 2,
        out_shape=[
            jax.ShapeDtypeStruct((TILES, ROWS1, 128), jnp.float32),
            jax.ShapeDtypeStruct((TILES, ROWS2, 128), jnp.float32),
        ],
        scratch_shapes=[
            pltpu.VMEM((2, 1536 + 16, COLS), jnp.float32),
            pltpu.VMEM((2, 2, LANE_TILES, TILE_ROWS + 40, 128), jnp.float32),
            pltpu.VMEM((TILES, ROWS1, 128), jnp.float32),
            pltpu.VMEM((TILES, ROWS2, 128), jnp.float32),
            pltpu.SemaphoreType.DMA((PIECES,)),
            pltpu.SemaphoreType.DMA((2, TILES)),
        ],
        compiler_params=pltpu.CompilerParams(vmem_limit_bytes=GRANT),
        cost_estimate=pl.CostEstimate(flops=10**6, bytes_accessed=2 * 10**7, transcendentals=0),
        name="pack",
    )(valid, slc)


def split(x):
    high = x.astype(jnp.bfloat16)
    return high, (x - high.astype(jnp.float32)).astype(jnp.bfloat16)


def field_of(t, u):
    return t if t == u else DATES + 2 * PAIR_AT[t, u]


def cross_products(data, t_part, u_tile, lanes, rows):
    real = imag = None
    for re_row, im_row in rows:
        a_t = data[re_row, pl.ds(t_part, 1), lanes]
        b_t = data[im_row, pl.ds(t_part, 1), lanes]
        a_u = data[re_row, pl.ds(u_tile * 8, 8), lanes]
        b_u = data[im_row, pl.ds(u_tile * 8, 8), lanes]
        re = a_t * a_u + b_t * b_u
        im = b_t * a_u - a_t * b_u
        real = re if real is None else real + re
        imag = im if imag is None else imag + im
    return real, imag


def dot(a, b):
    return jnp.dot(a, b, preferred_element_type=jnp.float32)


def main_products(msg, sums, lhs, pooled):
    last = lax.broadcasted_iota(jnp.int32, (8, 128), 0) == 7
    state = {"fields": 0, "chunks": 0}

    def load(kind, date, phase, half):
        source = msg if kind in "ab" else sums
        base = 0 if kind in "as" else 96
        return source[date, pl.ds(base + phase * 16 + half * 8, 8), :]

    def emit(field, first, whole):
        out0 = whole[0] + first[1]
        rolled = jnp.where(last, 0.0, pltpu.roll(first[0], 7, 0))
        out1 = whole[1] + rolled
        high, low = split(jnp.concatenate([out0, out1], axis=0))
        lhs[pl.ds(field * 16, 16), 0:128] = high
        lhs[pl.ds(field * 16, 16), 128:256] = low
        state["fields"] += 1

    def drain():
        while (state["chunks"] + 1) * CHUNK <= state["fields"] * 16:
            pooled(state["chunks"])
            state["chunks"] += 1

    for t in range(DATES):
        first, whole = [], []
        for half in range(2):
            total = None
            for phase in range(6):
                a, b = load("a", t, phase, half), load("b", t, phase, half)
                term = a * a + b * b
                if phase == 5:
                    first.append(total)
                total = term if total is None else total + term
            whole.append(total)
        emit(t, first, whole)

    for ts, us in GROUPS:
        pairs = [(t, u) for t in ts for u in us]
        first = {pair: ([], []) for pair in pairs}
        whole = {pair: ([], []) for pair in pairs}
        for half in range(2):
            acc = {}
            for phase in range(6):
                s_t = {t: load("s", t, phase, half) for t in ts}
                a_t = {t: load("a", t, phase, half) for t in ts}
                b_t = {t: load("b", t, phase, half) for t in ts}
                a_u = {u: load("a", u, phase, half) for u in us}
                s_u = {u: load("s", u, phase, half) for u in us}
                d_u = {u: load("d", u, phase, half) for u in us}
                for t, u in pairs:
                    p = a_u[u] * s_t[t]
                    q = d_u[u] * b_t[t]
                    r = s_u[u] * a_t[t]
                    if phase == 0:
                        acc[t, u] = (p, q, r)
                    elif phase < 5:
                        p0, q0, r0 = acc[t, u]
                        acc[t, u] = (p0 + p, q0 + q, r0 + r)
                    else:
                        p0, q0, r0 = acc[t, u]
                        re5, im5 = p0 - q0, p0 - r0
                        first[t, u][0].append(re5)
                        first[t, u][1].append(im5)
                        whole[t, u][0].append(re5 + (p - q))
                        whole[t, u][1].append(im5 + (p - r))
        for pair in pairs:
            for part in range(2):
                emit(field_of(*pair) + part, first[pair][part], whole[pair][part])
        drain()


def dot(a, b):
    return jnp.dot(a, b, preferred_element_type=jnp.float32)


def side_products(small, t, rows, put):
    for u_tile in range(2):
        if u_tile < t // 8:
            values = (jnp.zeros((8, 128), jnp.float32),) * 2
        else:
            values = cross_products(small, t, u_tile, pl.ds(0, 128), rows)
        for part in range(2):
            put(part * 256 + t * 16 + u_tile * 8, values[part])


def fill_sums(msg, sums):
    def fill(date, carry):
        a = msg[date, pl.ds(0, 96), :]
        b = msg[date, pl.ds(96, 96), :]
        sums[date, pl.ds(0, 96), :] = a + b
        sums[date, pl.ds(96, 96), :] = a - b
        return carry

    for date in range(DATES):
        fill(date, 0)


def halo_products(small, side_lhs):
    def put(at, value):
        side_lhs[pl.ds(at, 8), :] = value

    for t in range(DATES):
        side_products(small, t, [(p, 5 + p) for p in range(5)], put)


def pool_side(side_lhs, table):
    high, low = split(side_lhs[...])
    return dot(jnp.concatenate([high, low], axis=1), table)


def chunk_rows(chunk):
    return pl.ds(chunk * CHUNK, CHUNK)


def done_rows(part, date, mt):
    return pl.ds(FIELDS * 8 + ((part * DATES + date) * 2 + mt) * BLOCKS, BLOCKS)


def first_kernel(
    msg, below_msg, table, part_out, sums, lhs, small, side_lhs, res, halo, coh, vec, weight,
    rows, weights,
):
    step = pl.program_id(0)
    weights[...] = table[0].astype(jnp.bfloat16)
    fill_sums(msg, sums)
    for date in range(DATES):
        for row in range(10):
            small[row, date : date + 1, :] = below_msg[date, pl.ds(step * 10 + row, 1), :]

    def pooled(chunk):
        res[step, chunk_rows(chunk), :] = dot(lhs[chunk_rows(chunk), :], weights[...])

    main_products(msg, sums, lhs, pooled)
    halo_products(small, side_lhs)
    halo[step] = pool_side(side_lhs, weights[...])

    @pl.when(step == FIRST - 1)
    def _():
        lane = lax.broadcasted_iota(jnp.int32, (8, 128), 1)
        last = lax.broadcasted_iota(jnp.int32, (8, 128), 0) == 7

        def total(ref, group, at, count):
            value = None
            for lt in range(FIRST):
                if group in FEEDS[lt]:
                    place = FEEDS[lt].index(group) * 128
                    own = ref[lt, pl.ds(at, count), place : place + 128]
                    value = own if value is None else value + own
            return value

        def below(group, t, u, part):
            return total(halo, group, part * 256 + t * 16 + u, 1)

        def paired(group, even, t, u, part):
            at = (field_of(t, u) + part) * 16
            value = jnp.where(even, total(res, group, at, 8), total(res, group, at + 8, 8))
            return value + jnp.where(last & ~even, below(group, t, u, part), 0.0)

        even = (lane < 32) | (lane >= 96)
        for t in range(DATES):
            for u in range(t, DATES):
                for part in range(1 if t == u else 2):
                    at = (field_of(t, u) + part) * 8
                    part_out[pl.ds(at, 8), :] = paired(2, even, t, u, part)

        for half in range(2):

            def cov(t, u, part):
                value = total(res, 0, (field_of(t, u) + part) * 16 + half * 8, 8)
                if half == 1:
                    value = value + jnp.where(last, below(0, t, u, part), 0.0)
                return value

            solve(cov, coh, vec, weight)
            for date in range(DATES):
                for part in range(2):
                    rows[part, date, 0, pl.ds(half, 8, stride=2), :] = vec[part, date]

        even_b = (lane >= 32) & (lane < 96)
        solve(functools.partial(paired, 1, even_b), coh, vec, weight)
        for date in range(DATES):
            for part in range(2):
                value = vec[part, date]
                rows[part, date, 1, pl.ds(0, 8, stride=2), :] = value
                rows[part, date, 1, pl.ds(1, 8, stride=2), :] = pltpu.roll(value, 64, 1)
        left = lax.broadcasted_iota(jnp.int32, (BLOCKS, 128), 1) < 32
        for part in range(2):
            for date in range(DATES):
                one, two = rows[part, date, 0], rows[part, date, 1]
                part_out[done_rows(part, date, 0), :] = one
                part_out[done_rows(part, date, 1), :] = jnp.where(left, one, two)


def last_kernel(
    msg, left, right, table, pool, partial_hbm, out, sums, lhs, small, side_lhs, res, halo,
    pairs, edge, coh, vec, weight, rows, weights, partial, sem,
):
    copy = pltpu.make_async_copy(partial_hbm, partial, sem)
    copy.start()
    fill_sums(msg, sums)
    for date in range(DATES):
        for row in range(10):
            small[row, date : date + 1, :] = msg[date, HALO2 + row : HALO2 + row + 1, :]
        for part in range(2):
            own = OWN_ROW - OWN_TILE + part
            small[10 + part, date : date + 1, :] = left[date, own + 2 : own + 3, :]
            small[12 + part, date : date + 1, :] = right[date, own : own + 1, :]
    halo_products(small, side_lhs)
    weights[...] = table[0].astype(jnp.bfloat16)
    halo[...] = pool_side(side_lhs, weights[...])
    for side in range(2):
        row = 10 + 2 * side

        def put(at, value):
            pairs[pl.ds(2 * at + 1 - side, 8, stride=2), :] = value

        for t in range(DATES):
            side_products(small, t, [(row, row + 1)], put)
    dims = (((1,), (1,)), ((), ()))
    high, low = split(pairs[...])
    pool2 = pool[...].astype(jnp.bfloat16)
    sides = lax.dot_general(
        pool2, high, dims, preferred_element_type=jnp.float32
    ) + lax.dot_general(pool2, low, dims, preferred_element_type=jnp.float32)
    lower = lax.broadcasted_iota(jnp.int32, (8, 128), 1) < 64
    for group in range(SIDE // 64):
        tile = slice(group * 128, group * 128 + 128)
        even_rows, odd_rows = sides[0:8, tile], sides[8:16, tile]
        edge[2 * group] = jnp.where(lower, even_rows, pltpu.roll(odd_rows, 64, 1))
        edge[2 * group + 1] = jnp.where(lower, pltpu.roll(even_rows, 64, 1), odd_rows)

    def pooled(chunk):
        res[chunk_rows(chunk), :] = dot(lhs[chunk_rows(chunk), :], weights[...])

    main_products(msg, sums, lhs, pooled)

    lane = lax.broadcasted_iota(jnp.int32, (8, 128), 1)
    last = lax.broadcasted_iota(jnp.int32, (8, 128), 0) == 7
    even = (lane < 32) | (lane >= 96)
    beside = (lane == 0) | (lane == 127) | (lane == 63) | (lane == 64)
    copy.wait()

    def cov(t, u, part):
        field = field_of(t, u) + part
        at = field * 16
        value = jnp.where(even, res[pl.ds(at, 8), :], res[pl.ds(at + 8, 8), :])
        index = part * 256 + t * 16 + u
        value = value + jnp.where(last & ~even, halo[pl.ds(index, 1), :], 0.0)
        turned = pltpu.roll(edge[index // 32], (127 - 2 * (index % 32)) % 128, 1)
        return value + partial[pl.ds(field * 8, 8), :] + jnp.where(beside, turned, 0.0)

    solve(cov, coh, vec, weight)
    for date in range(DATES):
        for part in range(2):
            value = vec[part, date]
            rows[part, date, 0, pl.ds(0, 8, stride=2), :] = value
            rows[part, date, 0, pl.ds(1, 8, stride=2), :] = pltpu.roll(value, 64, 1)
    place = lax.broadcasted_iota(jnp.int32, (BLOCKS, 128), 1)
    for part in range(2):
        for date in range(DATES):
            own = rows[part, date, 0]
            for mt, mine in ((0, place < 32), (1, place >= 96)):
                out[part, date, :, mt * 128 : mt * 128 + 128] = jnp.where(
                    mine, own, partial[done_rows(part, date, mt), :]
                )


def inverse_norm(vec):
    terms = [vec[part, t] * vec[part, t] for t in range(DATES) for part in range(2)]
    while len(terms) > 1:
        terms = [terms[i] + terms[i + 1] for i in range(0, len(terms), 2)]
    return lax.rsqrt(terms[0])


def solve(cov, coh, vec, weight):
    inv = []
    for t in range(DATES):
        diag = cov(t, t, 0)
        root = lax.rsqrt(jnp.maximum(diag, FLOOR))
        inv.append(root)
        weight[t] = diag * (root * root) + 1.0
    row_real = [weight[t] for t in range(DATES)]
    row_imag = [None] * DATES
    for i, (t, u) in enumerate(PAIRS):
        factor = inv[t] * inv[u]
        real = cov(t, u, 0) * factor
        imag = cov(t, u, 1) * factor
        coh[i, 0] = real
        coh[i, 1] = real + imag
        coh[i, 2] = imag - real
        row_real[t] = row_real[t] + real
        row_real[u] = row_real[u] + real
        row_imag[t] = imag if row_imag[t] is None else row_imag[t] + imag
        row_imag[u] = -imag if row_imag[u] is None else row_imag[u] - imag
    for t in range(DATES):
        real, imag = 0.25 * row_real[t], 0.25 * row_imag[t]
        vec[0, t] = real
        vec[1, t] = imag
        vec[2, t] = real + imag

    def iterate(_, carry):
        scale = inverse_norm(vec)
        new_real, new_imag = [None] * DATES, [None] * DATES
        sums = [[None, None, None] for _ in range(DATES)]

        def add(t, which, value, minus=False):
            if sums[t][which] is None:
                sums[t][which] = -value if minus else value
            elif minus:
                sums[t][which] = sums[t][which] - value
            else:
                sums[t][which] = sums[t][which] + value

        def pair(t, u, v):
            i = PAIR_AT[t, u]
            real, plus, minus = coh[i, 0], coh[i, 1], coh[i, 2]
            add(t, 0, real * v[u][2])
            add(t, 1, plus * v[u][1])
            add(t, 2, minus * v[u][0])
            add(u, 0, real * v[t][2])
            add(u, 1, minus * v[t][1], True)
            add(u, 2, plus * v[t][0], True)

        for first in range(0, DATES, 4):
            for second in range(first, DATES, 4):
                dates = sorted(set(range(first, first + 4)) | set(range(second, second + 4)))
                v = {t: (vec[0, t], vec[1, t], vec[2, t]) for t in dates}
                for t in range(first, first + 4):
                    for u in range(second, second + 4):
                        if t < u:
                            pair(t, u, v)
        for t in range(DATES):
            own = weight[t]
            new_real[t] = (sums[t][0] - sums[t][1]) + own * vec[0, t]
            new_imag[t] = (sums[t][0] + sums[t][2]) + own * vec[1, t]
        for t in range(DATES):
            real, imag = new_real[t] * scale, new_imag[t] * scale
            vec[0, t] = real
            vec[1, t] = imag
            vec[2, t] = real + imag
        return carry

    lax.fori_loop(0, ITERS - 1, iterate, 0, unroll=3)
    scale = inverse_norm(vec)
    for t in range(DATES):
        for part in range(2):
            vec[part, t] = vec[part, t] * scale


def whole(*shape):
    return pl.BlockSpec(shape, lambda i: (0,) * len(shape))


def common_scratch(small_rows):
    return [
        pltpu.VMEM((DATES, TILE_LANES, 128), jnp.float32),
        pltpu.VMEM((FIELDS * 16, 256), jnp.bfloat16),
        pltpu.VMEM((small_rows, DATES, 128), jnp.float32),
        pltpu.VMEM((SIDE, 128), jnp.float32),
    ]


SOLVE_SCRATCH = [
    pltpu.VMEM((len(PAIRS), 3, 8, 128), jnp.float32),
    pltpu.VMEM((3, DATES, 8, 128), jnp.float32),
    pltpu.VMEM((DATES, 8, 128), jnp.float32),
]
LINKED = (2, DATES, BLOCKS, OUT_COLS)
PARTIAL = (FIELDS * 8 + 2 * DATES * 2 * BLOCKS, 128)


def cut_kernel(in_ref, out_ref):
    out_ref[...] = in_ref[...]


def cut_columns(message):
    return pl.pallas_call(
        cut_kernel,
        grid=(1,),
        in_specs=[pl.BlockSpec((DATES, 8, 128), lambda i: (0, OWN_TILE // 8, 0))],
        out_specs=whole(DATES, 8, 128),
        out_shape=jax.ShapeDtypeStruct((DATES, 8, 128), jnp.float32),
        compiler_params=pltpu.CompilerParams(vmem_limit_bytes=GRANT),
        name="cut_columns",
    )(message)


def link_first(message, tables):
    return pl.pallas_call(
        first_kernel,
        grid=(FIRST,),
        in_specs=[
            pl.BlockSpec((DATES, TILE_LANES, 128), lambda i: (0, i, 0)),
            pl.BlockSpec((DATES, 64, 128), lambda i: (0, HALO1 // 64, 0)),
            pl.BlockSpec((1, 256, 256), lambda i: (i, 0, 0)),
        ],
        out_specs=whole(*PARTIAL),
        out_shape=jax.ShapeDtypeStruct(PARTIAL, jnp.float32),
        scratch_shapes=common_scratch(10)
        + [
            pltpu.VMEM((FIRST, FIELDS * 16, 256), jnp.float32),
            pltpu.VMEM((FIRST, SIDE, 256), jnp.float32),
        ]
        + SOLVE_SCRATCH
        + [pltpu.VMEM((2, DATES, 2, BLOCKS, 128), jnp.float32), pltpu.VMEM((256, 256), jnp.bfloat16)],
        compiler_params=pltpu.CompilerParams(vmem_limit_bytes=GRANT),
        cost_estimate=pl.CostEstimate(flops=10**9, bytes_accessed=10**7, transcendentals=0),
        name="link_first",
    )(message, message, tables)


def link_last(message, left, right, tables, pool, partial):
    return pl.pallas_call(
        last_kernel,
        grid=(1,),
        in_specs=[
            whole(DATES, ROWS2, 128),
            whole(DATES, 8, 128),
            whole(DATES, 8, 128),
            whole(1, 256, 128),
            whole(16, 128),
            pl.BlockSpec(memory_space=pl.ANY),
        ],
        out_specs=whole(*LINKED),
        out_shape=jax.ShapeDtypeStruct(LINKED, jnp.float32),
        scratch_shapes=common_scratch(14)
        + [
            pltpu.VMEM((FIELDS * 16, 128), jnp.float32),
            pltpu.VMEM((SIDE, 128), jnp.float32),
            pltpu.VMEM((2 * SIDE, 128), jnp.float32),
            pltpu.VMEM((SIDE // 32, 8, 128), jnp.float32),
        ]
        + SOLVE_SCRATCH
        + [
            pltpu.VMEM((2, DATES, 1, BLOCKS, 128), jnp.float32),
            pltpu.VMEM((256, 128), jnp.bfloat16),
            pltpu.VMEM(PARTIAL, jnp.float32),
            pltpu.SemaphoreType.DMA,
        ],
        compiler_params=pltpu.CompilerParams(vmem_limit_bytes=49 * 1024 * 1024),
        cost_estimate=pl.CostEstimate(flops=10**8, bytes_accessed=10**7, transcendentals=0),
        name="link_last",
    )(message, left, right, tables, pool, partial)


def local(slc, valid_rows):
    valid = valid_rows.T
    size = lax.axis_size("col")
    up = [(i, i + 1) for i in range(size - 1)]
    down = [(i + 1, i) for i in range(size - 1)]
    message1, message2 = pack(slc, valid)
    received1 = lax.all_to_all(message1, "row", 0, 0, tiled=True)
    received1, message2 = lax.optimization_barrier((received1, message2))
    received2 = lax.all_to_all(message2, "row", 0, 0, tiled=True)
    own = cut_columns(received1)
    left = lax.ppermute(own, "col", up)
    right = lax.ppermute(own, "col", down)
    tables, pool = column_tables()
    last_table = jnp.asarray(tables[FIRST:, :, 0:128])
    partial = link_first(received1, jnp.asarray(tables))
    return link_last(received2, left, right, last_table, jnp.asarray(pool), partial)


def solution(mesh):
    return jax.shard_map(
        local,
        mesh=mesh,
        in_specs=(P(None, "row", None, "col"), P()),
        out_specs=P(None, None, "row", "col"),
        check_vma=False,
    )
```
